32 devices in a mesh: parts: 2 (over x), gx: 16 (over z, y, core).
Axes of the slice: x: 2, y: 2, z: 4, core: 2. Of those that a mesh axis runs over, the one named last changes fastest.
Arguments:
- right_side: float32 [512, 32, 128], P(('parts', 'gx')), parts along dimension 0, may hold values from -9 to 9
- wet_quarters: int32 [512, 32, 128], P(('parts', 'gx')), parts along dimension 0, may hold values from 0 to 4, as said below
- trans_x: bfloat16 [512, 32, 128], P(('parts', 'gx')), parts along dimension 0, may hold values from 0.049804688 to 1
- trans_y: bfloat16 [512, 32, 128], P(('parts', 'gx')), parts along dimension 0, may hold values from 0.049804688 to 1
- trans_z: bfloat16 [512, 32, 128], P(('parts', 'gx')), parts along dimension 0, may hold values from 0.049804688 to 1
- storage: bfloat16 [512, 32, 128], P(('parts', 'gx')), parts along dimension 0, may hold values from 0.099609375 to 2
- basis: bfloat16 [8, 512, 32, 128], P(None, ('parts', 'gx')), parts along dimension 1, may hold values from 0 to 0.25
- coupling: float32 [6, 8, 8, 512], P(None, None, None, ('parts', 'gx')), parts along dimension 3, may hold values from -2.4 to 2.4
- coarse_inverse: float32 [8, 8, 512], P(None, None, 'parts'), parts along dimension 2, may hold values from -0.1 to 0.45
- owned_block: int32 [256], replicated, may hold values from 0 to 255, as said below
- block_slot: int32 [256], P('gx'), may hold values from 0 to 255, as said below
- neighbours: int32 [6, 256], P(None, 'gx'), may hold values from -1 to 255, as said below
Outputs:
- pressure: float32 [512, 32, 128], P(('parts', 'gx')), parts along dimension 0
- residual: float32 [512, 32, 128], P(('parts', 'gx')), parts along dimension 0
The draws below stay inside these ranges and needn't reach their ends.
There are 2 independent parts, one for each index of `parts`. The reference program is written for one: setup_inputs(seed, part) draws one part's arguments, and reference() takes and returns one part's arrays. A program takes and returns all parts, laid end to end along the dimension named above; an argument that names none is the same for every part. Nothing has to cross between parts.
Inputs may be any that keep to these rules, and one draw needn't show every extreme that they name: `wet_quarters`: in every column of 128 cells the cells below a water table hold 4, the cell at the table 1 to 3, the cells above it 0. `owned_block`: A permutation of the 256 block numbers. `block_slot`: the inverse permutation of owned_block. `neighbours`: entry [k, s] is the slot of the block sharing the k-th face (order +x, -x, +y, -y, +z, -z) with the block in slot s, or -1 where that block lies outside the grid.
All inputs are finite; a program needn't handle non-finite values.
Results may differ from the reference program's by a relative error of at most 0.0003.
Values may be sent and summed in bfloat16 or wider, within the bound.
No kernel may reach another device: no remote copies, remote signals or barrier semaphores. Data moves between devices by JAX's collectives and lax.ppermute only.
A program may use at most 64 MiB of HBM per device.

```python
import math
import jax
import jax.numpy as jnp
from jax import lax

NY = 32
NZ = 128
BLK = 16
NBF = 8
NNB = 6
ITERS = 2
SWEEPS = 3
CSWEEPS = 4
NX = 256
NXB = 16
NYB = 2
NZB = 8
NB = 256


def coarse_order(key):
    return jax.random.permutation(key, NB).astype(jnp.int32)


def draw_owned_block(key, part):
    order = coarse_order(key)
    return order


def draw_block_slot(key, part):
    order = coarse_order(key)
    return jnp.argsort(order).astype(jnp.int32)


def draw_neighbours(key, part):
    order = coarse_order(key)
    slot_of = jnp.argsort(order).astype(jnp.int32)
    per_plane = NYB * NZB
    block_x = order // per_plane
    block_y = order // NZB % NYB
    block_z = order % NZB
    directions = ((1, 0, 0), (-1, 0, 0), (0, 1, 0), (0, -1, 0), (0, 0, 1), (0, 0, -1))
    listed = []
    for step_x, step_y, step_z in directions:
        near_x = block_x + step_x
        near_y = block_y + step_y
        near_z = block_z + step_z
        inside = (near_x >= 0) & (near_x < NXB) & (near_y >= 0) & (near_y < NYB) & (near_z >= 0) & (near_z < NZB)
        target = (jnp.clip(near_x, 0, NXB - 1) * NYB + jnp.clip(near_y, 0, NYB - 1)) * NZB + jnp.clip(near_z, 0, NZB - 1)
        listed.append(jnp.where(inside, slot_of[target], -1))
    return jnp.stack(listed).astype(jnp.int32)


def draw_wet_quarters(key, part):
    key = jax.random.fold_in(key, 5)
    first_key, second_key = jax.random.split(key)
    x_index = lax.broadcasted_iota(jnp.int32, (NX, NY), 0)
    y_index = lax.broadcasted_iota(jnp.int32, (NX, NY), 1)
    reach = 1 + NZ // 2 * x_index // NX
    lowered = jax.random.randint(first_key, (NX, NY), 0, reach)
    lowered = jnp.where((x_index == NX - 1) & (y_index == 0), NZ // 2, lowered)
    table = (NZ - 1 - lowered)[:, :, None]
    z_index = lax.broadcasted_iota(jnp.int32, (NX, NY, NZ), 2)
    partial_wet = jax.random.randint(second_key, (NX, NY, NZ), 1, 4)
    filled = jnp.where(z_index < table, 4, jnp.where(z_index == table, partial_wet, 0))
    return filled.astype(jnp.int32)


def draw_right_side(key, part):
    key = jax.random.fold_in(key, 11)
    first_key = jax.random.fold_in(key, 0)
    return jnp.clip(jax.random.normal(first_key, (NX, NY, NZ), jnp.float32), -6.0, 6.0)


def draw_coarse_inverse(key, part):
    key = jax.random.fold_in(key, 7)
    first_key, second_key = jax.random.split(key)
    leading = jnp.exp(jax.random.uniform(first_key, (NBF, NB), jnp.float32, math.log(0.03), math.log(0.3)))
    off_part = jnp.clip(0.025 * jax.random.normal(second_key, (NBF, NBF, NB), jnp.float32), -0.1, 0.1)
    identity = (lax.broadcasted_iota(jnp.int32, (NBF, NBF), 0) == lax.broadcasted_iota(jnp.int32, (NBF, NBF), 1)).astype(jnp.float32)
    return identity[:, :, None] * leading[None] + off_part


def block_scale(own_key, dims, cuts, least, high):
    def one(dim, blocks):
        heights = jax.random.uniform(jax.random.fold_in(jax.random.fold_in(own_key, 6), dim), (blocks,), jnp.float32, least / len(cuts), high / len(cuts))
        return jnp.repeat(jnp.exp(heights), dims[dim] // blocks).reshape((-1,) + (1,) * (len(dims) - dim - 1))

    gain = one(*cuts[0])
    for cut in cuts[1:]:
        gain = gain * one(*cut)
    return gain


def bell_draw(rng, dims, width, most, cuts=(), held_as=jnp.bfloat16):
    level = block_scale(rng, dims, cuts, -0.22, 0.18) if cuts else 1.0
    entries = jax.random.normal(rng, dims, jnp.float32) * width * level
    return jnp.minimum(jnp.maximum(entries, -most), most).astype(held_as)


def setup_inputs(seed: int = 0, part: int = 0) -> dict:
    splits = jax.random.split(jax.random.key(seed), 13)
    part_keys = jax.random.split(jax.random.fold_in(splits[12], part), 13)
    right_side = draw_right_side(jax.random.fold_in(jax.random.fold_in(splits[12], part), 71), part)
    wet_quarters = draw_wet_quarters(jax.random.fold_in(jax.random.fold_in(splits[12], part), 71), part)
    trans_x = jnp.clip(jnp.exp(math.log(1.0) - 2.9996462 * jax.random.uniform(part_keys[2], (NX, NY, NZ), jnp.float32) ** block_scale(part_keys[2], (NX, NY, NZ), ((0, 16),), -0.2, 0.2)), 0.049804688, 1.0).astype(jnp.bfloat16)
    trans_y = jnp.clip(jnp.exp(math.log(1.0) - 2.9996462 * jax.random.uniform(part_keys[3], (NX, NY, NZ), jnp.float32) ** block_scale(part_keys[3], (NX, NY, NZ), ((0, 16),), -0.2, 0.2)), 0.049804688, 1.0).astype(jnp.bfloat16)
    trans_z = jnp.clip(jnp.exp(math.log(1.0) - 2.9996462 * jax.random.uniform(part_keys[4], (NX, NY, NZ), jnp.float32) ** block_scale(part_keys[4], (NX, NY, NZ), ((0, 16),), -0.2, 0.2)), 0.049804688, 1.0).astype(jnp.bfloat16)
    storage = jnp.clip(jnp.exp(math.log(2.0) - 2.9996462 * jax.random.uniform(part_keys[5], (NX, NY, NZ), jnp.float32) ** block_scale(part_keys[5], (NX, NY, NZ), ((0, 16),), -0.2, 0.2)), 0.099609375, 2.0).astype(jnp.bfloat16)
    basis = jnp.clip(0.25 * jax.random.uniform(part_keys[6], (NBF, NX, NY, NZ), jnp.float32) ** block_scale(part_keys[6], (NBF, NX, NY, NZ), ((1, 16),), -0.2, 0.2), 0.0, 0.25).astype(jnp.bfloat16)
    coupling = bell_draw(part_keys[7], (NNB, NBF, NBF, NB), 0.4, 2.4, ((3, 16),), jnp.float32)
    coarse_inverse = draw_coarse_inverse(jax.random.fold_in(jax.random.fold_in(splits[12], part), 71), part)
    owned_block = draw_owned_block(jax.random.fold_in(splits[12], 71), part)
    block_slot = draw_block_slot(jax.random.fold_in(splits[12], 71), part)
    neighbours = draw_neighbours(jax.random.fold_in(splits[12], 71), part)
    return {"right_side": right_side, "wet_quarters": wet_quarters, "trans_x": trans_x, "trans_y": trans_y, "trans_z": trans_z, "storage": storage, "basis": basis, "coupling": coupling, "coarse_inverse": coarse_inverse, "owned_block": owned_block, "block_slot": block_slot, "neighbours": neighbours}


relaxation = 2.0 / 3.0


def lower_shift(values, axis_number):
    pieces = [(0, 0), (0, 0), (0, 0)]
    pieces[axis_number] = (1, 0)
    padded = jnp.pad(values, pieces)
    return lax.slice_in_dim(padded, 0, values.shape[axis_number], axis=axis_number)


def upper_lower(state_field, axis_number):
    pieces = [(0, 0), (0, 0), (0, 0)]
    pieces[axis_number] = (1, 1)
    padded = jnp.pad(state_field, pieces)
    length = state_field.shape[axis_number]
    upper_side = lax.slice_in_dim(padded, 2, length + 2, axis=axis_number)
    lower_side = lax.slice_in_dim(padded, 0, length, axis=axis_number)
    return upper_side, lower_side


def operate(state_field, faces, wet_share, dry_cell, storage_f):
    east_face, west_face, north_face, south_face, upper_face, lower_face = faces
    east_cell, west_cell = upper_lower(state_field, 0)
    north_cell, south_cell = upper_lower(state_field, 1)
    top_cell, bottom_cell = upper_lower(state_field, 2)
    face_flux = east_face * (state_field - east_cell) + west_face * (state_field - west_cell)
    face_flux = face_flux + north_face * (state_field - north_cell) + south_face * (state_field - south_cell)
    face_flux = face_flux + upper_face * (state_field - top_cell) + lower_face * (state_field - bottom_cell)
    return wet_share * (storage_f * state_field + face_flux) + dry_cell * state_field


def restrict(misfit, basis):
    restricted = []
    for basis_index in range(NBF):
        weighted = basis[basis_index].astype(jnp.float32) * misfit
        summed = weighted.reshape(NXB, BLK, NYB, BLK, NZB, BLK).sum(axis=(1, 3, 5))
        restricted.append(summed.reshape(NB))
    return jnp.stack(restricted)


def prolong(coarse_slab, basis):
    correction = jnp.zeros(basis.shape[1:], jnp.float32)
    for basis_index in range(NBF):
        block_grid = coarse_slab[basis_index].reshape(NXB, 1, NYB, 1, NZB, 1)
        spread_out = jnp.broadcast_to(block_grid, (NXB, BLK, NYB, BLK, NZB, BLK)).reshape(NX, NY, NZ)
        correction = correction + basis[basis_index].astype(jnp.float32) * spread_out
    return correction


def coarse_solve(coarse_slab, coupling, coarse_inverse, owned_block, block_slot, neighbours):
    exact_mode = lax.Precision.HIGHEST
    own_residual = coarse_slab[:, owned_block]
    own_inverse = coarse_inverse[:, :, owned_block]
    present = (neighbours >= 0).astype(jnp.float32)
    safe_index = jnp.maximum(neighbours, 0).astype(jnp.int32)
    values = jnp.einsum('ijb,jb->ib', own_inverse, own_residual, precision=exact_mode)
    for sweep_index in range(CSWEEPS - 1):
        nearby = values[:, safe_index] * present[None]
        coupled = jnp.einsum('kijb,jkb->ib', coupling, nearby, precision=exact_mode)
        values = jnp.einsum('ijb,jb->ib', own_inverse, own_residual - coupled, precision=exact_mode)
    return values[:, block_slot]


def reference(right_side, wet_quarters, trans_x, trans_y, trans_z, storage, basis, coupling, coarse_inverse, owned_block, block_slot, neighbours):
    wet_share = wet_quarters.astype(jnp.float32) * 0.25
    dry_cell = 1.0 - jnp.minimum(wet_quarters, 1).astype(jnp.float32)
    east_face = trans_x.astype(jnp.float32)
    west_face = lower_shift(east_face, 0)
    north_face = trans_y.astype(jnp.float32)
    south_face = lower_shift(north_face, 1)
    upper_face = trans_z.astype(jnp.float32)
    lower_face = lower_shift(upper_face, 2)
    storage_f = storage.astype(jnp.float32)
    faces = (east_face, west_face, north_face, south_face, upper_face, lower_face)
    diagonal_coef = wet_share * (storage_f + east_face + west_face + north_face + south_face + upper_face + lower_face) + dry_cell
    pressure = jnp.zeros_like(right_side)
    for outer_step in range(ITERS):
        if outer_step == 0:
            misfit = right_side
        else:
            misfit = right_side - operate(pressure, faces, wet_share, dry_cell, storage_f)
        coarse_values = coarse_solve(restrict(misfit, basis), coupling, coarse_inverse, owned_block, block_slot, neighbours)
        pressure = pressure + prolong(coarse_values, basis)
        for sweep_index in range(SWEEPS):
            pressure = pressure + relaxation * (right_side - operate(pressure, faces, wet_share, dry_cell, storage_f)) / diagonal_coef
    residual = right_side - operate(pressure, faces, wet_share, dry_cell, storage_f)
    return pressure, residual
```

```python
import functools

import jax
import jax.numpy as jnp
from jax import lax
from jax.experimental import pallas as pl
from jax.experimental.pallas import tpu as pltpu
from jax.sharding import PartitionSpec as P

BLK = 16
NBF = 8
NNB = 6
SWEEPS = 3
CSWEEPS = 4
NYB = 2
NZB = 8
PER = NYB * NZB
WIN = 16 * PER
LEAD = 4
HALO = 4
OMEGA = 2.0 / 3.0
KROWS = NNB * NBF * NBF
F32 = jnp.float32
BF16 = jnp.bfloat16

THIN = HALO - 1
H_TX = NBF * HALO
H_REST = H_TX + HALO
H_ALL = H_REST + 6 * THIN


def three_parts(x):
    high = x.astype(BF16)
    rest = x - high.astype(F32)
    middle = rest.astype(BF16)
    low = (rest - middle.astype(F32)).astype(BF16)
    return high, middle, low


def restrict_to(basis_at, field_at, planes):
    def step(x, totals):
        field = field_at(x)
        out = []
        for i in range(NBF):
            for yb in range(NYB):
                rows = slice(yb * BLK, (yb + 1) * BLK)
                product = basis_at(i, x)[rows].astype(F32) * field[rows]
                out.append(totals[i * NYB + yb] + product[:8] + product[8:])
        return tuple(out)

    zero = jnp.zeros((8, 128), F32)
    totals = lax.fori_loop(0, planes, step, (zero,) * (NBF * NYB))
    groups = lax.broadcasted_iota(jnp.int32, (NZB, 3 * 128), 1)
    owner = lax.broadcasted_iota(jnp.int32, (NZB, 3 * 128), 0)
    spread = ((groups % 128) // BLK == owner).astype(F32).astype(BF16)
    halves = []
    for yb in range(NYB):
        rows = [jnp.sum(totals[i * NYB + yb], axis=0, keepdims=True) for i in range(NBF)]
        stacked = jnp.concatenate(three_parts(jnp.concatenate(rows, 0)), axis=1)
        halves.append(
            lax.dot_general(
                spread, stacked, (((1,), (1,)), ((), ())), preferred_element_type=F32
            )
        )
    return jnp.concatenate(halves, 0)


def first_kernel(count, owned_ref, basis_ref, field_ref, coupling_ref, out_ref):
    me = lax.axis_index("gx")
    coarse = restrict_to(lambda i, x: basis_ref[i, x], lambda x: field_ref[x], basis_ref.shape[1])
    slot = lax.broadcasted_iota(jnp.int32, (PER, 1), 0)
    block = jnp.zeros((PER, 1), jnp.int32)
    for s in range(PER):
        block = jnp.where(slot == s, owned_ref[me * PER + s], block)
    tail = jnp.concatenate(
        [coarse, block.astype(F32), jnp.zeros((PER, 128 - NBF - 1), F32)], axis=1
    )
    wide = jnp.concatenate(
        [coupling_ref[...], jnp.zeros((KROWS, 128 - PER), F32)], axis=1
    )
    rows = jnp.concatenate([wide.T[:PER], tail], axis=1)

    def put(e, carry):
        out_ref[e] = rows
        return carry

    lax.fori_loop(0, count, put, 0)


def coarse_solve(coupling_at, inverse_at, residual):
    lane = lax.broadcasted_iota(jnp.int32, (NBF, WIN), 1)
    in_z, in_y = lane % NZB, (lane // NZB) % NYB

    def rows_of(parts):
        return jnp.concatenate([jnp.sum(p, axis=0, keepdims=True) for p in parts], 0)

    def inverted(v):
        return rows_of([inverse_at(i) * v for i in range(NBF)])

    values = inverted(residual)
    for _ in range(CSWEEPS - 1):
        near = (
            pltpu.roll(values, WIN - PER, 1),
            pltpu.roll(values, PER, 1),
            jnp.where(in_y < NYB - 1, pltpu.roll(values, WIN - NZB, 1), 0.0),
            jnp.where(in_y > 0, pltpu.roll(values, NZB, 1), 0.0),
            jnp.where(in_z < NZB - 1, pltpu.roll(values, WIN - 1, 1), 0.0),
            jnp.where(in_z > 0, pltpu.roll(values, 1, 1), 0.0),
        )
        parts = []
        for i in range(NBF):
            total = coupling_at(0, i) * near[0]
            for k in range(1, NNB):
                total = total + coupling_at(k, i) * near[k]
            parts.append(total)
        values = inverted(residual - rows_of(parts))
    return values


def spread_blocks(values):
    width = 3 * NYB * 128
    block = lax.broadcasted_iota(jnp.int32, (128, width), 0)
    column = lax.broadcasted_iota(jnp.int32, (128, width), 1)
    wanted = (LEAD - 1) * PER + column // BLK
    chosen = (block == wanted).astype(F32).astype(BF16)
    stacked = jnp.concatenate(three_parts(values[:, :128]), axis=0)
    spread = jnp.dot(stacked, chosen, preferred_element_type=F32)
    return spread[:NBF] + spread[NBF : 2 * NBF] + spread[2 * NBF :]


def iteration_kernel(last, count, *refs):
    (
        gathered_ref, inverse_ref, coupling_ref, basis_hbm, right_hbm, wet_hbm, tx_hbm, ty_hbm, tz_hbm, st_hbm,
        near_hbm, far_hbm,
    ) = refs[:12]
    refs = refs[12:]
    if last:
        (pressure_hbm, near_p_hbm, far_p_hbm, out_ref, residual_ref) = refs[:5]
        refs = refs[5:]
    else:
        (out_ref, send_near_ref, send_far_ref, packed_ref, coupling_out_ref) = refs[:5]
        refs = refs[5:]
    (
        basis_s, right_s, wet_s, tx_s, ty_s, tz_s, st_s, wet_h, high_h, low_h,
        coef_s, scaled_s, diag_s, one_s, two_s, window_s, coupling_s, sems,
    ) = refs
    planes = right_s.shape[0]
    me = lax.axis_index("gx")
    even = lax.rem(me, 2) == 0
    top = planes + HALO
    near_at, far_at = jnp.where(even, top, 0), jnp.where(even, 0, top)
    near_thin, far_thin = jnp.where(even, top, 1), jnp.where(even, 1, top)

    jobs = [
        (tx_hbm, tx_s.at[pl.ds(HALO, planes)]),
        (ty_hbm, ty_s.at[pl.ds(HALO, planes)]),
        (tz_hbm, tz_s.at[pl.ds(HALO, planes)]),
        (st_hbm, st_s.at[pl.ds(HALO, planes)]),
        (wet_hbm, wet_s),
        (right_hbm, right_s),
    ]
    for halo, wide_at, thin_at in ((near_hbm, near_at, near_thin), (far_hbm, far_at, far_thin)):
        jobs.append((halo.at[pl.ds(H_TX, HALO)], tx_s.at[pl.ds(wide_at, HALO)]))
        for k, into in enumerate((wet_h, ty_s, tz_s, st_s, high_h, low_h)):
            jobs.append((halo.at[pl.ds(H_REST + k * THIN, THIN)], into.at[pl.ds(thin_at, THIN)]))
    statics = len(jobs)
    jobs.append((basis_hbm, basis_s.at[:, pl.ds(HALO, planes)]))
    for halo, wide_at in ((near_hbm, near_at), (far_hbm, far_at)):
        for i in range(NBF):
            jobs.append((halo.at[pl.ds(i * HALO, HALO)], basis_s.at[i, pl.ds(wide_at, HALO)]))
    if last:
        jobs.append((pressure_hbm, one_s.at[pl.ds(HALO, planes)]))
        jobs.append((near_p_hbm, one_s.at[pl.ds(near_at, HALO)]))
        jobs.append((far_p_hbm, one_s.at[pl.ds(far_at, HALO)]))
    copies = [pltpu.make_async_copy(a, b, sems.at[k]) for k, (a, b) in enumerate(jobs)]
    for copy in copies:
        copy.start()

    tall = gathered_ref.shape[0] * PER
    window_s[...] = jnp.zeros_like(window_s)
    first = 0 if last else KROWS
    for e in range(count):
        window_s[pl.ds(LEAD * PER + e * PER, PER)] = gathered_ref[e, :, pl.ds(first, 128)]
    residual = window_s[pl.ds(pl.multiple_of(me * PER, PER), WIN)].T[:NBF]
    if not last:
        lane = lax.broadcasted_iota(jnp.int32, (WIN, WIN), 1) + (me - LEAD) * PER
        for part in range(tall // WIN):
            span = pl.ds(part * (WIN // PER), WIN // PER)
            rows = gathered_ref[span].reshape(WIN, KROWS + 128)
            block = rows[:, KROWS + NBF : KROWS + NBF + 1].astype(jnp.int32)
            chosen = (block == lane).astype(F32).astype(BF16)
            stacked = jnp.concatenate(three_parts(rows[:, :KROWS].T), axis=0)
            found = jnp.dot(stacked, chosen, preferred_element_type=F32)
            found = found[:KROWS] + found[KROWS : 2 * KROWS] + found[2 * KROWS :]
            coupling_s[...] = found if part == 0 else coupling_s[...] + found
        coupling_out_ref[...] = coupling_s[...]
        coupling_from = coupling_s
    else:
        coupling_from = coupling_ref
    values = coarse_solve(
        lambda k, i: coupling_from[pl.ds((k * NBF + i) * NBF, NBF)],
        lambda i: inverse_ref[pl.ds(i * NBF, NBF)],
        residual,
    )
    spread = spread_blocks(values)

    for copy in copies[:statics]:
        copy.wait()
    in_y = lax.broadcasted_iota(jnp.int32, (32, 128), 0)
    in_z = lax.broadcasted_iota(jnp.int32, (32, 128), 1)

    def coefficients(x, quarters, right, own):
        wet = quarters * 0.25
        dry = 1.0 - jnp.minimum(quarters, 1.0)
        east, west = tx_s[x].astype(F32), tx_s[x - 1].astype(F32)
        north, upper = ty_s[x].astype(F32), tz_s[x].astype(F32)
        south = jnp.where(in_y > 0, pltpu.roll(north, 1, 0), 0.0)
        lower = jnp.where(in_z > 0, pltpu.roll(upper, 1, 1), 0.0)
        total = st_s[x].astype(F32) + east + west + north + south + upper + lower
        diag = wet * total + dry
        share = OMEGA / diag
        scale = wet * share
        coef_s[x, 0] = scale * east
        coef_s[x, 1] = scale * west
        coef_s[x, 2] = jnp.where(in_y < 31, scale * north, 0.0)
        coef_s[x, 3] = scale * south
        coef_s[x, 4] = jnp.where(in_z < 127, scale * upper, 0.0)
        coef_s[x, 5] = scale * lower
        scaled_s[x] = right * share
        if own:
            diag_s[x - HALO] = diag * (1.0 / OMEGA)

    def own_plane(k, carry):
        coefficients(k + HALO, wet_s[k].astype(F32), right_s[k], True)
        return carry

    def halo_plane(k, carry):
        x = jnp.where(k < THIN, k + 1, k - THIN + top)
        coefficients(x, wet_h[x].astype(F32), high_h[x].astype(F32) + low_h[x].astype(F32), False)
        return carry

    lax.fori_loop(0, planes, own_plane, 0)
    lax.fori_loop(0, 2 * THIN, halo_plane, 0)

    for copy in copies[statics:]:
        copy.wait()

    def corrected(slab):
        start = slab * NYB * 128
        gains = [
            [jnp.broadcast_to(spread[i : i + 1, start + yb * 128 : start + (yb + 1) * 128], (BLK, 128)) for i in range(NBF)]
            for yb in range(NYB)
        ]

        def step(x, carry):
            for yb in range(NYB):
                rows = slice(yb * BLK, (yb + 1) * BLK)
                total = basis_s[0, x, rows].astype(F32) * gains[yb][0]
                for i in range(1, NBF):
                    total = total + basis_s[i, x, rows].astype(F32) * gains[yb][i]
                one_s[x, rows] = one_s[x, rows] + total if last else total
            return carry

        return step

    lax.fori_loop(0, HALO, corrected(0), 0)
    lax.fori_loop(HALO, top, corrected(1), 0)
    lax.fori_loop(top, top + HALO, corrected(2), 0)

    def pulled(state, x):
        here = state[x]
        total = scaled_s[x] + coef_s[x, 0] * state[x + 1] + coef_s[x, 1] * state[x - 1]
        total = total + coef_s[x, 2] * pltpu.roll(here, 31, 0) + coef_s[x, 3] * pltpu.roll(here, 1, 0)
        total = total + coef_s[x, 4] * pltpu.roll(here, 127, 1) + coef_s[x, 5] * pltpu.roll(here, 1, 1)
        return here, total

    def sweep(source, target):
        def step(x, carry):
            here, total = pulled(source, x)
            target[x] = (1.0 - OMEGA) * here + total
            return carry

        return step

    source, target = one_s, two_s
    for k in range(SWEEPS):
        lax.fori_loop(k + 1, top + HALO - 1 - k, sweep(source, target), 0)
        source, target = target, source

    def misfit(x, carry):
        here, total = pulled(source, x)
        value = (total - OMEGA * here) * diag_s[x - HALO]
        out_ref[x - HALO] = here
        if last:
            residual_ref[x - HALO] = value
        else:
            target[x] = value
        return carry

    lax.fori_loop(HALO, top, misfit, 0)
    if not last:
        send_near_ref[...] = source[pl.ds(jnp.where(even, planes, HALO), HALO)]
        send_far_ref[...] = source[pl.ds(jnp.where(even, HALO, planes), HALO)]
        coarse = restrict_to(
            lambda i, x: basis_s[i, x + HALO], lambda x: target[x + HALO], planes
        )
        tail = jnp.concatenate([coarse, jnp.zeros((PER, 128 - NBF), F32)], axis=1)

        def put(e, carry):
            packed_ref[e] = tail
            return carry

        lax.fori_loop(0, count, put, 0)


VMEM = pl.BlockSpec(memory_space=pltpu.VMEM)
SMEM = pl.BlockSpec(memory_space=pltpu.SMEM)
HBM = pl.BlockSpec(memory_space=pl.ANY)
PARAMS = pltpu.CompilerParams(vmem_limit_bytes=40 * 1024 * 1024)


def local(
    right_side, wet_quarters, trans_x, trans_y, trans_z, storage, basis, coupling, coarse_inverse,
    owned_block, block_slot, neighbours,
):
    count = lax.axis_size("gx")
    me = lax.axis_index("gx")
    planes, ny, nz = right_side.shape
    even = lax.rem(me, 2) == 0
    near_pairs = [(i, i ^ 1) for i in range(count)]
    far_pairs = [(i, i + 1) for i in range(1, count - 1, 2)]
    far_pairs = far_pairs + [(b, a) for a, b in far_pairs]

    def packed_halo(upper):
        wide = jnp.where(upper, planes - HALO, 0)
        thin = jnp.where(upper, planes - THIN, 0)
        pieces = [lax.dynamic_slice_in_dim(basis, wide, HALO, 1).reshape(NBF * HALO, ny, nz)]
        pieces.append(lax.dynamic_slice_in_dim(trans_x, wide, HALO, 0))
        right = lax.dynamic_slice_in_dim(right_side, thin, THIN, 0)
        high = right.astype(BF16)
        for field in (wet_quarters, trans_y, trans_z, storage):
            pieces.append(lax.dynamic_slice_in_dim(field, thin, THIN, 0).astype(BF16))
        pieces.append(high)
        pieces.append((right - high.astype(F32)).astype(BF16))
        return jnp.concatenate(pieces, 0)

    far = lax.ppermute(packed_halo(~even), "gx", far_pairs)
    near = lax.ppermute(packed_halo(even), "gx", near_pairs)

    packed = pl.pallas_call(
        functools.partial(first_kernel, count),
        out_shape=jax.ShapeDtypeStruct((count, PER, KROWS + 128), F32),
        in_specs=[SMEM, VMEM, VMEM, VMEM],
        out_specs=VMEM,
        compiler_params=PARAMS,
        name="restrict_first",
    )(owned_block, basis, right_side, coupling.reshape(KROWS, PER))
    gathered = lax.all_to_all(packed, "gx", 0, 0, tiled=True)

    padded = jnp.pad(coarse_inverse, ((0, 0), (0, 0), (LEAD * PER, WIN - LEAD * PER)))
    inverse = lax.dynamic_slice_in_dim(padded, me * PER, WIN, 2).reshape(NBF * NBF, WIN)

    full = planes + 2 * HALO
    field = (ny, nz)
    scratch = [
        pltpu.VMEM((NBF, full) + field, BF16),
        pltpu.VMEM((planes,) + field, F32),
        pltpu.VMEM((planes,) + field, jnp.int32),
        pltpu.VMEM((full,) + field, BF16),
        pltpu.VMEM((full,) + field, BF16),
        pltpu.VMEM((full,) + field, BF16),
        pltpu.VMEM((full,) + field, BF16),
        pltpu.VMEM((full,) + field, BF16),
        pltpu.VMEM((full,) + field, BF16),
        pltpu.VMEM((full,) + field, BF16),
        pltpu.VMEM((full, 6) + field, F32),
        pltpu.VMEM((full,) + field, F32),
        pltpu.VMEM((planes,) + field, F32),
        pltpu.VMEM((full,) + field, F32),
        pltpu.VMEM((full,) + field, F32),
        pltpu.VMEM((count * PER + WIN, 128), F32),
        pltpu.VMEM((KROWS, WIN), F32),
        pltpu.SemaphoreType.DMA((48,)),
    ]
    statics = (basis, right_side, wet_quarters, trans_x, trans_y, trans_z, storage, near, far)
    whole = jax.ShapeDtypeStruct((planes,) + field, F32)
    halo = jax.ShapeDtypeStruct((HALO,) + field, F32)
    blank = jnp.zeros((8, 128), F32)
    pressure, send_near, send_far, packed, coupled = pl.pallas_call(
        functools.partial(iteration_kernel, False, count),
        out_shape=(
            whole, halo, halo,
            jax.ShapeDtypeStruct((count, PER, 128), F32),
            jax.ShapeDtypeStruct((KROWS, WIN), F32),
        ),
        in_specs=[VMEM] * 3 + [HBM] * 9,
        out_specs=(VMEM,) * 5,
        scratch_shapes=scratch,
        compiler_params=PARAMS,
        name="iteration_first",
    )(gathered, inverse, blank, *statics)

    far_p = lax.ppermute(send_far, "gx", far_pairs)
    near_p = lax.ppermute(send_near, "gx", near_pairs)
    gathered = lax.all_to_all(packed, "gx", 0, 0, tiled=True)
    return pl.pallas_call(
        functools.partial(iteration_kernel, True, count),
        out_shape=(whole, whole),
        in_specs=[VMEM] * 3 + [HBM] * 12,
        out_specs=(VMEM,) * 2,
        scratch_shapes=scratch,
        compiler_params=PARAMS,
        name="iteration_last",
    )(gathered, inverse, coupled, *statics, pressure, near_p, far_p)


def solution(mesh):
    slabs = P(("parts", "gx"), None, None)
    placed = (
        slabs, slabs, slabs, slabs, slabs, slabs,
        P(None, ("parts", "gx"), None, None),
        P(None, None, None, ("parts", "gx")),
        P(None, None, "parts"),
        P(),
        P("gx"),
        P(None, "gx"),
    )
    return jax.shard_map(local, mesh=mesh, in_specs=placed, out_specs=(slabs, slabs), check_vma=False)
```

```python
import functools

import jax
import jax.numpy as jnp
from jax import lax
from jax.experimental import pallas as pl
from jax.experimental.pallas import tpu as pltpu
from jax.sharding import PartitionSpec as P

BLK = 16
NBF = 8
NNB = 6
SWEEPS = 3
CSWEEPS = 4
NYB = 2
NZB = 8
PER = NYB * NZB
WIN = 16 * PER
LEAD = 4
HALO = 4
OMEGA = 2.0 / 3.0
KROWS = NNB * NBF * NBF
F32 = jnp.float32
BF16 = jnp.bfloat16

THIN = HALO - 1
H_TX = NBF * HALO
H_REST = H_TX + HALO
H_WET = H_REST + 3 * THIN
H_ALL = H_REST + 6 * THIN


def planes_in_groups(low, high, group, step):
    count = (high - low) // group

    def body(k, carry):
        for j in range(group):
            step(low + k * group + j)
        return carry

    lax.fori_loop(0, count, body, 0)
    for x in range(low + count * group, high):
        step(x)


def three_parts(x):
    high = x.astype(BF16)
    rest = x - high.astype(F32)
    middle = rest.astype(BF16)
    low = (rest - middle.astype(F32)).astype(BF16)
    return high, middle, low


def restrict_to(basis_at, field_at, planes):
    def step(x, totals):
        field = field_at(x)
        out = []
        for i in range(NBF):
            for yb in range(NYB):
                rows = slice(yb * BLK, (yb + 1) * BLK)
                product = basis_at(i, x)[rows].astype(F32) * field[rows]
                out.append(totals[i * NYB + yb] + product[:8] + product[8:])
        return tuple(out)

    zero = jnp.zeros((8, 128), F32)
    totals = lax.fori_loop(0, planes, step, (zero,) * (NBF * NYB))
    groups = lax.broadcasted_iota(jnp.int32, (NZB, 3 * 128), 1)
    owner = lax.broadcasted_iota(jnp.int32, (NZB, 3 * 128), 0)
    spread = ((groups % 128) // BLK == owner).astype(F32).astype(BF16)
    halves = []
    for yb in range(NYB):
        rows = [jnp.sum(totals[i * NYB + yb], axis=0, keepdims=True) for i in range(NBF)]
        stacked = jnp.concatenate(three_parts(jnp.concatenate(rows, 0)), axis=1)
        halves.append(
            lax.dot_general(
                spread, stacked, (((1,), (1,)), ((), ())), preferred_element_type=F32
            )
        )
    return jnp.concatenate(halves, 0)


def started(pairs, sems, first=0):
    copies = [pltpu.make_async_copy(a, b, sems.at[first + k]) for k, (a, b) in enumerate(pairs)]
    for copy in copies:
        copy.start()
    return copies


def first_kernel(
    count, owned_hbm, basis_hbm, right_hbm, wet_hbm, tx_hbm, ty_hbm, tz_hbm, st_hbm, coupling_hbm,
    near_hbm, far_hbm, packed_hbm, owned_s, basis_s, right_s, thin_wet, coupling_s, rows_s, halo_s, sems,
):
    me = lax.axis_index("gx")
    even = lax.rem(me, 2) == 0
    planes = right_s.shape[0]
    sides = (jnp.logical_not(even), even)
    wides = [jnp.where(upper, planes - HALO, 0) for upper in sides]
    thins = [jnp.where(upper, planes - THIN, 0) for upper in sides]
    quarter = planes // 4
    pairs = [(right_hbm, right_s)]
    for side in range(2):
        thin = pl.ds(thins[side], THIN)
        pairs.append((wet_hbm.at[thin], thin_wet.at[side]))
        pairs.append((tx_hbm.at[pl.ds(wides[side], HALO)], halo_s.at[side, pl.ds(H_TX, HALO)]))
        for k, field in enumerate((ty_hbm, tz_hbm, st_hbm)):
            pairs.append((field.at[thin], halo_s.at[side, pl.ds(H_REST + k * THIN, THIN)]))
    edge = len(pairs)
    for k in (0, 3, 1, 2):
        span = pl.ds(k * quarter, quarter)
        pairs.append((basis_hbm.at[:, span], basis_s.at[:, span]))
    pairs += [(owned_hbm, owned_s), (coupling_hbm, coupling_s)]
    loads = started(pairs, sems)

    for copy in loads[: edge + 2]:
        copy.wait()
    stores = []
    for side in range(2):
        for i in range(NBF):
            halo_s[side, pl.ds(i * HALO, HALO)] = basis_s[i, pl.ds(wides[side], HALO)]
        for k in range(THIN):
            field = right_s[thins[side] + k]
            high = field.astype(BF16)
            halo_s[side, H_WET + k] = thin_wet[side, k].astype(F32).astype(BF16)
            halo_s[side, H_WET + THIN + k] = high
            halo_s[side, H_WET + 2 * THIN + k] = (field - high.astype(F32)).astype(BF16)
        stores += started(
            ((halo_s.at[side], (far_hbm, near_hbm)[side]),), sems, len(loads) + side
        )
    for copy in loads[edge + 2 :]:
        copy.wait()
    coarse = restrict_to(lambda i, x: basis_s[i, x], lambda x: right_s[x], planes)
    slot = lax.broadcasted_iota(jnp.int32, (PER, 1), 0)
    block = jnp.zeros((PER, 1), jnp.int32)
    for s in range(PER):
        block = jnp.where(slot == s, owned_s[me * PER + s], block)
    tail = jnp.concatenate(
        [coarse, block.astype(F32), jnp.zeros((PER, 128 - NBF - 1), F32)], axis=1
    )
    wide = jnp.concatenate([coupling_s[...], jnp.zeros((KROWS, 128 - PER), F32)], axis=1)
    rows_s[...] = jnp.concatenate([wide.T[:PER], tail], axis=1)
    stores += started(
        [(rows_s, packed_hbm.at[e]) for e in range(count)], sems, len(loads) + 2
    )
    for copy in stores:
        copy.wait()


def coarse_solve(coupling_at, inverse_at, residual):
    lane = lax.broadcasted_iota(jnp.int32, (NBF, WIN), 1)
    in_z, in_y = lane % NZB, (lane // NZB) % NYB

    def rows_of(parts):
        return jnp.concatenate([jnp.sum(p, axis=0, keepdims=True) for p in parts], 0)

    def inverted(v):
        return rows_of([inverse_at(i) * v for i in range(NBF)])

    values = inverted(residual)
    for _ in range(CSWEEPS - 1):
        near = (
            pltpu.roll(values, WIN - PER, 1),
            pltpu.roll(values, PER, 1),
            jnp.where(in_y < NYB - 1, pltpu.roll(values, WIN - NZB, 1), 0.0),
            jnp.where(in_y > 0, pltpu.roll(values, NZB, 1), 0.0),
            jnp.where(in_z < NZB - 1, pltpu.roll(values, WIN - 1, 1), 0.0),
            jnp.where(in_z > 0, pltpu.roll(values, 1, 1), 0.0),
        )
        parts = []
        for i in range(NBF):
            total = coupling_at(0, i) * near[0]
            for k in range(1, NNB):
                total = total + coupling_at(k, i) * near[k]
            parts.append(total)
        values = inverted(residual - rows_of(parts))
    return values


def spread_blocks(values):
    width = 3 * NYB * 128
    block = lax.broadcasted_iota(jnp.int32, (128, width), 0)
    column = lax.broadcasted_iota(jnp.int32, (128, width), 1)
    wanted = (LEAD - 1) * PER + column // BLK
    chosen = (block == wanted).astype(F32).astype(BF16)
    stacked = jnp.concatenate(three_parts(values[:, :128]), axis=0)
    spread = jnp.dot(stacked, chosen, preferred_element_type=F32)
    return spread[:NBF] + spread[NBF : 2 * NBF] + spread[2 * NBF :]


def coefficients(coef_ref, x, quarters, right, east, west, north, upper, storage):
    in_y = lax.broadcasted_iota(jnp.int32, north.shape, 0)
    in_z = lax.broadcasted_iota(jnp.int32, north.shape, 1)
    last_y, last_z = north.shape[0] - 1, north.shape[1] - 1
    east, west, north, upper = (a.astype(F32) for a in (east, west, north, upper))
    wet = quarters * 0.25
    dry = 1.0 - jnp.minimum(quarters, 1.0)
    south = jnp.where(in_y > 0, pltpu.roll(north, 1, 0), 0.0)
    lower = jnp.where(in_z > 0, pltpu.roll(upper, 1, 1), 0.0)
    diag = wet * (storage.astype(F32) + east + west + north + south + upper + lower) + dry
    share = OMEGA / diag
    scale = wet * share
    coef_ref[x, 0] = scale * east
    coef_ref[x, 1] = scale * west
    coef_ref[x, 2] = jnp.where(in_y < last_y, scale * north, 0.0)
    coef_ref[x, 3] = scale * south
    coef_ref[x, 4] = jnp.where(in_z < last_z, scale * upper, 0.0)
    coef_ref[x, 5] = scale * lower
    coef_ref[x, 6] = right * share
    coef_ref[x, 7] = diag * (1.0 / OMEGA)


def prepare_kernel(
    right_hbm, wet_hbm, tx_hbm, ty_hbm, tz_hbm, st_hbm, all_inverse_hbm,
    right_ref, wet_ref, tx_ref, ty_ref, tz_ref, st_ref, inverse_ref, _room_ref, _more_room_ref,
    quarters, all_inverse, sems,
):
    me = lax.axis_index("gx")
    pairs = (
        (right_hbm, right_ref), (wet_hbm, quarters), (tx_hbm, tx_ref), (ty_hbm, ty_ref), (tz_hbm, tz_ref),
        (st_hbm, st_ref), (all_inverse_hbm, all_inverse),
    )
    for copy in started(pairs, sems):
        copy.wait()
    wet_ref[...] = quarters[...].astype(F32).astype(BF16)
    blocks = all_inverse.shape[1]
    start = (me - LEAD) * PER
    turned = pltpu.roll(all_inverse[...], lax.rem(blocks - start, blocks), 1)[:, :WIN]
    block = lax.broadcasted_iota(jnp.int32, turned.shape, 1) + start
    inverse_ref[...] = jnp.where((block >= 0) & (block < blocks), turned, 0.0)


def all_coefficients(coef_ref, near_ref, far_ref, statics, tx_s, even):
    right_ref, wet_ref, tx_ref, ty_ref, tz_ref, st_ref = statics
    planes = right_ref.shape[0]
    top = planes + HALO
    tx_s[HALO] = tx_ref[0]
    tx_s[top - 1] = tx_ref[planes - 1]
    for halo, wide in ((near_ref, jnp.where(even, top, 0)), (far_ref, jnp.where(even, 0, top))):
        tx_s[pl.ds(wide, HALO)] = halo[pl.ds(H_TX, HALO)]

    def own(x, before):
        coefficients(
            coef_ref, x + HALO, wet_ref[x].astype(F32), right_ref[x], tx_ref[x], before, ty_ref[x], tz_ref[x],
            st_ref[x],
        )

    planes_in_groups(1, planes, 5, lambda x: own(x, tx_ref[x - 1]))
    own(0, tx_s[HALO - 1])
    for halo, thin in ((near_ref, jnp.where(even, top, 1)), (far_ref, jnp.where(even, 1, top))):
        for k in range(THIN):
            right = halo[H_WET + THIN + k].astype(F32) + halo[H_WET + 2 * THIN + k].astype(F32)
            coefficients(
                coef_ref, thin + k, halo[H_WET + k].astype(F32), right, tx_s[thin + k],
                tx_s[thin + k - 1], halo[H_REST + k], halo[H_REST + THIN + k],
                halo[H_REST + 2 * THIN + k],
            )


def window_of(gathered_ref, window_s, me, count, first):
    window_s[...] = jnp.zeros_like(window_s)
    for e in range(count):
        window_s[pl.ds(LEAD * PER + e * PER, PER)] = gathered_ref[e, :, pl.ds(first, 128)]
    return window_s[pl.ds(pl.multiple_of(me * PER, PER), WIN)].T[:NBF]


def blocks_in_order(gathered_ref, coupling_ref, me, count):
    lane = lax.broadcasted_iota(jnp.int32, (WIN, WIN), 1) + (me - LEAD) * PER
    for part in range(count * PER // WIN):
        span = pl.ds(part * (WIN // PER), WIN // PER)
        rows = gathered_ref[span].reshape(WIN, KROWS + 128)
        block = rows[:, KROWS + NBF : KROWS + NBF + 1].astype(jnp.int32)
        chosen = (block == lane).astype(F32).astype(BF16)
        stacked = jnp.concatenate(three_parts(rows[:, :KROWS].T), axis=0)
        found = jnp.dot(stacked, chosen, preferred_element_type=F32)
        found = found[:KROWS] + found[KROWS : 2 * KROWS] + found[2 * KROWS :]
        coupling_ref[...] = found if part == 0 else coupling_ref[...] + found


def corrected_values(coupling_ref, inverse_ref, residual):
    values = coarse_solve(
        lambda k, i: coupling_ref[pl.ds((k * NBF + i) * NBF, NBF)],
        lambda i: inverse_ref[pl.ds(i * NBF, NBF)],
        residual,
    )
    return spread_blocks(values)


def prolong(state, spread, basis_ref, near_ref, far_ref, even, planes, before):
    top = planes + HALO

    def gains_of(values):
        return [
            [
                jnp.broadcast_to(values[i : i + 1, yb * 128 : (yb + 1) * 128], (BLK, 128))
                for i in range(NBF)
            ]
            for yb in range(NYB)
        ]

    def plane(x, at, gains, base):
        for yb in range(NYB):
            rows = slice(yb * BLK, (yb + 1) * BLK)
            total = at(0, rows).astype(F32) * gains[yb][0]
            for i in range(1, NBF):
                total = total + at(i, rows).astype(F32) * gains[yb][i]
            state[x, rows] = total if base is None else base[rows] + total

    width = NYB * 128
    below, own, above = (spread[:, s * width : (s + 1) * width] for s in range(3))
    for near, halo, wide in (
        (True, near_ref, jnp.where(even, top, 0)), (False, far_ref, jnp.where(even, 0, top))
    ):
        upper = even if near else jnp.logical_not(even)
        gains = gains_of(jnp.where(upper, above, below))
        for k in range(HALO):
            base = before(k, near)
            plane(wide + k, lambda i, rows: halo[i * HALO + k, rows], gains, base)
    gains = gains_of(own)

    def step(x):
        plane(x + HALO, lambda i, rows: basis_ref[i, x, rows], gains, before(x, None))

    planes_in_groups(0, planes, 4, step)


def pulled(coef_ref, state, x):
    here = state[x]
    ny, nz = here.shape
    total = coef_ref[x, 6] + coef_ref[x, 0] * state[x + 1] + coef_ref[x, 1] * state[x - 1]
    total = total + coef_ref[x, 2] * pltpu.roll(here, ny - 1, 0) + coef_ref[x, 3] * pltpu.roll(here, 1, 0)
    total = total + coef_ref[x, 4] * pltpu.roll(here, nz - 1, 1) + coef_ref[x, 5] * pltpu.roll(here, 1, 1)
    return here, total


def smooth(coef_ref, one, two, planes):
    source, target = one, two
    for k in range(SWEEPS):

        def step(x):
            here, total = pulled(coef_ref, source, x)
            target[x] = (1.0 - OMEGA) * here + total

        low, high = k + 1, planes + 2 * HALO - 1 - k
        planes_in_groups(low, high, (high - low) // 2, step)
        source, target = target, source
    return source, target


def misfit(coef_ref, source, x):
    here, total = pulled(coef_ref, source, x)
    return (total - OMEGA * here) * coef_ref[x, 7]


def second_kernel(
    count, basis_hbm, gathered_ref, inverse_ref, near_ref, far_ref, *refs
):
    statics, refs = refs[:6], refs[8:]
    pressure_ref, coupling_ref, send_near_hbm, send_far_hbm, packed_hbm = refs[:5]
    coef_ref, one_s, two_s, tx_s, window_s, tail_s, basis_ref, sems = refs[5:]
    load = started(((basis_hbm, basis_ref),), sems, 2 + count)
    planes = pressure_ref.shape[0]
    me = lax.axis_index("gx")
    even = lax.rem(me, 2) == 0
    blocks_in_order(gathered_ref, coupling_ref, me, count)
    spread = corrected_values(
        coupling_ref, inverse_ref, window_of(gathered_ref, window_s, me, count, KROWS)
    )
    all_coefficients(coef_ref, near_ref, far_ref, statics, tx_s, even)
    load[0].wait()
    prolong(one_s, spread, basis_ref, near_ref, far_ref, even, planes, lambda k, near: None)
    source, target = smooth(coef_ref, one_s, two_s, planes)
    near_from, far_from = jnp.where(even, planes, HALO), jnp.where(even, HALO, planes)
    stores = started(
        (
            (source.at[pl.ds(far_from, HALO)], send_far_hbm),
            (source.at[pl.ds(near_from, HALO)], send_near_hbm),
        ),
        sems,
    )
    pressure_ref[...] = source[pl.ds(HALO, planes)]

    def step(x):
        target[x] = misfit(coef_ref, source, x)

    planes_in_groups(HALO, planes + HALO, 8, step)
    coarse = restrict_to(lambda i, x: basis_ref[i, x], lambda x: target[x + HALO], planes)
    tail_s[...] = jnp.concatenate([coarse, jnp.zeros((PER, 128 - NBF), F32)], axis=1)
    stores += started([(tail_s, packed_hbm.at[e]) for e in range(count)], sems, 2)
    for copy in stores:
        copy.wait()


def last_kernel(
    count, basis_hbm, gathered_ref, inverse_ref, near_ref, far_ref, coupling_ref, pressure_ref, near_p_ref,
    far_p_ref, *refs
):
    statics, refs = refs[:6], refs[6:]
    pressure_out, residual_out, coef_ref, one_s, two_s, tx_s, residual_s, window_s, basis_ref, sems = refs
    load = started(((basis_hbm, basis_ref),), sems, 3)
    planes = pressure_ref.shape[0]
    me = lax.axis_index("gx")
    even = lax.rem(me, 2) == 0
    spread = corrected_values(
        coupling_ref, inverse_ref, window_of(gathered_ref, window_s, me, count, 0)
    )

    def before(k, near):
        if near is None:
            return pressure_ref[k]
        return near_p_ref[k] if near else far_p_ref[k]

    all_coefficients(coef_ref, near_ref, far_ref, statics, tx_s, even)
    load[0].wait()
    prolong(one_s, spread, basis_ref, near_ref, far_ref, even, planes, before)
    source, _ = smooth(coef_ref, one_s, two_s, planes)
    stores = started(((source.at[pl.ds(HALO, planes)], pressure_out),), sems)
    half = planes // 2

    def step(x):
        residual_s[x - HALO] = misfit(coef_ref, source, x)

    for k in range(2):
        planes_in_groups(HALO + k * half, HALO + (k + 1) * half, half, step)
        span = pl.ds(k * half, half)
        stores += started(((residual_s.at[span], residual_out.at[span]),), sems, 1 + k)
    for copy in stores:
        copy.wait()


VMEM = pl.BlockSpec(memory_space=pltpu.VMEM)
ANY = pl.BlockSpec(memory_space=pl.ANY)


def kernel_call(name, body, arguments, outputs, scratch, aliases=None):
    spec = {pltpu.HBM: ANY, pltpu.VMEM: VMEM}
    call = pl.pallas_call(
        body,
        out_shape=[space(shape, dtype) for space, shape, dtype in outputs],
        in_specs=[spec[space] for space, _ in arguments],
        out_specs=[spec[space] for space, _, _ in outputs],
        scratch_shapes=scratch,
        input_output_aliases=aliases or {},
        compiler_params=pltpu.CompilerParams(vmem_limit_bytes=16 * 1024 * 1024),
        name=name,
    )
    return call(*[pltpu.with_memory_space_constraint(value, space) for space, value in arguments])


def local(
    right_side, wet_quarters, trans_x, trans_y, trans_z, storage, basis, coupling, coarse_inverse,
    owned_block, block_slot, neighbours,
):
    count = lax.axis_size("gx")
    planes, ny, nz = right_side.shape
    field = (ny, nz)
    full = planes + 2 * HALO
    near_pairs = [(i, i ^ 1) for i in range(count)]
    far_pairs = [(i, i + 1) for i in range(1, count - 1, 2)]
    far_pairs = far_pairs + [(b, a) for a, b in far_pairs]
    H, V = pltpu.HBM, pltpu.VMEM
    statics = [(H, a) for a in (right_side, wet_quarters, trans_x, trans_y, trans_z, storage)]
    halo = (H_ALL,) + field

    near, far, packed = kernel_call(
        "restrict_first",
        functools.partial(first_kernel, count),
        [(H, owned_block), (H, basis), *statics, (H, coupling.reshape(KROWS, PER))],
        [(H, halo, BF16), (H, halo, BF16), (H, (count, PER, KROWS + 128), F32)],
        [
            pltpu.SMEM(owned_block.shape, jnp.int32),
            pltpu.VMEM(basis.shape, BF16),
            pltpu.VMEM(right_side.shape, F32),
            pltpu.VMEM((2, THIN) + field, jnp.int32),
            pltpu.VMEM((KROWS, PER), F32),
            pltpu.VMEM((PER, KROWS + 128), F32),
            pltpu.VMEM((2,) + halo, BF16),
            pltpu.SemaphoreType.DMA((20 + count,)),
        ],
    )
    far = lax.ppermute(far, "gx", far_pairs)
    near = lax.ppermute(near, "gx", near_pairs)
    gathered = lax.all_to_all(packed, "gx", 0, 0, tiled=True)

    blocks = coarse_inverse.shape[2]
    *fields, inverse, room, more_room = kernel_call(
        "prepare",
        prepare_kernel,
        [*statics, (H, coarse_inverse.reshape(NBF * NBF, blocks))],
        [(V, right_side.shape, F32)]
        + [(V, right_side.shape, BF16)] * 5
        + [(V, (NBF * NBF, WIN), F32), (V, right_side.shape, F32), (V, (KROWS, WIN), F32)],
        [
            pltpu.VMEM(right_side.shape, jnp.int32),
            pltpu.VMEM((NBF * NBF, blocks), F32),
            pltpu.SemaphoreType.DMA((7,)),
        ],
    )

    factors = pltpu.VMEM((full, 8) + field, F32)
    state = pltpu.VMEM((full,) + field, F32)
    window = pltpu.VMEM((count * PER + WIN, 128), F32)
    around = pltpu.VMEM((full,) + field, BF16)
    pressure, coupled, send_near, send_far, packed = kernel_call(
        "iteration_first",
        functools.partial(second_kernel, count),
        [(H, basis)] + [(V, a) for a in (gathered, inverse, near, far, *fields, room, more_room)],
        [
            (V, (planes,) + field, F32),
            (V, (KROWS, WIN), F32),
            (H, (HALO,) + field, F32),
            (H, (HALO,) + field, F32),
            (H, (count, PER, 128), F32),
        ],
        [
            factors, state, state, around, window,
            pltpu.VMEM((PER, 128), F32), pltpu.VMEM(basis.shape, BF16), pltpu.SemaphoreType.DMA((3 + count,)),
        ],
        {11: 0, 12: 1},
    )

    far_p = lax.ppermute(send_far, "gx", far_pairs)
    near_p = lax.ppermute(send_near, "gx", near_pairs)
    gathered = lax.all_to_all(packed, "gx", 0, 0, tiled=True)
    whole = (H, (planes,) + field, F32)
    return kernel_call(
        "iteration_last",
        functools.partial(last_kernel, count),
        [(H, basis)]
        + [(V, a) for a in (gathered, inverse, near, far, coupled, pressure, near_p, far_p, *fields)],
        [whole, whole],
        [
            factors, state, state, around,
            pltpu.VMEM((planes,) + field, F32), window, pltpu.VMEM(basis.shape, BF16),
            pltpu.SemaphoreType.DMA((4,)),
        ],
    )


def solution(mesh):
    slabs = P(("parts", "gx"), None, None)
    placed = (
        slabs, slabs, slabs, slabs, slabs, slabs,
        P(None, ("parts", "gx"), None, None),
        P(None, None, None, ("parts", "gx")),
        P(None, None, "parts"),
        P(),
        P("gx"),
        P(None, "gx"),
    )
    return jax.shard_map(local, mesh=mesh, in_specs=placed, out_specs=(slabs, slabs), check_vma=False)
```

```python
import functools

import jax
import jax.numpy as jnp
from jax import lax
from jax.experimental import pallas as pl
from jax.experimental.pallas import tpu as pltpu
from jax.sharding import PartitionSpec as P

BLK = 16
NBF = 8
NNB = 6
SWEEPS = 3
CSWEEPS = 4
NYB = 2
NZB = 8
PER = NYB * NZB
WIN = 16 * PER
LEAD = 4
HALO = 4
OMEGA = 2.0 / 3.0
KROWS = NNB * NBF * NBF
F32 = jnp.float32
BF16 = jnp.bfloat16

THIN = HALO - 1
H_TX = NBF * HALO
H_REST = H_TX + HALO
H_WET = H_REST + 3 * THIN
H_ALL = H_REST + 6 * THIN


def planes_in_groups(low, high, group, step):
    count = (high - low) // group

    def body(k, carry):
        for j in range(group):
            step(low + k * group + j)
        return carry

    lax.fori_loop(0, count, body, 0)
    for x in range(low + count * group, high):
        step(x)


def three_parts(x):
    high = x.astype(BF16)
    rest = x - high.astype(F32)
    middle = rest.astype(BF16)
    low = (rest - middle.astype(F32)).astype(BF16)
    return high, middle, low


def restrict_to(basis_at, field_at, planes):
    def step(x, totals):
        field = field_at(x)
        out = []
        for i in range(NBF):
            for yb in range(NYB):
                rows = slice(yb * BLK, (yb + 1) * BLK)
                product = basis_at(i, x)[rows].astype(F32) * field[rows]
                out.append(totals[i * NYB + yb] + product[:8] + product[8:])
        return tuple(out)

    zero = jnp.zeros((8, 128), F32)
    totals = lax.fori_loop(0, planes, step, (zero,) * (NBF * NYB))
    groups = lax.broadcasted_iota(jnp.int32, (NZB, 3 * 128), 1)
    owner = lax.broadcasted_iota(jnp.int32, (NZB, 3 * 128), 0)
    spread = ((groups % 128) // BLK == owner).astype(F32).astype(BF16)
    halves = []
    for yb in range(NYB):
        rows = [jnp.sum(totals[i * NYB + yb], axis=0, keepdims=True) for i in range(NBF)]
        stacked = jnp.concatenate(three_parts(jnp.concatenate(rows, 0)), axis=1)
        halves.append(
            lax.dot_general(
                spread, stacked, (((1,), (1,)), ((), ())), preferred_element_type=F32
            )
        )
    return jnp.concatenate(halves, 0)


def started(pairs, sems, first=0):
    copies = [pltpu.make_async_copy(a, b, sems.at[first + k]) for k, (a, b) in enumerate(pairs)]
    for copy in copies:
        copy.start()
    return copies


def first_kernel(
    owned_hbm, basis_hbm, right_hbm, wet_hbm, tx_hbm, ty_hbm, tz_hbm, st_hbm, coupling_hbm,
    near_hbm, far_hbm, packed_hbm, owned_s, basis_s, right_s, thin_wet, coupling_s, rows_s, halo_s, sems,
):
    me = lax.axis_index("gx")
    even = lax.rem(me, 2) == 0
    planes = right_s.shape[0]
    sides = (jnp.logical_not(even), even)
    wides = [jnp.where(upper, planes - HALO, 0) for upper in sides]
    thins = [jnp.where(upper, planes - THIN, 0) for upper in sides]
    quarter = planes // 4
    pairs = [(right_hbm, right_s)]
    for side in range(2):
        thin = pl.ds(thins[side], THIN)
        pairs.append((wet_hbm.at[thin], thin_wet.at[side]))
        pairs.append((tx_hbm.at[pl.ds(wides[side], HALO)], halo_s.at[side, pl.ds(H_TX, HALO)]))
        for k, field in enumerate((ty_hbm, tz_hbm, st_hbm)):
            pairs.append((field.at[thin], halo_s.at[side, pl.ds(H_REST + k * THIN, THIN)]))
    edge = len(pairs)
    for k in (0, 3, 1, 2):
        span = pl.ds(k * quarter, quarter)
        pairs.append((basis_hbm.at[:, span], basis_s.at[:, span]))
    pairs += [(owned_hbm, owned_s), (coupling_hbm, coupling_s)]
    loads = started(pairs, sems)

    for copy in loads[: edge + 2]:
        copy.wait()
    stores = []
    for side in range(2):
        for i in range(NBF):
            halo_s[side, pl.ds(i * HALO, HALO)] = basis_s[i, pl.ds(wides[side], HALO)]
        for k in range(THIN):
            field = right_s[thins[side] + k]
            high = field.astype(BF16)
            halo_s[side, H_WET + k] = thin_wet[side, k].astype(F32).astype(BF16)
            halo_s[side, H_WET + THIN + k] = high
            halo_s[side, H_WET + 2 * THIN + k] = (field - high.astype(F32)).astype(BF16)
        stores += started(
            ((halo_s.at[side], (far_hbm, near_hbm)[side]),), sems, len(loads) + side
        )
    for copy in loads[edge + 2 :]:
        copy.wait()
    coarse = restrict_to(lambda i, x: basis_s[i, x], lambda x: right_s[x], planes)
    slot = lax.broadcasted_iota(jnp.int32, (PER, 1), 0)
    block = jnp.zeros((PER, 1), jnp.int32)
    for s in range(PER):
        block = jnp.where(slot == s, owned_s[me * PER + s], block)
    tail = jnp.concatenate(
        [coarse, block.astype(F32), jnp.zeros((PER, 128 - NBF - 1), F32)], axis=1
    )
    wide = jnp.concatenate([coupling_s[...], jnp.zeros((KROWS, 128 - PER), F32)], axis=1)
    rows_s[...] = jnp.concatenate([wide.T[:PER], tail], axis=1)
    stores += started(
        [(rows_s, packed_hbm.at[chip]) for chip in range(packed_hbm.shape[0])], sems, len(loads) + 3
    )
    for copy in stores:
        copy.wait()


def coarse_solve(coupling_at, inverse_at, residual):
    lane = lax.broadcasted_iota(jnp.int32, (NBF, WIN), 1)
    in_z, in_y = lane % NZB, (lane // NZB) % NYB

    def rows_of(parts):
        return jnp.concatenate([jnp.sum(p, axis=0, keepdims=True) for p in parts], 0)

    def inverted(v):
        return rows_of([inverse_at(i) * v for i in range(NBF)])

    values = inverted(residual)
    for _ in range(CSWEEPS - 1):
        near = (
            pltpu.roll(values, WIN - PER, 1),
            pltpu.roll(values, PER, 1),
            jnp.where(in_y < NYB - 1, pltpu.roll(values, WIN - NZB, 1), 0.0),
            jnp.where(in_y > 0, pltpu.roll(values, NZB, 1), 0.0),
            jnp.where(in_z < NZB - 1, pltpu.roll(values, WIN - 1, 1), 0.0),
            jnp.where(in_z > 0, pltpu.roll(values, 1, 1), 0.0),
        )
        parts = []
        for i in range(NBF):
            total = coupling_at(0, i) * near[0]
            for k in range(1, NNB):
                total = total + coupling_at(k, i) * near[k]
            parts.append(total)
        values = inverted(residual - rows_of(parts))
    return values


def spread_blocks(values):
    width = 3 * NYB * 128
    block = lax.broadcasted_iota(jnp.int32, (128, width), 0)
    column = lax.broadcasted_iota(jnp.int32, (128, width), 1)
    wanted = (LEAD - 1) * PER + column // BLK
    chosen = (block == wanted).astype(F32).astype(BF16)
    stacked = jnp.concatenate(three_parts(values[:, :128]), axis=0)
    spread = jnp.dot(stacked, chosen, preferred_element_type=F32)
    return spread[:NBF] + spread[NBF : 2 * NBF] + spread[2 * NBF :]


def coefficients(coef_ref, x, quarters, right, east, west, north, upper, storage):
    in_y = lax.broadcasted_iota(jnp.int32, north.shape, 0)
    in_z = lax.broadcasted_iota(jnp.int32, north.shape, 1)
    last_y, last_z = north.shape[0] - 1, north.shape[1] - 1
    east, west, north, upper = (a.astype(F32) for a in (east, west, north, upper))
    wet = quarters * 0.25
    dry = 1.0 - jnp.minimum(quarters, 1.0)
    south = jnp.where(in_y > 0, pltpu.roll(north, 1, 0), 0.0)
    lower = jnp.where(in_z > 0, pltpu.roll(upper, 1, 1), 0.0)
    diag = wet * (storage.astype(F32) + east + west + north + south + upper + lower) + dry
    share = OMEGA / diag
    scale = wet * share
    coef_ref[x, 0] = scale * east
    coef_ref[x, 1] = scale * west
    coef_ref[x, 2] = jnp.where(in_y < last_y, scale * north, 0.0)
    coef_ref[x, 3] = scale * south
    coef_ref[x, 4] = jnp.where(in_z < last_z, scale * upper, 0.0)
    coef_ref[x, 5] = scale * lower
    coef_ref[x, 6] = right * share
    coef_ref[x, 7] = diag * (1.0 / OMEGA)


def prepare_kernel(
    right_hbm, wet_hbm, tx_hbm, ty_hbm, tz_hbm, st_hbm, all_inverse_hbm,
    right_ref, wet_ref, tx_ref, ty_ref, tz_ref, st_ref, inverse_ref, _room_ref, _more_room_ref,
    quarters, all_inverse, sems,
):
    me = lax.axis_index("gx")
    pairs = (
        (right_hbm, right_ref), (wet_hbm, quarters), (tx_hbm, tx_ref), (ty_hbm, ty_ref), (tz_hbm, tz_ref),
        (st_hbm, st_ref), (all_inverse_hbm, all_inverse),
    )
    for copy in started(pairs, sems):
        copy.wait()
    wet_ref[...] = quarters[...].astype(F32).astype(BF16)
    blocks = all_inverse.shape[1]
    start = (me - LEAD) * PER
    turned = pltpu.roll(all_inverse[...], lax.rem(blocks - start, blocks), 1)[:, :WIN]
    block = lax.broadcasted_iota(jnp.int32, turned.shape, 1) + start
    inverse_ref[...] = jnp.where((block >= 0) & (block < blocks), turned, 0.0)


def all_coefficients(coef_ref, near_ref, far_ref, statics, tx_s, even):
    right_ref, wet_ref, tx_ref, ty_ref, tz_ref, st_ref = statics
    planes = right_ref.shape[0]
    top = planes + HALO
    tx_s[HALO] = tx_ref[0]
    tx_s[top - 1] = tx_ref[planes - 1]
    for halo, wide in ((near_ref, jnp.where(even, top, 0)), (far_ref, jnp.where(even, 0, top))):
        tx_s[pl.ds(wide, HALO)] = halo[pl.ds(H_TX, HALO)]

    def own(x, before):
        coefficients(
            coef_ref, x + HALO, wet_ref[x].astype(F32), right_ref[x], tx_ref[x], before, ty_ref[x], tz_ref[x],
            st_ref[x],
        )

    planes_in_groups(1, planes, 5, lambda x: own(x, tx_ref[x - 1]))
    own(0, tx_s[HALO - 1])
    for halo, thin in ((near_ref, jnp.where(even, top, 1)), (far_ref, jnp.where(even, 1, top))):
        for k in range(THIN):
            right = halo[H_WET + THIN + k].astype(F32) + halo[H_WET + 2 * THIN + k].astype(F32)
            coefficients(
                coef_ref, thin + k, halo[H_WET + k].astype(F32), right, tx_s[thin + k],
                tx_s[thin + k - 1], halo[H_REST + k], halo[H_REST + THIN + k],
                halo[H_REST + 2 * THIN + k],
            )


def window_of(pieces, window_s, me):
    window_s[...] = jnp.zeros_like(window_s)
    for device, piece in pieces:
        window_s[pl.ds(pl.multiple_of((LEAD + device) * PER, PER), PER)] = piece
    return window_s[pl.ds(pl.multiple_of(me * PER, PER), WIN)].T[:NBF]


def blocks_in_order(halves, coupling_ref, me):
    lane = lax.broadcasted_iota(jnp.int32, (WIN, WIN), 1) + (me - LEAD) * PER
    tall = halves[0].shape[0]
    for start in range(0, 2 * tall, WIN):
        if tall >= WIN:
            rows = halves[start // tall][pl.ds(start % tall, WIN)]
        else:
            rows = jnp.concatenate([half[...] for half in halves], axis=0)
        block = rows[:, KROWS + NBF : KROWS + NBF + 1].astype(jnp.int32)
        chosen = (block == lane).astype(F32).astype(BF16)
        stacked = jnp.concatenate(three_parts(rows[:, :KROWS].T), axis=0)
        found = jnp.dot(stacked, chosen, preferred_element_type=F32)
        found = found[:KROWS] + found[KROWS : 2 * KROWS] + found[2 * KROWS :]
        coupling_ref[...] = found if start == 0 else coupling_ref[...] + found


def corrected_values(coupling_ref, inverse_ref, residual):
    values = coarse_solve(
        lambda k, i: coupling_ref[pl.ds((k * NBF + i) * NBF, NBF)],
        lambda i: inverse_ref[pl.ds(i * NBF, NBF)],
        residual,
    )
    return spread_blocks(values)


def gains_of(values):
    return [
        [
            jnp.broadcast_to(values[i : i + 1, yb * 128 : (yb + 1) * 128], (BLK, 128))
            for i in range(NBF)
        ]
        for yb in range(NYB)
    ]


def prolong_plane(state, x, basis_at, gains, base):
    for yb in range(NYB):
        rows = slice(yb * BLK, (yb + 1) * BLK)
        total = basis_at(0, rows).astype(F32) * gains[yb][0]
        for i in range(1, NBF):
            total = total + basis_at(i, rows).astype(F32) * gains[yb][i]
        state[x, rows] = total if base is None else base[rows] + total


def prolong_own(state, first, spread, basis_ref, pressure_ref=None):
    width = NYB * 128
    gains = gains_of(spread[:, width : 2 * width])

    def step(x):
        base = None if pressure_ref is None else pressure_ref[x]
        prolong_plane(state, x + first, lambda i, rows: basis_ref[i, x, rows], gains, base)

    planes_in_groups(0, basis_ref.shape[1], 4, step)


def prolong_halo(state, spread, near_ref, far_ref, even, planes, near_p=None, far_p=None):
    top = planes + HALO
    width = NYB * 128
    below, above = spread[:, :width], spread[:, 2 * width :]
    for halo, before, upper in ((near_ref, near_p, even), (far_ref, far_p, jnp.logical_not(even))):
        gains = gains_of(jnp.where(upper, above, below))
        wide = jnp.where(upper, top, 0)
        for k in range(HALO):
            base = None if before is None else before[k]
            prolong_plane(state, wide + k, lambda i, rows: halo[i * HALO + k, rows], gains, base)


def pulled(coef_ref, state, x):
    here = state[x]
    ny, nz = here.shape
    total = coef_ref[x, 6] + coef_ref[x, 0] * state[x + 1] + coef_ref[x, 1] * state[x - 1]
    total = total + coef_ref[x, 2] * pltpu.roll(here, ny - 1, 0) + coef_ref[x, 3] * pltpu.roll(here, 1, 0)
    total = total + coef_ref[x, 4] * pltpu.roll(here, nz - 1, 1) + coef_ref[x, 5] * pltpu.roll(here, 1, 1)
    return here, total


def smooth(coef_ref, one, two, planes):
    source, target = one, two
    for k in range(SWEEPS):

        def step(x):
            here, total = pulled(coef_ref, source, x)
            target[x] = (1.0 - OMEGA) * here + total

        low, high = k + 1, planes + 2 * HALO - 1 - k
        planes_in_groups(low, high, (high - low) // 2, step)
        source, target = target, source
    return source, target


def misfit(coef_ref, source, x):
    here, total = pulled(coef_ref, source, x)
    return (total - OMEGA * here) * coef_ref[x, 7]


def coarse_kernel(
    count, basis_hbm, half_ref, other_ref, inverse_ref, _room, _more_room,
    corrected_ref, coupling_ref, spread_ref, window_s, basis_ref, sems,
):
    me = lax.axis_index("gx")
    load = started(((basis_hbm, basis_ref),), sems)
    blocks_in_order((half_ref, other_ref), coupling_ref, me)
    core = lax.rem(me, 2)
    pieces = []
    for chip in range(count // 2):
        rows = pl.ds(chip * PER, PER), pl.ds(KROWS, 128)
        pieces.append((2 * chip + core, half_ref[rows]))
        pieces.append((2 * chip + 1 - core, other_ref[rows]))
    spread = corrected_values(coupling_ref, inverse_ref, window_of(pieces, window_s, me))
    spread_ref[...] = spread
    load[0].wait()
    prolong_own(corrected_ref, 0, spread, basis_ref)


def second_kernel(count, basis_hbm, spread_ref, near_ref, far_ref, corrected_ref, *refs):
    statics, refs = refs[:6], refs[6:]
    pressure_ref, send_near_hbm, send_far_hbm, packed_hbm = refs[:4]
    coef_ref, one_s, two_s, tx_s, tail_s, basis_ref, sems = refs[4:]
    load = started(((basis_hbm, basis_ref),), sems, 2 + count)
    planes = pressure_ref.shape[0]
    me = lax.axis_index("gx")
    even = lax.rem(me, 2) == 0
    for x in range(planes):
        one_s[x + HALO] = corrected_ref[x]
    prolong_halo(one_s, spread_ref[...], near_ref, far_ref, even, planes)
    all_coefficients(coef_ref, near_ref, far_ref, statics, tx_s, even)
    source, target = smooth(coef_ref, one_s, two_s, planes)
    near_from, far_from = jnp.where(even, planes, HALO), jnp.where(even, HALO, planes)
    stores = started(
        (
            (source.at[pl.ds(far_from, HALO)], send_far_hbm),
            (source.at[pl.ds(near_from, HALO)], send_near_hbm),
        ),
        sems,
    )
    pressure_ref[...] = source[pl.ds(HALO, planes)]

    def step(x):
        target[x] = misfit(coef_ref, source, x)

    planes_in_groups(HALO, planes + HALO, 8, step)
    load[0].wait()
    coarse = restrict_to(lambda i, x: basis_ref[i, x], lambda x: target[x + HALO], planes)
    tail_s[...] = jnp.concatenate([coarse, jnp.zeros((PER, 128 - NBF), F32)], axis=1)
    stores += started([(tail_s, packed_hbm.at[e]) for e in range(count)], sems, 2)
    for copy in stores:
        copy.wait()


def last_kernel(
    count, basis_hbm, gathered_ref, inverse_ref, near_ref, far_ref, coupling_ref, pressure_ref, near_p_ref,
    far_p_ref, *refs
):
    statics, refs = refs[:6], refs[6:]
    pressure_out, residual_out, coef_ref, one_s, two_s, tx_s, residual_s, window_s, basis_ref, sems = refs
    load = started(((basis_hbm, basis_ref),), sems, 3)
    planes = pressure_ref.shape[0]
    me = lax.axis_index("gx")
    even = lax.rem(me, 2) == 0
    pieces = [(device, gathered_ref[device]) for device in range(count)]
    spread = corrected_values(coupling_ref, inverse_ref, window_of(pieces, window_s, me))

    all_coefficients(coef_ref, near_ref, far_ref, statics, tx_s, even)
    load[0].wait()
    prolong_own(one_s, HALO, spread, basis_ref, pressure_ref)
    prolong_halo(one_s, spread, near_ref, far_ref, even, planes, near_p_ref, far_p_ref)
    source, _ = smooth(coef_ref, one_s, two_s, planes)
    stores = started(((source.at[pl.ds(HALO, planes)], pressure_out),), sems)
    half = planes // 2

    def step(x):
        residual_s[x - HALO] = misfit(coef_ref, source, x)

    for k in range(2):
        planes_in_groups(HALO + k * half, HALO + (k + 1) * half, half, step)
        span = pl.ds(k * half, half)
        stores += started(((residual_s.at[span], residual_out.at[span]),), sems, 1 + k)
    for copy in stores:
        copy.wait()


VMEM = pl.BlockSpec(memory_space=pltpu.VMEM)
ANY = pl.BlockSpec(memory_space=pl.ANY)


def kernel_call(name, body, arguments, outputs, scratch, aliases=None):
    spec = {pltpu.HBM: ANY, pltpu.VMEM: VMEM}
    call = pl.pallas_call(
        body,
        out_shape=[space(shape, dtype) for space, shape, dtype in outputs],
        in_specs=[spec[space] for space, _ in arguments],
        out_specs=[spec[space] for space, _, _ in outputs],
        scratch_shapes=scratch,
        input_output_aliases=aliases or {},
        compiler_params=pltpu.CompilerParams(vmem_limit_bytes=16 * 1024 * 1024),
        name=name,
    )
    return call(*[pltpu.with_memory_space_constraint(value, space) for space, value in arguments])


def local(
    right_side, wet_quarters, trans_x, trans_y, trans_z, storage, basis, coupling, coarse_inverse,
    owned_block, block_slot, neighbours,
):
    count = lax.axis_size("gx")
    planes, ny, nz = right_side.shape
    field = (ny, nz)
    full = planes + 2 * HALO
    near_pairs = [(i, i ^ 1) for i in range(count)]
    far_pairs = [(i, i + 1) for i in range(1, count - 1, 2)]
    far_pairs = far_pairs + [(b, a) for a, b in far_pairs]
    H, V = pltpu.HBM, pltpu.VMEM
    statics = [(H, a) for a in (right_side, wet_quarters, trans_x, trans_y, trans_z, storage)]
    halo = (H_ALL,) + field

    near, far, packed = kernel_call(
        "restrict_first",
        first_kernel,
        [(H, owned_block), (H, basis), *statics, (H, coupling.reshape(KROWS, PER))],
        [(H, halo, BF16), (H, halo, BF16), (H, (count // 2, PER, KROWS + 128), F32)],
        [
            pltpu.SMEM(owned_block.shape, jnp.int32),
            pltpu.VMEM(basis.shape, BF16),
            pltpu.VMEM(right_side.shape, F32),
            pltpu.VMEM((2, THIN) + field, jnp.int32),
            pltpu.VMEM((KROWS, PER), F32),
            pltpu.VMEM((PER, KROWS + 128), F32),
            pltpu.VMEM((2,) + halo, BF16),
            pltpu.SemaphoreType.DMA((24 + count // 2,)),
        ],
    )
    far = lax.ppermute(far, "gx", far_pairs)
    near = lax.ppermute(near, "gx", near_pairs)
    blocks = coarse_inverse.shape[2]
    *fields, inverse, room, more_room = kernel_call(
        "prepare",
        prepare_kernel,
        [*statics, (H, coarse_inverse.reshape(NBF * NBF, blocks))],
        [(V, right_side.shape, F32)]
        + [(V, right_side.shape, BF16)] * 5
        + [(V, (NBF * NBF, WIN), F32), (V, right_side.shape, F32), (V, (KROWS, WIN), F32)],
        [
            pltpu.VMEM(right_side.shape, jnp.int32),
            pltpu.VMEM((NBF * NBF, blocks), F32),
            pltpu.SemaphoreType.DMA((7,)),
        ],
    )

    chips = [[core + 2 * chip for chip in range(count // 2)] for core in range(2)]
    half = lax.all_to_all(packed, "gx", 0, 0, axis_index_groups=chips, tiled=True)
    half = half.reshape(count // 2 * PER, KROWS + 128)
    half, near, fields = lax.optimization_barrier((half, near, fields))
    parts = [half, lax.ppermute(half, "gx", near_pairs)]

    factors = pltpu.VMEM((full, 8) + field, F32)
    state = pltpu.VMEM((full,) + field, F32)
    window = pltpu.VMEM((count * PER + WIN, 128), F32)
    around = pltpu.VMEM((full,) + field, BF16)
    corrected, coupled, spread = kernel_call(
        "coarse_first",
        functools.partial(coarse_kernel, count),
        [(H, basis)] + [(V, a) for a in (*parts, inverse, room, more_room)],
        [
            (V, (planes,) + field, F32),
            (V, (KROWS, WIN), F32),
            (V, (NBF, 3 * NYB * nz), F32),
        ],
        [window, pltpu.VMEM(basis.shape, BF16), pltpu.SemaphoreType.DMA((1,))],
        {4: 0, 5: 1},
    )
    pressure, send_near, send_far, packed = kernel_call(
        "iteration_first",
        functools.partial(second_kernel, count),
        [(H, basis)] + [(V, a) for a in (spread, near, far, corrected, *fields)],
        [
            (V, (planes,) + field, F32),
            (H, (HALO,) + field, F32),
            (H, (HALO,) + field, F32),
            (H, (count, PER, 128), F32),
        ],
        [
            factors, state, state, around,
            pltpu.VMEM((PER, 128), F32), pltpu.VMEM(basis.shape, BF16), pltpu.SemaphoreType.DMA((3 + count,)),
        ],
        {4: 0},
    )

    far_p = lax.ppermute(send_far, "gx", far_pairs)
    near_p = lax.ppermute(send_near, "gx", near_pairs)
    gathered = lax.all_to_all(packed, "gx", 0, 0, tiled=True)
    whole = (H, (planes,) + field, F32)
    return kernel_call(
        "iteration_last",
        functools.partial(last_kernel, count),
        [(H, basis)]
        + [(V, a) for a in (gathered, inverse, near, far, coupled, pressure, near_p, far_p, *fields)],
        [whole, whole],
        [
            factors, state, state, around,
            pltpu.VMEM((planes,) + field, F32), window, pltpu.VMEM(basis.shape, BF16),
            pltpu.SemaphoreType.DMA((4,)),
        ],
    )


def solution(mesh):
    slabs = P(("parts", "gx"), None, None)
    placed = (
        slabs, slabs, slabs, slabs, slabs, slabs,
        P(None, ("parts", "gx"), None, None),
        P(None, None, None, ("parts", "gx")),
        P(None, None, "parts"),
        P(),
        P("gx"),
        P(None, "gx"),
    )
    return jax.shard_map(local, mesh=mesh, in_specs=placed, out_specs=(slabs, slabs), check_vma=False)
```

```python
import functools

import jax
import jax.numpy as jnp
from jax import lax
from jax.experimental import pallas as pl
from jax.experimental.pallas import tpu as pltpu
from jax.sharding import PartitionSpec as P

BLK = 16
NBF = 8
NNB = 6
SWEEPS = 3
CSWEEPS = 4
NYB = 2
NZB = 8
PER = NYB * NZB
WIN = 16 * PER
LEAD = 4
HALO = 4
OMEGA = 2.0 / 3.0
KROWS = NNB * NBF * NBF
ROWS = (KROWS // 128 * 2 + 1) * 8
F32 = jnp.float32
BF16 = jnp.bfloat16


THIN = HALO - 1
H_TX = NBF * HALO
H_REST = H_TX + HALO
H_WET = H_REST + 3 * THIN
H_ALL = H_REST + 6 * THIN


def planes_in_groups(low, high, group, step):
    count = (high - low) // group

    def body(k, carry):
        for j in range(group):
            step(low + k * group + j)
        return carry

    if count > 1:
        lax.fori_loop(0, count, body, 0)
    elif count:
        body(0, 0)
    for x in range(low + count * group, high):
        step(x)


def three_parts(x):
    high = x.astype(BF16)
    rest = x - high.astype(F32)
    middle = rest.astype(BF16)
    low = (rest - middle.astype(F32)).astype(BF16)
    return high, middle, low


def restrict_totals(basis_at, field_at, low, high, totals=None):
    def step(x, totals):
        field = field_at(x)
        out = []
        for i in range(NBF):
            for yb in range(NYB):
                rows = slice(yb * BLK, (yb + 1) * BLK)
                product = basis_at(i, x)[rows].astype(F32) * field[rows]
                out.append(totals[i * NYB + yb] + product[:8] + product[8:])
        return tuple(out)

    if totals is None:
        totals = (jnp.zeros((8, 128), F32),) * (NBF * NYB)
    return lax.fori_loop(low, high, step, tuple(totals))


def restricted(totals):
    groups = lax.broadcasted_iota(jnp.int32, (NZB, 3 * 128), 1)
    owner = lax.broadcasted_iota(jnp.int32, (NZB, 3 * 128), 0)
    spread = ((groups % 128) // BLK == owner).astype(F32).astype(BF16)
    halves = []
    for yb in range(NYB):
        rows = [jnp.sum(totals[i * NYB + yb], axis=0, keepdims=True) for i in range(NBF)]
        stacked = jnp.concatenate(three_parts(jnp.concatenate(rows, 0)), axis=1)
        halves.append(
            lax.dot_general(
                spread, stacked, (((1,), (1,)), ((), ())), preferred_element_type=F32
            )
        )
    return halves


def restricted_tile(totals, first):
    block = lax.broadcasted_iota(jnp.int32, (128, 128), 0) // BLK + first
    lane = lax.broadcasted_iota(jnp.int32, (128, 128), 1)
    tile = 0.0
    for yb in range(NYB):
        rows = [jnp.sum(totals[i * NYB + yb], axis=0, keepdims=True) for i in range(NBF)]
        stacked = jnp.concatenate(three_parts(jnp.concatenate(rows, 0)), axis=0)
        chosen = (lane == block + yb * NZB).astype(F32).astype(BF16)
        tile = tile + jnp.dot(stacked, chosen, preferred_element_type=F32)
    return tile[:NBF] + tile[NBF : 2 * NBF] + tile[2 * NBF :]


def lane_of(device):
    return lax.rem(device, 128 // PER) * PER


def window_of_tiles(gathered_ref, me):
    count = gathered_ref.shape[0]
    halves = []
    for half in range(WIN // 128):
        total = 0.0
        for w in range(128 // PER):
            device = me - LEAD + half * (128 // PER) + w
            inside = (device >= 0) & (device < count)
            total = total + jnp.where(inside, gathered_ref[jnp.clip(device, 0, count - 1)], 0.0)
        halves.append(pltpu.roll(total, lax.rem(128 - lane_of(me + 128 // PER - LEAD), 128), 1))
    return jnp.concatenate(halves, axis=1)


def started(pairs, sems, first=0):
    copies = [pltpu.make_async_copy(a, b, sems.at[first + k]) for k, (a, b) in enumerate(pairs)]
    for copy in copies:
        copy.start()
    return copies


def is_even():
    return lax.rem(lax.axis_index("gx"), 2) == 0


def plane_at(place, planes):
    return jnp.where(is_even(), place, planes - 1 - place)


def first_kernel(
    owned_hbm, basis_hbm, right_hbm, wet_hbm, tx_hbm, ty_hbm, tz_hbm, st_hbm, coupling_hbm, all_inverse_hbm,
    near_hbm, far_hbm, packed_hbm, *rest
):
    field_refs, inverse_ref, rest = rest[:6], rest[6], rest[9:]
    (
        owned_s, basis_s, right_s, wet_s, tx_s, ty_s, tz_s, st_s, coupling_s, all_inverse, rows_s, halo_s, sems
    ) = rest
    me = lax.axis_index("gx")
    planes = right_s.shape[0]
    wides = [[plane_at(HALO - 1 - k, planes) for k in range(HALO)], [plane_at(planes - 1 - k, planes) for k in range(HALO)]]
    thins = [wides[0][1:], wides[1][:THIN]]
    quarter = planes // 4
    spans = [pl.ds(k * quarter, quarter) for k in (0, 3, 1, 2)]
    pairs = [(right_hbm, right_s)] + [(basis_hbm.at[:, span], basis_s.at[:, span]) for span in spans[:2]]
    pairs += list(zip((wet_hbm, tx_hbm, ty_hbm, tz_hbm, st_hbm), (wet_s, tx_s, ty_s, tz_s, st_s)))
    edge = len(pairs)
    pairs += [(basis_hbm.at[:, span], basis_s.at[:, span]) for span in spans[2:]]
    pairs += [(owned_hbm, owned_s), (coupling_hbm, coupling_s), (all_inverse_hbm, all_inverse)]
    loads = started(pairs, sems)

    def basis_at(i, x):
        return basis_s[i, x]

    def right_at(x):
        return right_s[x]

    loads[0].wait()
    totals = None
    for k in (0, 3):
        loads[1 + k // 3].wait()
        totals = restrict_totals(basis_at, right_at, k * quarter, (k + 1) * quarter, totals)
    for copy in loads[3:edge]:
        copy.wait()
    stores = []
    for side in range(2):
        for k in range(HALO):
            for i in range(NBF):
                halo_s[side, i * HALO + k] = basis_s[i, wides[side][k]]
            halo_s[side, H_TX + k] = tx_s[wides[side][k]]
        for k, x in enumerate(thins[side]):
            for j, field in enumerate((ty_s, tz_s, st_s)):
                halo_s[side, H_REST + j * THIN + k] = field[x]
            right = right_s[x]
            high = right.astype(BF16)
            halo_s[side, H_WET + k] = wet_s[x].astype(F32).astype(BF16)
            halo_s[side, H_WET + THIN + k] = high
            halo_s[side, H_WET + 2 * THIN + k] = (right - high.astype(F32)).astype(BF16)
        stores += started(
            ((halo_s.at[side], (far_hbm, near_hbm)[side]),), sems, len(loads) + side
        )
    for k in (1, 2):
        loads[edge + k - 1].wait()
        totals = restrict_totals(basis_at, right_at, k * quarter, (k + 1) * quarter, totals)
    for copy in loads[edge + 2 :]:
        copy.wait()
    slot = lax.broadcasted_iota(jnp.int32, (8, 1), 0)
    parts = []
    for half, coarse in enumerate(restricted(totals)):
        block = jnp.zeros((8, 1), jnp.int32)
        for s in range(8):
            block = jnp.where(slot == s, owned_s[me * PER + half * 8 + s], block)
        parts += [coarse, block.astype(F32), jnp.zeros((8, 64 - NBF - 1), F32)]
    wide = jnp.concatenate([coupling_s[...], jnp.zeros((KROWS, 128 - PER), F32)], axis=1).T
    for r in range(2):
        for l in range(KROWS // 128):
            rows_s[pl.ds((r * (KROWS // 128) + l) * 8, 8)] = wide[r * 8 : r * 8 + 8, l * 128 : l * 128 + 128]
    rows_s[pl.ds(ROWS - 8, 8)] = jnp.concatenate(parts, axis=1)
    stores += started(
        [(rows_s, packed_hbm.at[chip]) for chip in range(packed_hbm.shape[0])], sems, len(loads) + 2
    )

    def place_fields(place):
        x = plane_at(place, planes)
        for source, target in zip((right_s, wet_s, tx_s, ty_s, tz_s, st_s), field_refs):
            plane = source[x]
            target[place] = plane.astype(F32).astype(BF16) if source is wet_s else plane

    planes_in_groups(0, planes, 4, place_fields)
    blocks = all_inverse.shape[1]
    start = (me - LEAD) * PER
    turned = pltpu.roll(all_inverse[...], lax.rem(blocks - start, blocks), 1)[:, :WIN]
    block = lax.broadcasted_iota(jnp.int32, turned.shape, 1) + start
    inverse_ref[...] = jnp.where((block >= 0) & (block < blocks), turned, 0.0)
    for copy in stores:
        copy.wait()


def coarse_solve(coupling_at, inverse_at, residual):
    lane = lax.broadcasted_iota(jnp.int32, (NBF, WIN), 1)
    in_z, in_y = lane % NZB, (lane // NZB) % NYB

    def rows_of(parts):
        return jnp.concatenate([jnp.sum(p, axis=0, keepdims=True) for p in parts], 0)

    def inverted(v):
        return rows_of([inverse_at(i) * v for i in range(NBF)])

    values = inverted(residual)
    for _ in range(CSWEEPS - 1):
        near = (
            pltpu.roll(values, WIN - PER, 1),
            pltpu.roll(values, PER, 1),
            jnp.where(in_y < NYB - 1, pltpu.roll(values, WIN - NZB, 1), 0.0),
            jnp.where(in_y > 0, pltpu.roll(values, NZB, 1), 0.0),
            jnp.where(in_z < NZB - 1, pltpu.roll(values, WIN - 1, 1), 0.0),
            jnp.where(in_z > 0, pltpu.roll(values, 1, 1), 0.0),
        )
        parts = []
        for i in range(NBF):
            total = coupling_at(0, i) * near[0]
            for k in range(1, NNB):
                total = total + coupling_at(k, i) * near[k]
            parts.append(total)
        values = inverted(residual - rows_of(parts))
    return values


def spread_blocks(values):
    width = 3 * NYB * 128
    block = lax.broadcasted_iota(jnp.int32, (128, width), 0)
    column = lax.broadcasted_iota(jnp.int32, (128, width), 1)
    wanted = (LEAD - 1) * PER + column // BLK
    chosen = (block == wanted).astype(F32).astype(BF16)
    stacked = jnp.concatenate(three_parts(values[:, :128]), axis=0)
    spread = jnp.dot(stacked, chosen, preferred_element_type=F32)
    return spread[:NBF] + spread[NBF : 2 * NBF] + spread[2 * NBF :]


def coefficients(coef_ref, x, quarters, right, east, west, north, upper, storage):
    in_y = lax.broadcasted_iota(jnp.int32, north.shape, 0)
    in_z = lax.broadcasted_iota(jnp.int32, north.shape, 1)
    last_y, last_z = north.shape[0] - 1, north.shape[1] - 1
    east, west, north, upper = (a.astype(F32) for a in (east, west, north, upper))
    wet = quarters * 0.25
    dry = 1.0 - jnp.minimum(quarters, 1.0)
    south = jnp.where(in_y > 0, pltpu.roll(north, 1, 0), 0.0)
    lower = jnp.where(in_z > 0, pltpu.roll(upper, 1, 1), 0.0)
    diag = wet * (storage.astype(F32) + east + west + north + south + upper + lower) + dry
    share = OMEGA / diag
    scale = wet * share
    coef_ref[x, 0] = scale * east
    coef_ref[x, 1] = scale * west
    coef_ref[x, 2] = jnp.where(in_y < last_y, scale * north, 0.0)
    coef_ref[x, 3] = scale * south
    coef_ref[x, 4] = jnp.where(in_z < last_z, scale * upper, 0.0)
    coef_ref[x, 5] = scale * lower
    coef_ref[x, 6] = right * share
    coef_ref[x, 7] = diag * (1.0 / OMEGA)


def all_coefficients(coef_ref, near_ref, far_ref, statics, tx_s, low, high):
    right_ref, wet_ref, tx_ref, ty_ref, tz_ref, st_ref = statics
    top = right_ref.shape[0] + HALO
    tx_s[pl.ds(HALO, top - HALO)] = tx_ref[...]
    if near_ref is not None:
        tx_s[pl.ds(top, HALO)] = near_ref[pl.ds(H_TX, HALO)]
    if far_ref is not None:
        tx_s[pl.ds(0, HALO)] = far_ref[pl.ds(H_TX, HALO)]
    turn = jnp.where(is_even(), 0, 1)

    def plane(u, quarters, right, north, upper, storage):
        coefficients(
            coef_ref, u, quarters.astype(F32), right, tx_s[u + turn], tx_s[u - 1 + turn], north, upper, storage
        )

    def own(u):
        x = u - HALO
        plane(u, wet_ref[x], right_ref[x], ty_ref[x], tz_ref[x], st_ref[x])

    def outside(u, halo, k):
        right = halo[H_WET + THIN + k].astype(F32) + halo[H_WET + 2 * THIN + k].astype(F32)
        plane(u, halo[H_WET + k], right, halo[H_REST + k], halo[H_REST + THIN + k], halo[H_REST + 2 * THIN + k])

    for u in range(low, HALO):
        outside(u, far_ref, u - 1)
    planes_in_groups(max(low, HALO), min(high, top), 8, own)
    for u in range(top, high):
        outside(u, near_ref, u - top)


def window_of(pieces, window_s, me):
    window_s[...] = jnp.zeros_like(window_s)
    for device, piece in pieces:
        window_s[pl.ds(pl.multiple_of((LEAD + device) * PER, PER), PER)] = piece
    return window_s[pl.ds(pl.multiple_of(me * PER, PER), WIN)].T[:NBF]


def blocks_in_order(rows_s, coupling_ref, me):
    lane = lax.broadcasted_iota(jnp.int32, (WIN, WIN), 1) + (me - LEAD) * PER
    for start in range(0, rows_s.shape[0], WIN):
        rows = rows_s[pl.ds(start, WIN)]
        block = rows[:, KROWS + NBF : KROWS + NBF + 1].astype(jnp.int32)
        chosen = (block == lane).astype(F32).astype(BF16)
        stacked = jnp.concatenate(three_parts(rows[:, :KROWS].T), axis=0)
        found = jnp.dot(stacked, chosen, preferred_element_type=F32)
        found = found[:KROWS] + found[KROWS : 2 * KROWS] + found[2 * KROWS :]
        coupling_ref[...] = found if start == 0 else coupling_ref[...] + found


def corrected_values(coupling_ref, inverse_ref, residual):
    values = coarse_solve(
        lambda k, i: coupling_ref[pl.ds((k * NBF + i) * NBF, NBF)],
        lambda i: inverse_ref[pl.ds(i * NBF, NBF)],
        residual,
    )
    return spread_blocks(values)


def prolong(state, places, gains, basis_at, base_at=None):
    wide = [
        [
            jnp.broadcast_to(gains[i : i + 1, yb * 128 : (yb + 1) * 128], (BLK, 128))
            for i in range(NBF)
        ]
        for yb in range(NYB)
    ]

    def step(u):
        for yb in range(NYB):
            rows = slice(yb * BLK, (yb + 1) * BLK)
            total = basis_at(0, u, rows).astype(F32) * wide[yb][0]
            for i in range(1, NBF):
                total = total + basis_at(i, u, rows).astype(F32) * wide[yb][i]
            state[u, rows] = total if base_at is None else base_at(u)[rows] + total

    planes_in_groups(places[0], places[1], 4, step)


def gains_of(spread, side):
    width = NYB * 128
    below, own, above = (spread[:, s * width : (s + 1) * width] for s in range(3))
    if side == 0:
        return own
    return jnp.where(is_even(), below if side < 0 else above, above if side < 0 else below)


def pulled(coef_ref, state, x):
    here = state[x]
    ny, nz = here.shape
    total = coef_ref[x, 6] + coef_ref[x, 0] * state[x + 1] + coef_ref[x, 1] * state[x - 1]
    total = total + coef_ref[x, 2] * pltpu.roll(here, ny - 1, 0) + coef_ref[x, 3] * pltpu.roll(here, 1, 0)
    total = total + coef_ref[x, 4] * pltpu.roll(here, nz - 1, 1) + coef_ref[x, 5] * pltpu.roll(here, 1, 1)
    return here, total


def sweep(coef_ref, source, target, low, high):
    def step(u):
        here, total = pulled(coef_ref, source, u)
        target[u] = (1.0 - OMEGA) * here + total

    planes_in_groups(low, high, high - low, step)


def misfit(coef_ref, source, x):
    here, total = pulled(coef_ref, source, x)
    return (total - OMEGA * here) * coef_ref[x, 7]


def body_kernel(
    basis_hbm, half_ref, other_ref, inverse_ref, near_ref, *refs
):
    statics, refs = refs[:6], refs[8:]
    pressure_ref, coupling_ref, spread_ref, one_out, two_out, totals_ref, edge_basis, send_near_hbm = refs[:8]
    rows_s, window_s, basis_ref, coef_ref, one_s, two_s, tx_s, sems = refs[8:]
    planes = pressure_ref.shape[0]
    top = planes + HALO
    me = lax.axis_index("gx")
    load = started(((basis_hbm, basis_ref),), sems)[0]
    core = lax.rem(me, 2)
    chips = half_ref.shape[0]

    def unpack(chip, carry):
        for ref, device in ((half_ref, 2 * chip + core), (other_ref, 2 * chip + 1 - core)):
            at = device * PER
            for r in range(2):
                rows = pl.ds(pl.multiple_of(at + r * 8, 8), 8)
                for l in range(KROWS // 128):
                    piece = ref[chip, pl.ds((r * (KROWS // 128) + l) * 8, 8)]
                    rows_s[rows, pl.ds(l * 128, 128)] = piece
                piece = ref[chip, pl.ds(ROWS - 8, 8)]
                rows_s[rows, pl.ds(KROWS, 128)] = pltpu.roll(piece, 64, 1) if r else piece
        return carry

    lax.fori_loop(0, chips, unpack, 0)
    blocks_in_order(rows_s, coupling_ref, me)
    pieces = [(e, rows_s[pl.ds(e * PER, PER), pl.ds(KROWS, 128)]) for e in range(2 * chips)]
    spread = corrected_values(coupling_ref, inverse_ref, window_of(pieces, window_s, me))
    spread_ref[...] = spread
    near_thin = near_ref.at[pl.ds(0, H_ALL)]
    all_coefficients(coef_ref, near_thin, None, statics, tx_s, HALO + 1, top + THIN)
    load.wait()
    prolong(one_s, (HALO, top), gains_of(spread, 0), lambda i, u, rows: basis_ref[i, plane_at(u - HALO, planes), rows])
    prolong(
        one_s, (top, top + HALO), gains_of(spread, 1), lambda i, u, rows: near_ref[i * HALO + u - top, rows]
    )
    sweep(coef_ref, one_s, two_s, HALO + 1, top + HALO - 1)
    sweep(coef_ref, two_s, one_s, HALO + 2, top + HALO - 2)
    sweep(coef_ref, one_s, two_s, HALO + 3, top + HALO - 3)
    for k in range(HALO):
        for i in range(NBF):
            edge_basis[i, k] = basis_ref[i, plane_at(k, planes)]
    one_out[...] = one_s[pl.ds(HALO, HALO)]
    two_out[...] = two_s[pl.ds(HALO + 1, HALO)]
    stores = started(
        [(two_s.at[pl.ds(top - 1 - k, 1)], send_near_hbm.at[pl.ds(k, 1)]) for k in range(HALO)], sems, 1
    )
    done = planes - THIN
    pressure_ref[pl.ds(THIN, done)] = two_s[pl.ds(HALO + THIN, done)]

    def step(u):
        one_s[u] = misfit(coef_ref, two_s, u)

    planes_in_groups(HALO + THIN + 1, top, planes - THIN - 1, step)
    totals = restrict_totals(
        lambda i, u: basis_ref[i, plane_at(u - HALO, planes)], lambda u: one_s[u], HALO + THIN + 1, top
    )
    for k, total in enumerate(totals):
        totals_ref[k] = total
    for copy in stores:
        copy.wait()


def edge_kernel(
    count, spread_ref, one_in, two_in, totals_in, basis_ref, pressure_in, far_ref, *refs
):
    statics, refs = refs[:6], refs[6:]
    pressure_ref, send_far_hbm, packed_hbm = refs[:3]
    coef_ref, one_s, two_s, tx_s, tail_s, sems = refs[3:]
    me = lax.axis_index("gx")
    planes = pressure_ref.shape[0]
    pressure_ref[pl.ds(THIN, planes - THIN)] = pressure_in[pl.ds(THIN, planes - THIN)]
    one_s[pl.ds(HALO, HALO)] = one_in[...]
    two_s[pl.ds(HALO + 1, HALO)] = two_in[...]
    all_coefficients(coef_ref, None, far_ref, statics, tx_s, 1, 2 * HALO)
    prolong(
        one_s, (0, HALO), gains_of(spread_ref[...], -1), lambda i, u, rows: far_ref[i * HALO + u, rows]
    )
    sweep(coef_ref, one_s, two_s, 1, HALO + 1)
    sweep(coef_ref, two_s, one_s, 2, HALO + 2)
    sweep(coef_ref, one_s, two_s, 3, HALO + 3)
    stores = started(
        [(two_s.at[pl.ds(2 * HALO - 1 - k, 1)], send_far_hbm.at[pl.ds(k, 1)]) for k in range(HALO)], sems
    )
    pressure_ref[pl.ds(0, THIN)] = two_s[pl.ds(HALO, THIN)]
    for u in range(HALO, 2 * HALO):
        one_s[u] = misfit(coef_ref, two_s, u)
    totals = restrict_totals(
        lambda i, u: basis_ref[i, u - HALO],
        lambda u: one_s[u],
        HALO,
        2 * HALO,
        [totals_in[k] for k in range(NBF * NYB)],
    )
    tail_s[...] = restricted_tile(totals, lane_of(me))
    stores += started(
        [(tail_s, packed_hbm.at[e]) for e in range(count)], sems, HALO
    )
    for copy in stores:
        copy.wait()


def last_kernel(
    basis_hbm, gathered_ref, inverse_ref, near_ref, far_ref, coupling_ref, pressure_ref, near_p_ref, far_p_ref,
    *refs
):
    statics, refs = refs[:6], refs[6:]
    pressure_out, residual_out, basis_ref, coef_ref, one_s, two_s, tx_s, pressure_s, residual_s, sems = refs
    planes = pressure_ref.shape[0]
    top = planes + HALO
    me = lax.axis_index("gx")
    load = started(((basis_hbm, basis_ref),), sems)[0]
    spread = corrected_values(coupling_ref, inverse_ref, window_of_tiles(gathered_ref, me))
    all_coefficients(coef_ref, near_ref, far_ref, statics, tx_s, 1, top + THIN)
    prolong(
        one_s, (0, HALO), gains_of(spread, -1), lambda i, u, rows: far_ref[i * HALO + u, rows],
        lambda u: far_p_ref[u],
    )
    prolong(
        one_s, (top, top + HALO), gains_of(spread, 1), lambda i, u, rows: near_ref[i * HALO + u - top, rows],
        lambda u: near_p_ref[u - top],
    )
    load.wait()
    prolong(
        one_s, (HALO, top), gains_of(spread, 0), lambda i, u, rows: basis_ref[i, plane_at(u - HALO, planes), rows],
        lambda u: pressure_ref[u - HALO],
    )
    sweep(coef_ref, one_s, two_s, 1, top + HALO - 1)
    sweep(coef_ref, two_s, one_s, 2, top + HALO - 2)
    sweep(coef_ref, one_s, two_s, 3, top + HALO - 3)
    for place in range(planes):
        pressure_s[plane_at(place, planes)] = two_s[place + HALO]
    stores = started(((pressure_s, pressure_out),), sems, 1)

    def step(u):
        residual_s[plane_at(u - HALO, planes)] = misfit(coef_ref, two_s, u)

    planes_in_groups(HALO, top, planes, step)
    stores += started(((residual_s, residual_out),), sems, 2)
    for copy in stores:
        copy.wait()


VMEM = pl.BlockSpec(memory_space=pltpu.VMEM)
ANY = pl.BlockSpec(memory_space=pl.ANY)


def kernel_call(name, body, arguments, outputs, scratch, aliases=None):
    spec = {pltpu.HBM: ANY, pltpu.VMEM: VMEM}
    call = pl.pallas_call(
        body,
        out_shape=[space(shape, dtype) for space, shape, dtype in outputs],
        in_specs=[spec[space] for space, _ in arguments],
        out_specs=[spec[space] for space, _, _ in outputs],
        scratch_shapes=scratch,
        input_output_aliases=aliases or {},
        compiler_params=pltpu.CompilerParams(vmem_limit_bytes=16 * 1024 * 1024),
        name=name,
    )
    return call(*[pltpu.with_memory_space_constraint(value, space) for space, value in arguments])


def local(
    right_side, wet_quarters, trans_x, trans_y, trans_z, storage, basis, coupling, coarse_inverse,
    owned_block, block_slot, neighbours,
):
    count = lax.axis_size("gx")
    planes, ny, nz = right_side.shape
    field = (ny, nz)
    full = planes + 2 * HALO
    near_pairs = [(i, i ^ 1) for i in range(count)]
    far_pairs = [(i, i + 1) for i in range(1, count - 1, 2)]
    far_pairs = far_pairs + [(b, a) for a, b in far_pairs]
    H, V = pltpu.HBM, pltpu.VMEM
    statics = [(H, a) for a in (right_side, wet_quarters, trans_x, trans_y, trans_z, storage)]
    halo = (H_ALL,) + field
    factors = pltpu.VMEM((full, 8) + field, F32)
    state = pltpu.VMEM((full,) + field, F32)
    own = pltpu.VMEM((planes,) + field, F32)
    window = pltpu.VMEM((count * PER + WIN, 128), F32)
    around = pltpu.VMEM((full,) + field, BF16)
    whole_basis = pltpu.VMEM(basis.shape, BF16)

    blocks = coarse_inverse.shape[2]
    near, far, packed, *fields, inverse, room, more_room = kernel_call(
        "restrict_first",
        first_kernel,
        [
            (H, owned_block), (H, basis), *statics, (H, coupling.reshape(KROWS, PER)),
            (H, coarse_inverse.reshape(NBF * NBF, blocks)),
        ],
        [(H, halo, BF16), (H, halo, BF16), (H, (count // 2, ROWS, 128), F32), (V, right_side.shape, F32)]
        + [(V, right_side.shape, BF16)] * 5
        + [(V, (NBF * NBF, WIN), F32), (V, right_side.shape, F32), (V, (KROWS, WIN), F32)],
        [
            pltpu.SMEM(owned_block.shape, jnp.int32),
            whole_basis,
            *[pltpu.VMEM(a.shape, a.dtype) for _, a in statics],
            pltpu.VMEM((KROWS, PER), F32),
            pltpu.VMEM((NBF * NBF, blocks), F32),
            pltpu.VMEM((ROWS, 128), F32),
            pltpu.VMEM((2,) + halo, BF16),
            pltpu.SemaphoreType.DMA((16 + count // 2,)),
        ],
    )
    far = lax.ppermute(far, "gx", far_pairs)
    chips = [[core + 2 * chip for chip in range(count // 2)] for core in range(2)]
    half = lax.all_to_all(packed, "gx", 0, 0, axis_index_groups=chips, tiled=True)
    near = lax.ppermute(near, "gx", near_pairs)
    other = lax.ppermute(half, "gx", near_pairs)

    pressure, coupled, spread, one, two, totals, edge_basis, send_near = kernel_call(
        "iteration_first",
        body_kernel,
        [(H, basis)] + [(V, a) for a in (half, other, inverse, near, *fields, room, more_room)],
        [
            (V, (planes,) + field, F32),
            (V, (KROWS, WIN), F32),
            (V, (NBF, 3 * NYB * nz), F32),
            (V, (HALO,) + field, F32),
            (V, (HALO,) + field, F32),
            (V, (NBF * NYB, 8, nz), F32),
            (V, (NBF, HALO) + field, BF16),
            (H, (HALO,) + field, F32),
        ],
        [
            pltpu.VMEM((count * PER, KROWS + 128), F32),
            window, whole_basis, factors, state, state, around, pltpu.SemaphoreType.DMA((1 + HALO,)),
        ],
        {11: 0, 12: 1},
    )
    near_p = lax.ppermute(send_near, "gx", near_pairs)
    far, near_p = lax.optimization_barrier((far, near_p))
    pressure, send_far, packed = kernel_call(
        "edge_first",
        functools.partial(edge_kernel, count),
        [(V, a) for a in (spread, one, two, totals, edge_basis, pressure, far, *fields)],
        [
            (V, (planes,) + field, F32),
            (H, (HALO,) + field, F32),
            (H, (count, NBF, 128), F32),
        ],
        [
            factors, state, state, around,
            pltpu.VMEM((NBF, 128), F32), pltpu.SemaphoreType.DMA((HALO + count,)),
        ],
        {5: 0},
    )

    far_p = lax.ppermute(send_far, "gx", far_pairs)
    gathered = lax.all_to_all(packed, "gx", 0, 0, tiled=True)
    whole = (H, (planes,) + field, F32)
    return kernel_call(
        "iteration_last",
        last_kernel,
        [(H, basis)]
        + [(V, a) for a in (gathered, inverse, near, far, coupled, pressure, near_p, far_p, *fields)],
        [whole, whole],
        [
            whole_basis, factors, state, state, around, own, own,
            pltpu.SemaphoreType.DMA((3,)),
        ],
    )


def solution(mesh):
    slabs = P(("parts", "gx"), None, None)
    placed = (
        slabs, slabs, slabs, slabs, slabs, slabs,
        P(None, ("parts", "gx"), None, None),
        P(None, None, None, ("parts", "gx")),
        P(None, None, "parts"),
        P(),
        P("gx"),
        P(None, "gx"),
    )
    return jax.shard_map(local, mesh=mesh, in_specs=placed, out_specs=(slabs, slabs), check_vma=False)
```

```python
import functools

import jax
import jax.numpy as jnp
from jax import lax
from jax.experimental import pallas as pl
from jax.experimental.pallas import tpu as pltpu
from jax.sharding import PartitionSpec as P

BLK = 16
NBF = 8
NNB = 6
SWEEPS = 3
CSWEEPS = 4
NYB = 2
NZB = 8
PER = NYB * NZB
WIN = 16 * PER
LEAD = 4
HALO = 4
OMEGA = 2.0 / 3.0
KROWS = NNB * NBF * NBF
ROWS = (KROWS // 128 * 2 + 1) * 8
F32 = jnp.float32
BF16 = jnp.bfloat16


THIN = HALO - 1
H_TX = NBF * HALO
H_REST = H_TX + HALO
H_WET = H_REST + 3 * THIN
H_ALL = H_REST + 6 * THIN


def planes_in_groups(low, high, group, step):
    count = (high - low) // group

    def body(k, carry):
        for j in range(group):
            step(low + k * group + j)
        return carry

    if count > 1:
        lax.fori_loop(0, count, body, 0)
    elif count:
        body(0, 0)
    for x in range(low + count * group, high):
        step(x)


def three_parts(x):
    high = x.astype(BF16)
    rest = x - high.astype(F32)
    middle = rest.astype(BF16)
    low = (rest - middle.astype(F32)).astype(BF16)
    return high, middle, low


def restrict_totals(basis_at, field_at, low, high, totals=None):
    def step(x, totals):
        field = field_at(x)
        out = []
        for i in range(NBF):
            for yb in range(NYB):
                rows = slice(yb * BLK, (yb + 1) * BLK)
                product = basis_at(i, x)[rows].astype(F32) * field[rows]
                out.append(totals[i * NYB + yb] + product[:8] + product[8:])
        return tuple(out)

    if totals is None:
        totals = (jnp.zeros((8, 128), F32),) * (NBF * NYB)
    return lax.fori_loop(low, high, step, tuple(totals))


def restricted(totals):
    groups = lax.broadcasted_iota(jnp.int32, (NZB, 3 * 128), 1)
    owner = lax.broadcasted_iota(jnp.int32, (NZB, 3 * 128), 0)
    spread = ((groups % 128) // BLK == owner).astype(F32).astype(BF16)
    halves = []
    for yb in range(NYB):
        rows = [jnp.sum(totals[i * NYB + yb], axis=0, keepdims=True) for i in range(NBF)]
        stacked = jnp.concatenate(three_parts(jnp.concatenate(rows, 0)), axis=1)
        halves.append(
            lax.dot_general(
                spread, stacked, (((1,), (1,)), ((), ())), preferred_element_type=F32
            )
        )
    return halves


def restricted_tile(totals, first):
    block = lax.broadcasted_iota(jnp.int32, (128, 128), 0) // BLK + first
    lane = lax.broadcasted_iota(jnp.int32, (128, 128), 1)
    tile = 0.0
    for yb in range(NYB):
        rows = [jnp.sum(totals[i * NYB + yb], axis=0, keepdims=True) for i in range(NBF)]
        stacked = jnp.concatenate(three_parts(jnp.concatenate(rows, 0)), axis=0)
        chosen = (lane == block + yb * NZB).astype(F32).astype(BF16)
        tile = tile + jnp.dot(stacked, chosen, preferred_element_type=F32)
    return tile[:NBF] + tile[NBF : 2 * NBF] + tile[2 * NBF :]


def lane_of(device):
    return lax.rem(device, 128 // PER) * PER


def tile_order(count):
    order = list(range(count))
    order[0], order[3] = order[3], order[0]
    return order


def window_of_tiles(gathered_ref, me):
    per = 128 // PER
    halves = [0.0] * (WIN // 128)
    for rank, device in enumerate(tile_order(gathered_ref.shape[0])):
        place = device - me + LEAD
        for half in range(WIN // 128):
            inside = (place >= half * per) & (place < (half + 1) * per)
            halves[half] = halves[half] + jnp.where(inside, gathered_ref[rank], 0.0)
    turn = lax.rem(128 - lane_of(me + per - LEAD), 128)
    return jnp.concatenate([pltpu.roll(half, turn, 1) for half in halves], axis=1)


def started(pairs, sems, first=0):
    copies = [pltpu.make_async_copy(a, b, sems.at[first + k]) for k, (a, b) in enumerate(pairs)]
    for copy in copies:
        copy.start()
    return copies


def is_even():
    return lax.rem(lax.axis_index("gx"), 2) == 0


def plane_at(place, planes):
    return jnp.where(is_even(), place, planes - 1 - place)


def first_kernel(
    owned_hbm, basis_hbm, right_hbm, wet_hbm, tx_hbm, ty_hbm, tz_hbm, st_hbm, coupling_hbm, all_inverse_hbm,
    near_hbm, far_hbm, packed_hbm, *rest
):
    field_refs, inverse_ref, rest = rest[:6], rest[6], rest[9:]
    (
        owned_s, basis_s, right_s, wet_s, tx_s, ty_s, tz_s, st_s, coupling_s, all_inverse, rows_s, halo_s, sems
    ) = rest
    me = lax.axis_index("gx")
    planes = right_s.shape[0]
    wides = [[plane_at(HALO - 1 - k, planes) for k in range(HALO)], [plane_at(planes - 1 - k, planes) for k in range(HALO)]]
    thins = [wides[0][1:], wides[1][:THIN]]
    quarter = planes // 4
    spans = [pl.ds(k * quarter, quarter) for k in (0, 3, 1, 2)]
    pairs = [(right_hbm, right_s)] + [(basis_hbm.at[:, span], basis_s.at[:, span]) for span in spans[:2]]
    pairs += list(zip((wet_hbm, tx_hbm, ty_hbm, tz_hbm, st_hbm), (wet_s, tx_s, ty_s, tz_s, st_s)))
    edge = len(pairs)
    pairs += [(basis_hbm.at[:, span], basis_s.at[:, span]) for span in spans[2:]]
    pairs += [(owned_hbm, owned_s), (coupling_hbm, coupling_s), (all_inverse_hbm, all_inverse)]
    loads = started(pairs, sems)

    def basis_at(i, x):
        return basis_s[i, x]

    def right_at(x):
        return right_s[x]

    loads[0].wait()
    totals = None
    for k in (0, 3):
        loads[1 + k // 3].wait()
        totals = restrict_totals(basis_at, right_at, k * quarter, (k + 1) * quarter, totals)
    for copy in loads[3:edge]:
        copy.wait()
    stores = []
    for side in range(2):
        for k in range(HALO):
            for i in range(NBF):
                halo_s[side, i * HALO + k] = basis_s[i, wides[side][k]]
            halo_s[side, H_TX + k] = tx_s[wides[side][k]]
        for k, x in enumerate(thins[side]):
            for j, field in enumerate((ty_s, tz_s, st_s)):
                halo_s[side, H_REST + j * THIN + k] = field[x]
            right = right_s[x]
            high = right.astype(BF16)
            halo_s[side, H_WET + k] = wet_s[x].astype(F32).astype(BF16)
            halo_s[side, H_WET + THIN + k] = high
            halo_s[side, H_WET + 2 * THIN + k] = (right - high.astype(F32)).astype(BF16)
        stores += started(
            ((halo_s.at[side], (far_hbm, near_hbm)[side]),), sems, len(loads) + side
        )
    for k in (1, 2):
        loads[edge + k - 1].wait()
        totals = restrict_totals(basis_at, right_at, k * quarter, (k + 1) * quarter, totals)
    for copy in loads[edge + 2 :]:
        copy.wait()
    slot = lax.broadcasted_iota(jnp.int32, (8, 1), 0)
    parts = []
    for half, coarse in enumerate(restricted(totals)):
        block = jnp.zeros((8, 1), jnp.int32)
        for s in range(8):
            block = jnp.where(slot == s, owned_s[me * PER + half * 8 + s], block)
        parts += [coarse, block.astype(F32), jnp.zeros((8, 64 - NBF - 1), F32)]
    wide = jnp.concatenate([coupling_s[...], jnp.zeros((KROWS, 128 - PER), F32)], axis=1).T
    for r in range(2):
        for l in range(KROWS // 128):
            rows_s[pl.ds((r * (KROWS // 128) + l) * 8, 8)] = wide[r * 8 : r * 8 + 8, l * 128 : l * 128 + 128]
    rows_s[pl.ds(ROWS - 8, 8)] = jnp.concatenate(parts, axis=1)
    stores += started(
        [(rows_s, packed_hbm.at[chip]) for chip in range(packed_hbm.shape[0])], sems, len(loads) + 2
    )

    def place_fields(place):
        x = plane_at(place, planes)
        for source, target in zip((right_s, wet_s, tx_s, ty_s, tz_s, st_s), field_refs):
            plane = source[x]
            target[place] = plane.astype(F32).astype(BF16) if source is wet_s else plane

    planes_in_groups(0, planes, 4, place_fields)
    blocks = all_inverse.shape[1]
    start = (me - LEAD) * PER
    turned = pltpu.roll(all_inverse[...], lax.rem(blocks - start, blocks), 1)[:, :WIN]
    block = lax.broadcasted_iota(jnp.int32, turned.shape, 1) + start
    inverse_ref[...] = jnp.where((block >= 0) & (block < blocks), turned, 0.0)
    for copy in stores:
        copy.wait()


def coarse_solve(coupling_at, inverse_at, residual):
    lane = lax.broadcasted_iota(jnp.int32, (NBF, WIN), 1)
    in_z, in_y = lane % NZB, (lane // NZB) % NYB

    def rows_of(parts):
        return jnp.concatenate([jnp.sum(p, axis=0, keepdims=True) for p in parts], 0)

    def inverted(v):
        return rows_of([inverse_at(i) * v for i in range(NBF)])

    values = inverted(residual)
    for _ in range(CSWEEPS - 1):
        near = (
            pltpu.roll(values, WIN - PER, 1),
            pltpu.roll(values, PER, 1),
            jnp.where(in_y < NYB - 1, pltpu.roll(values, WIN - NZB, 1), 0.0),
            jnp.where(in_y > 0, pltpu.roll(values, NZB, 1), 0.0),
            jnp.where(in_z < NZB - 1, pltpu.roll(values, WIN - 1, 1), 0.0),
            jnp.where(in_z > 0, pltpu.roll(values, 1, 1), 0.0),
        )
        parts = []
        for i in range(NBF):
            total = coupling_at(0, i) * near[0]
            for k in range(1, NNB):
                total = total + coupling_at(k, i) * near[k]
            parts.append(total)
        values = inverted(residual - rows_of(parts))
    return values


def spread_blocks(values):
    width = 3 * NYB * 128
    block = lax.broadcasted_iota(jnp.int32, (128, width), 0)
    column = lax.broadcasted_iota(jnp.int32, (128, width), 1)
    wanted = (LEAD - 1) * PER + column // BLK
    chosen = (block == wanted).astype(F32).astype(BF16)
    stacked = jnp.concatenate(three_parts(values[:, :128]), axis=0)
    spread = jnp.dot(stacked, chosen, preferred_element_type=F32)
    return spread[:NBF] + spread[NBF : 2 * NBF] + spread[2 * NBF :]


def coefficients(coef_ref, x, quarters, right, east, west, north, upper, storage):
    in_y = lax.broadcasted_iota(jnp.int32, north.shape, 0)
    in_z = lax.broadcasted_iota(jnp.int32, north.shape, 1)
    last_y, last_z = north.shape[0] - 1, north.shape[1] - 1
    east, west, north, upper = (a.astype(F32) for a in (east, west, north, upper))
    wet = quarters * 0.25
    dry = 1.0 - jnp.minimum(quarters, 1.0)
    south = jnp.where(in_y > 0, pltpu.roll(north, 1, 0), 0.0)
    lower = jnp.where(in_z > 0, pltpu.roll(upper, 1, 1), 0.0)
    diag = wet * (storage.astype(F32) + east + west + north + south + upper + lower) + dry
    share = OMEGA / diag
    scale = wet * share
    coef_ref[x, 0] = scale * east
    coef_ref[x, 1] = scale * west
    coef_ref[x, 2] = jnp.where(in_y < last_y, scale * north, 0.0)
    coef_ref[x, 3] = scale * south
    coef_ref[x, 4] = jnp.where(in_z < last_z, scale * upper, 0.0)
    coef_ref[x, 5] = scale * lower
    coef_ref[x, 6] = right * share
    coef_ref[x, 7] = diag * (1.0 / OMEGA)


def all_coefficients(coef_ref, near_ref, far_ref, statics, tx_s, low, high):
    right_ref, wet_ref, tx_ref, ty_ref, tz_ref, st_ref = statics
    top = right_ref.shape[0] + HALO
    tx_s[pl.ds(HALO, top - HALO)] = tx_ref[...]
    if near_ref is not None:
        tx_s[pl.ds(top, HALO)] = near_ref[pl.ds(H_TX, HALO)]
    if far_ref is not None:
        tx_s[pl.ds(0, HALO)] = far_ref[pl.ds(H_TX, HALO)]
    turn = jnp.where(is_even(), 0, 1)

    def plane(u, quarters, right, north, upper, storage):
        coefficients(
            coef_ref, u, quarters.astype(F32), right, tx_s[u + turn], tx_s[u - 1 + turn], north, upper, storage
        )

    def own(u):
        x = u - HALO
        plane(u, wet_ref[x], right_ref[x], ty_ref[x], tz_ref[x], st_ref[x])

    def outside(u, halo, k):
        right = halo[H_WET + THIN + k].astype(F32) + halo[H_WET + 2 * THIN + k].astype(F32)
        plane(u, halo[H_WET + k], right, halo[H_REST + k], halo[H_REST + THIN + k], halo[H_REST + 2 * THIN + k])

    for u in range(low, HALO):
        outside(u, far_ref, u - 1)
    planes_in_groups(max(low, HALO), min(high, top), 8, own)
    for u in range(top, high):
        outside(u, near_ref, u - top)


def window_of(pieces, window_s, me):
    window_s[...] = jnp.zeros_like(window_s)
    for device, piece in pieces:
        window_s[pl.ds(pl.multiple_of((LEAD + device) * PER, PER), PER)] = piece
    return window_s[pl.ds(pl.multiple_of(me * PER, PER), WIN)].T[:NBF]


def blocks_in_order(rows_s, coupling_ref, me):
    lane = lax.broadcasted_iota(jnp.int32, (WIN, WIN), 1) + (me - LEAD) * PER
    for start in range(0, rows_s.shape[0], WIN):
        rows = rows_s[pl.ds(start, WIN)]
        block = rows[:, KROWS + NBF : KROWS + NBF + 1].astype(jnp.int32)
        chosen = (block == lane).astype(F32).astype(BF16)
        stacked = jnp.concatenate(three_parts(rows[:, :KROWS].T), axis=0)
        found = jnp.dot(stacked, chosen, preferred_element_type=F32)
        found = found[:KROWS] + found[KROWS : 2 * KROWS] + found[2 * KROWS :]
        coupling_ref[...] = found if start == 0 else coupling_ref[...] + found


def corrected_values(coupling_ref, inverse_ref, residual):
    values = coarse_solve(
        lambda k, i: coupling_ref[pl.ds((k * NBF + i) * NBF, NBF)],
        lambda i: inverse_ref[pl.ds(i * NBF, NBF)],
        residual,
    )
    return spread_blocks(values)


def prolong(state, places, gains, basis_at, base_at=None):
    wide = [
        [
            jnp.broadcast_to(gains[i : i + 1, yb * 128 : (yb + 1) * 128], (BLK, 128))
            for i in range(NBF)
        ]
        for yb in range(NYB)
    ]

    def step(u):
        for yb in range(NYB):
            rows = slice(yb * BLK, (yb + 1) * BLK)
            total = basis_at(0, u, rows).astype(F32) * wide[yb][0]
            for i in range(1, NBF):
                total = total + basis_at(i, u, rows).astype(F32) * wide[yb][i]
            state[u, rows] = total if base_at is None else base_at(u)[rows] + total

    planes_in_groups(places[0], places[1], 4, step)


def gains_of(spread, side):
    width = NYB * 128
    below, own, above = (spread[:, s * width : (s + 1) * width] for s in range(3))
    if side == 0:
        return own
    return jnp.where(is_even(), below if side < 0 else above, above if side < 0 else below)


def pulled(coef_ref, state, x):
    here = state[x]
    ny, nz = here.shape
    total = coef_ref[x, 6] + coef_ref[x, 0] * state[x + 1] + coef_ref[x, 1] * state[x - 1]
    total = total + coef_ref[x, 2] * pltpu.roll(here, ny - 1, 0) + coef_ref[x, 3] * pltpu.roll(here, 1, 0)
    total = total + coef_ref[x, 4] * pltpu.roll(here, nz - 1, 1) + coef_ref[x, 5] * pltpu.roll(here, 1, 1)
    return here, total


def sweep(coef_ref, source, target, low, high):
    def step(u):
        here, total = pulled(coef_ref, source, u)
        target[u] = (1.0 - OMEGA) * here + total

    planes_in_groups(low, high, high - low, step)


def misfit(coef_ref, source, x):
    here, total = pulled(coef_ref, source, x)
    return (total - OMEGA * here) * coef_ref[x, 7]


def body_kernel(
    basis_hbm, half_ref, other_ref, inverse_ref, near_ref, *refs
):
    statics, refs = refs[:6], refs[8:]
    pressure_ref, coupling_ref, spread_ref, one_out, two_out, totals_ref, edge_basis, send_near_hbm = refs[:8]
    rows_s, window_s, basis_ref, coef_ref, one_s, two_s, tx_s, sems = refs[8:]
    planes = pressure_ref.shape[0]
    top = planes + HALO
    me = lax.axis_index("gx")
    load = started(((basis_hbm, basis_ref),), sems)[0]
    core = lax.rem(me, 2)
    chips = half_ref.shape[0]

    def unpack(chip, carry):
        for ref, device in ((half_ref, 2 * chip + core), (other_ref, 2 * chip + 1 - core)):
            at = device * PER
            for r in range(2):
                rows = pl.ds(pl.multiple_of(at + r * 8, 8), 8)
                for l in range(KROWS // 128):
                    piece = ref[chip, pl.ds((r * (KROWS // 128) + l) * 8, 8)]
                    rows_s[rows, pl.ds(l * 128, 128)] = piece
                piece = ref[chip, pl.ds(ROWS - 8, 8)]
                rows_s[rows, pl.ds(KROWS, 128)] = pltpu.roll(piece, 64, 1) if r else piece
        return carry

    lax.fori_loop(0, chips, unpack, 0)
    blocks_in_order(rows_s, coupling_ref, me)
    pieces = [(e, rows_s[pl.ds(e * PER, PER), pl.ds(KROWS, 128)]) for e in range(2 * chips)]
    spread = corrected_values(coupling_ref, inverse_ref, window_of(pieces, window_s, me))
    spread_ref[...] = spread
    near_thin = near_ref.at[pl.ds(0, H_ALL)]
    all_coefficients(coef_ref, near_thin, None, statics, tx_s, HALO + 1, top + THIN)
    load.wait()
    prolong(one_s, (HALO, top), gains_of(spread, 0), lambda i, u, rows: basis_ref[i, plane_at(u - HALO, planes), rows])
    prolong(
        one_s, (top, top + HALO), gains_of(spread, 1), lambda i, u, rows: near_ref[i * HALO + u - top, rows]
    )
    sweep(coef_ref, one_s, two_s, HALO + 1, top + HALO - 1)
    sweep(coef_ref, two_s, one_s, HALO + 2, top + HALO - 2)
    sweep(coef_ref, one_s, two_s, HALO + 3, top + HALO - 3)
    for k in range(HALO):
        for i in range(NBF):
            edge_basis[i, k] = basis_ref[i, plane_at(k, planes)]
    one_out[...] = one_s[pl.ds(HALO, HALO)]
    two_out[...] = two_s[pl.ds(HALO + 1, HALO)]
    stores = started(
        [(two_s.at[pl.ds(top - 1 - k, 1)], send_near_hbm.at[pl.ds(k, 1)]) for k in range(HALO)], sems, 1
    )
    done = planes - THIN
    pressure_ref[pl.ds(THIN, done)] = two_s[pl.ds(HALO + THIN, done)]

    def step(u):
        one_s[u] = misfit(coef_ref, two_s, u)

    planes_in_groups(HALO + THIN + 1, top, planes - THIN - 1, step)
    totals = restrict_totals(
        lambda i, u: basis_ref[i, plane_at(u - HALO, planes)], lambda u: one_s[u], HALO + THIN + 1, top
    )
    for k, total in enumerate(totals):
        totals_ref[k] = total
    for copy in stores:
        copy.wait()


def edge_kernel(
    count, spread_ref, one_in, two_in, totals_in, basis_ref, pressure_in, far_ref, *refs
):
    statics, refs = refs[:6], refs[6:]
    pressure_ref, send_far_hbm, packed_hbm = refs[:3]
    coef_ref, one_s, two_s, tx_s, tail_s, sems = refs[3:]
    me = lax.axis_index("gx")
    planes = pressure_ref.shape[0]
    pressure_ref[pl.ds(THIN, planes - THIN)] = pressure_in[pl.ds(THIN, planes - THIN)]
    one_s[pl.ds(HALO, HALO)] = one_in[...]
    two_s[pl.ds(HALO + 1, HALO)] = two_in[...]
    all_coefficients(coef_ref, None, far_ref, statics, tx_s, 1, 2 * HALO)
    prolong(
        one_s, (0, HALO), gains_of(spread_ref[...], -1), lambda i, u, rows: far_ref[i * HALO + u, rows]
    )
    sweep(coef_ref, one_s, two_s, 1, HALO + 1)
    sweep(coef_ref, two_s, one_s, 2, HALO + 2)
    sweep(coef_ref, one_s, two_s, 3, HALO + 3)
    stores = started(
        [(two_s.at[pl.ds(2 * HALO - 1 - k, 1)], send_far_hbm.at[pl.ds(k, 1)]) for k in range(HALO)], sems
    )
    pressure_ref[pl.ds(0, THIN)] = two_s[pl.ds(HALO, THIN)]
    for u in range(HALO, 2 * HALO):
        one_s[u] = misfit(coef_ref, two_s, u)
    totals = restrict_totals(
        lambda i, u: basis_ref[i, u - HALO],
        lambda u: one_s[u],
        HALO,
        2 * HALO,
        [totals_in[k] for k in range(NBF * NYB)],
    )
    tail_s[...] = restricted_tile(totals, lane_of(me))
    stores += started(
        [(tail_s, packed_hbm.at[e]) for e in range(count)], sems, HALO
    )
    for copy in stores:
        copy.wait()


def last_kernel(
    basis_hbm, gathered_ref, inverse_ref, near_ref, far_ref, coupling_ref, pressure_ref, near_p_ref, far_p_ref,
    *refs
):
    statics, refs = refs[:6], refs[6:]
    pressure_out, residual_out, basis_ref, coef_ref, one_s, two_s, tx_s, pressure_s, residual_s, sems = refs
    planes = pressure_ref.shape[0]
    top = planes + HALO
    me = lax.axis_index("gx")
    load = started(((basis_hbm, basis_ref),), sems)[0]
    spread = corrected_values(coupling_ref, inverse_ref, window_of_tiles(gathered_ref, me))
    all_coefficients(coef_ref, near_ref, far_ref, statics, tx_s, 1, top + THIN)
    prolong(
        one_s, (0, HALO), gains_of(spread, -1), lambda i, u, rows: far_ref[i * HALO + u, rows],
        lambda u: far_p_ref[u],
    )
    prolong(
        one_s, (top, top + HALO), gains_of(spread, 1), lambda i, u, rows: near_ref[i * HALO + u - top, rows],
        lambda u: near_p_ref[u - top],
    )
    load.wait()
    prolong(
        one_s, (HALO, top), gains_of(spread, 0), lambda i, u, rows: basis_ref[i, plane_at(u - HALO, planes), rows],
        lambda u: pressure_ref[u - HALO],
    )
    sweep(coef_ref, one_s, two_s, 1, top + HALO - 1)
    sweep(coef_ref, two_s, one_s, 2, top + HALO - 2)
    sweep(coef_ref, one_s, two_s, 3, top + HALO - 3)
    for place in range(planes):
        pressure_s[plane_at(place, planes)] = two_s[place + HALO]
    stores = started(((pressure_s, pressure_out),), sems, 1)

    def step(u):
        residual_s[plane_at(u - HALO, planes)] = misfit(coef_ref, two_s, u)

    half = planes // 2
    for part in range(2):
        planes_in_groups(HALO + part * half, HALO + (part + 1) * half, half, step)
        span = pl.ds(plane_at(part * half, planes) - jnp.where(is_even(), 0, half - 1), half)
        stores += started(((residual_s.at[span], residual_out.at[span]),), sems, 2 + part)
    for copy in stores:
        copy.wait()


VMEM = pl.BlockSpec(memory_space=pltpu.VMEM)
ANY = pl.BlockSpec(memory_space=pl.ANY)


def kernel_call(name, body, arguments, outputs, scratch, aliases=None):
    spec = {pltpu.HBM: ANY, pltpu.VMEM: VMEM}
    call = pl.pallas_call(
        body,
        out_shape=[space(shape, dtype) for space, shape, dtype in outputs],
        in_specs=[spec[space] for space, _ in arguments],
        out_specs=[spec[space] for space, _, _ in outputs],
        scratch_shapes=scratch,
        input_output_aliases=aliases or {},
        compiler_params=pltpu.CompilerParams(vmem_limit_bytes=16 * 1024 * 1024),
        name=name,
    )
    return call(*[pltpu.with_memory_space_constraint(value, space) for space, value in arguments])


def local(
    right_side, wet_quarters, trans_x, trans_y, trans_z, storage, basis, coupling, coarse_inverse,
    owned_block, block_slot, neighbours,
):
    count = lax.axis_size("gx")
    planes, ny, nz = right_side.shape
    field = (ny, nz)
    full = planes + 2 * HALO
    near_pairs = [(i, i ^ 1) for i in range(count)]
    far_pairs = [(i, i + 1) for i in range(1, count - 1, 2)]
    far_pairs = far_pairs + [(b, a) for a, b in far_pairs]
    H, V = pltpu.HBM, pltpu.VMEM
    statics = [(H, a) for a in (right_side, wet_quarters, trans_x, trans_y, trans_z, storage)]
    halo = (H_ALL,) + field
    factors = pltpu.VMEM((full, 8) + field, F32)
    state = pltpu.VMEM((full,) + field, F32)
    own = pltpu.VMEM((planes,) + field, F32)
    window = pltpu.VMEM((count * PER + WIN, 128), F32)
    around = pltpu.VMEM((full,) + field, BF16)
    whole_basis = pltpu.VMEM(basis.shape, BF16)

    blocks = coarse_inverse.shape[2]
    near, far, packed, *fields, inverse, room, more_room = kernel_call(
        "restrict_first",
        first_kernel,
        [
            (H, owned_block), (H, basis), *statics, (H, coupling.reshape(KROWS, PER)),
            (H, coarse_inverse.reshape(NBF * NBF, blocks)),
        ],
        [(H, halo, BF16), (H, halo, BF16), (H, (count // 2, ROWS, 128), F32), (V, right_side.shape, F32)]
        + [(V, right_side.shape, BF16)] * 5
        + [(V, (NBF * NBF, WIN), F32), (V, right_side.shape, F32), (V, (KROWS, WIN), F32)],
        [
            pltpu.SMEM(owned_block.shape, jnp.int32),
            whole_basis,
            *[pltpu.VMEM(a.shape, a.dtype) for _, a in statics],
            pltpu.VMEM((KROWS, PER), F32),
            pltpu.VMEM((NBF * NBF, blocks), F32),
            pltpu.VMEM((ROWS, 128), F32),
            pltpu.VMEM((2,) + halo, BF16),
            pltpu.SemaphoreType.DMA((16 + count // 2,)),
        ],
    )
    far = lax.ppermute(far, "gx", far_pairs)
    chips = [[core + 2 * chip for chip in range(count // 2)] for core in range(2)]
    half = lax.all_to_all(packed, "gx", 0, 0, axis_index_groups=chips, tiled=True)
    near = lax.ppermute(near, "gx", near_pairs)
    other = lax.ppermute(half, "gx", near_pairs)

    pressure, coupled, spread, one, two, totals, edge_basis, send_near = kernel_call(
        "iteration_first",
        body_kernel,
        [(H, basis)] + [(V, a) for a in (half, other, inverse, near, *fields, room, more_room)],
        [
            (V, (planes,) + field, F32),
            (V, (KROWS, WIN), F32),
            (V, (NBF, 3 * NYB * nz), F32),
            (V, (HALO,) + field, F32),
            (V, (HALO,) + field, F32),
            (V, (NBF * NYB, 8, nz), F32),
            (V, (NBF, HALO) + field, BF16),
            (H, (HALO,) + field, F32),
        ],
        [
            pltpu.VMEM((count * PER, KROWS + 128), F32),
            window, whole_basis, factors, state, state, around, pltpu.SemaphoreType.DMA((1 + HALO,)),
        ],
        {11: 0, 12: 1},
    )
    near_p = lax.ppermute(send_near, "gx", near_pairs)
    far, near_p = lax.optimization_barrier((far, near_p))
    pressure, send_far, packed = kernel_call(
        "edge_first",
        functools.partial(edge_kernel, count),
        [(V, a) for a in (spread, one, two, totals, edge_basis, pressure, far, *fields)],
        [
            (V, (planes,) + field, F32),
            (H, (HALO,) + field, F32),
            (H, (count, NBF, 128), F32),
        ],
        [
            factors, state, state, around,
            pltpu.VMEM((NBF, 128), F32), pltpu.SemaphoreType.DMA((HALO + count,)),
        ],
        {5: 0},
    )

    far_p = lax.ppermute(send_far, "gx", far_pairs)
    gathered = lax.all_to_all(packed, "gx", 0, 0, axis_index_groups=[tile_order(count)], tiled=True)
    whole = (H, (planes,) + field, F32)
    return kernel_call(
        "iteration_last",
        last_kernel,
        [(H, basis)]
        + [(V, a) for a in (gathered, inverse, near, far, coupled, pressure, near_p, far_p, *fields)],
        [whole, whole],
        [
            whole_basis, factors, state, state, around, own, own,
            pltpu.SemaphoreType.DMA((4,)),
        ],
    )


def solution(mesh):
    slabs = P(("parts", "gx"), None, None)
    placed = (
        slabs, slabs, slabs, slabs, slabs, slabs,
        P(None, ("parts", "gx"), None, None),
        P(None, None, None, ("parts", "gx")),
        P(None, None, "parts"),
        P(),
        P("gx"),
        P(None, "gx"),
    )
    return jax.shard_map(local, mesh=mesh, in_specs=placed, out_specs=(slabs, slabs), check_vma=False)
```

```python
import functools

import jax
import jax.numpy as jnp
from jax import lax
from jax.experimental import pallas as pl
from jax.experimental.pallas import tpu as pltpu
from jax.sharding import PartitionSpec as P

BLK = 16
NBF = 8
NNB = 6
SWEEPS = 3
CSWEEPS = 4
NYB = 2
NZB = 8
PER = NYB * NZB
WIN = 16 * PER
LEAD = 4
HALO = 4
OMEGA = 2.0 / 3.0
KROWS = NNB * NBF * NBF
ROWS = (KROWS // 128 * 2 + 1) * 8
F32 = jnp.float32
BF16 = jnp.bfloat16


THIN = HALO - 1
H_TX = NBF * HALO
H_REST = H_TX + HALO
H_WET = H_REST + 3 * THIN
H_ALL = H_REST + 6 * THIN


def planes_in_groups(low, high, group, step):
    count = (high - low) // group

    def body(k, carry):
        for j in range(group):
            step(low + k * group + j)
        return carry

    if count > 1:
        lax.fori_loop(0, count, body, 0)
    elif count:
        body(0, 0)
    for x in range(low + count * group, high):
        step(x)


def three_parts(x):
    high = x.astype(BF16)
    rest = x - high.astype(F32)
    middle = rest.astype(BF16)
    low = (rest - middle.astype(F32)).astype(BF16)
    return high, middle, low


def restrict_totals(basis_at, field_at, low, high, totals=None):
    def step(x, totals):
        field = field_at(x)
        out = []
        for i in range(NBF):
            for yb in range(NYB):
                rows = slice(yb * BLK, (yb + 1) * BLK)
                product = basis_at(i, x)[rows].astype(F32) * field[rows]
                out.append(totals[i * NYB + yb] + product[:8] + product[8:])
        return tuple(out)

    if totals is None:
        totals = (jnp.zeros((8, 128), F32),) * (NBF * NYB)
    return lax.fori_loop(low, high, step, tuple(totals))


def restricted(totals):
    groups = lax.broadcasted_iota(jnp.int32, (NZB, 3 * 128), 1)
    owner = lax.broadcasted_iota(jnp.int32, (NZB, 3 * 128), 0)
    spread = ((groups % 128) // BLK == owner).astype(F32).astype(BF16)
    halves = []
    for yb in range(NYB):
        rows = [jnp.sum(totals[i * NYB + yb], axis=0, keepdims=True) for i in range(NBF)]
        stacked = jnp.concatenate(three_parts(jnp.concatenate(rows, 0)), axis=1)
        halves.append(
            lax.dot_general(
                spread, stacked, (((1,), (1,)), ((), ())), preferred_element_type=F32
            )
        )
    return halves


def restricted_tile(totals, first):
    block = lax.broadcasted_iota(jnp.int32, (128, 128), 0) // BLK + first
    lane = lax.broadcasted_iota(jnp.int32, (128, 128), 1)
    tile = 0.0
    for yb in range(NYB):
        rows = [jnp.sum(totals[i * NYB + yb], axis=0, keepdims=True) for i in range(NBF)]
        stacked = jnp.concatenate(three_parts(jnp.concatenate(rows, 0)), axis=0)
        chosen = (lane == block + yb * NZB).astype(F32).astype(BF16)
        tile = tile + jnp.dot(stacked, chosen, preferred_element_type=F32)
    return tile[:NBF] + tile[NBF : 2 * NBF] + tile[2 * NBF :]


def lane_of(device):
    return lax.rem(device, 128 // PER) * PER


def tile_order(count):
    order = list(range(count))
    order[:8] = order[4:8] + order[:4]
    return order


def window_of_tiles(gathered_ref, me):
    per = 128 // PER
    halves = [0.0] * (WIN // 128)
    for rank, device in enumerate(tile_order(gathered_ref.shape[0])):
        place = device - me + LEAD
        for half in range(WIN // 128):
            inside = (place >= half * per) & (place < (half + 1) * per)
            halves[half] = halves[half] + jnp.where(inside, gathered_ref[rank], 0.0)
    turn = lax.rem(128 - lane_of(me + per - LEAD), 128)
    return jnp.concatenate([pltpu.roll(half, turn, 1) for half in halves], axis=1)


def started(pairs, sems, first=0):
    copies = [pltpu.make_async_copy(a, b, sems.at[first + k]) for k, (a, b) in enumerate(pairs)]
    for copy in copies:
        copy.start()
    return copies


def is_even():
    return lax.rem(lax.axis_index("gx"), 2) == 0


def plane_at(place, planes):
    return jnp.where(is_even(), place, planes - 1 - place)


def first_kernel(
    owned_hbm, basis_hbm, right_hbm, wet_hbm, tx_hbm, ty_hbm, tz_hbm, st_hbm, coupling_hbm, all_inverse_hbm,
    near_hbm, far_hbm, packed_hbm, *rest
):
    field_refs, inverse_ref, rest = rest[:6], rest[6], rest[9:]
    (
        owned_s, basis_s, right_s, wet_s, tx_s, ty_s, tz_s, st_s, coupling_s, all_inverse, rows_s, halo_s, sems
    ) = rest
    me = lax.axis_index("gx")
    planes = right_s.shape[0]
    wides = [[plane_at(HALO - 1 - k, planes) for k in range(HALO)], [plane_at(planes - 1 - k, planes) for k in range(HALO)]]
    thins = [wides[0][1:], wides[1][:THIN]]
    quarter = planes // 4
    spans = [pl.ds(k * quarter, quarter) for k in (0, 3, 1, 2)]
    pairs = [(right_hbm, right_s)] + [(basis_hbm.at[:, span], basis_s.at[:, span]) for span in spans[:2]]
    pairs += list(zip((wet_hbm, tx_hbm, ty_hbm, tz_hbm, st_hbm), (wet_s, tx_s, ty_s, tz_s, st_s)))
    edge = len(pairs)
    pairs += [(basis_hbm.at[:, span], basis_s.at[:, span]) for span in spans[2:]]
    pairs += [(owned_hbm, owned_s), (coupling_hbm, coupling_s), (all_inverse_hbm, all_inverse)]
    loads = started(pairs, sems)

    def basis_at(i, x):
        return basis_s[i, x]

    def right_at(x):
        return right_s[x]

    loads[0].wait()
    totals = None
    for k in (0, 3):
        loads[1 + k // 3].wait()
        totals = restrict_totals(basis_at, right_at, k * quarter, (k + 1) * quarter, totals)
    for copy in loads[3:edge]:
        copy.wait()
    stores = []
    for side in range(2):
        for k in range(HALO):
            for i in range(NBF):
                halo_s[side, i * HALO + k] = basis_s[i, wides[side][k]]
            halo_s[side, H_TX + k] = tx_s[wides[side][k]]
        for k, x in enumerate(thins[side]):
            for j, field in enumerate((ty_s, tz_s, st_s)):
                halo_s[side, H_REST + j * THIN + k] = field[x]
            right = right_s[x]
            high = right.astype(BF16)
            halo_s[side, H_WET + k] = wet_s[x].astype(F32).astype(BF16)
            halo_s[side, H_WET + THIN + k] = high
            halo_s[side, H_WET + 2 * THIN + k] = (right - high.astype(F32)).astype(BF16)
        stores += started(
            ((halo_s.at[side], (far_hbm, near_hbm)[side]),), sems, len(loads) + side
        )
    for k in (1, 2):
        loads[edge + k - 1].wait()
        totals = restrict_totals(basis_at, right_at, k * quarter, (k + 1) * quarter, totals)
    for copy in loads[edge + 2 :]:
        copy.wait()
    slot = lax.broadcasted_iota(jnp.int32, (8, 1), 0)
    parts = []
    for half, coarse in enumerate(restricted(totals)):
        block = jnp.zeros((8, 1), jnp.int32)
        for s in range(8):
            block = jnp.where(slot == s, owned_s[me * PER + half * 8 + s], block)
        parts += [coarse, block.astype(F32), jnp.zeros((8, 64 - NBF - 1), F32)]
    wide = jnp.concatenate([coupling_s[...], jnp.zeros((KROWS, 128 - PER), F32)], axis=1).T
    for r in range(2):
        for l in range(KROWS // 128):
            rows_s[pl.ds((r * (KROWS // 128) + l) * 8, 8)] = wide[r * 8 : r * 8 + 8, l * 128 : l * 128 + 128]
    rows_s[pl.ds(ROWS - 8, 8)] = jnp.concatenate(parts, axis=1)
    stores += started(
        [(rows_s, packed_hbm.at[chip]) for chip in range(packed_hbm.shape[0])], sems, len(loads) + 2
    )

    def place_fields(place):
        x = plane_at(place, planes)
        for source, target in zip((right_s, wet_s, tx_s, ty_s, tz_s, st_s), field_refs):
            plane = source[x]
            target[place] = plane.astype(F32).astype(BF16) if source is wet_s else plane

    planes_in_groups(0, planes, 4, place_fields)
    blocks = all_inverse.shape[1]
    start = (me - LEAD) * PER
    turned = pltpu.roll(all_inverse[...], lax.rem(blocks - start, blocks), 1)[:, :WIN]
    block = lax.broadcasted_iota(jnp.int32, turned.shape, 1) + start
    inverse_ref[...] = jnp.where((block >= 0) & (block < blocks), turned, 0.0)
    for copy in stores:
        copy.wait()


def coarse_solve(coupling_at, inverse_at, residual):
    lane = lax.broadcasted_iota(jnp.int32, (NBF, WIN), 1)
    in_z, in_y = lane % NZB, (lane // NZB) % NYB

    def rows_of(parts):
        return jnp.concatenate([jnp.sum(p, axis=0, keepdims=True) for p in parts], 0)

    def inverted(v):
        return rows_of([inverse_at(i) * v for i in range(NBF)])

    values = inverted(residual)
    for _ in range(CSWEEPS - 1):
        near = (
            pltpu.roll(values, WIN - PER, 1),
            pltpu.roll(values, PER, 1),
            jnp.where(in_y < NYB - 1, pltpu.roll(values, WIN - NZB, 1), 0.0),
            jnp.where(in_y > 0, pltpu.roll(values, NZB, 1), 0.0),
            jnp.where(in_z < NZB - 1, pltpu.roll(values, WIN - 1, 1), 0.0),
            jnp.where(in_z > 0, pltpu.roll(values, 1, 1), 0.0),
        )
        parts = []
        for i in range(NBF):
            total = coupling_at(0, i) * near[0]
            for k in range(1, NNB):
                total = total + coupling_at(k, i) * near[k]
            parts.append(total)
        values = inverted(residual - rows_of(parts))
    return values


def spread_blocks(values):
    width = 3 * NYB * 128
    block = lax.broadcasted_iota(jnp.int32, (128, width), 0)
    column = lax.broadcasted_iota(jnp.int32, (128, width), 1)
    wanted = (LEAD - 1) * PER + column // BLK
    chosen = (block == wanted).astype(F32).astype(BF16)
    stacked = jnp.concatenate(three_parts(values[:, :128]), axis=0)
    spread = jnp.dot(stacked, chosen, preferred_element_type=F32)
    return spread[:NBF] + spread[NBF : 2 * NBF] + spread[2 * NBF :]


def coefficients(coef_ref, x, quarters, right, east, west, north, upper, storage):
    in_y = lax.broadcasted_iota(jnp.int32, north.shape, 0)
    in_z = lax.broadcasted_iota(jnp.int32, north.shape, 1)
    last_y, last_z = north.shape[0] - 1, north.shape[1] - 1
    east, west, north, upper = (a.astype(F32) for a in (east, west, north, upper))
    wet = quarters * 0.25
    dry = 1.0 - jnp.minimum(quarters, 1.0)
    south = jnp.where(in_y > 0, pltpu.roll(north, 1, 0), 0.0)
    lower = jnp.where(in_z > 0, pltpu.roll(upper, 1, 1), 0.0)
    diag = wet * (storage.astype(F32) + east + west + north + south + upper + lower) + dry
    share = OMEGA / diag
    scale = wet * share
    coef_ref[x, 0] = scale * east
    coef_ref[x, 1] = scale * west
    coef_ref[x, 2] = jnp.where(in_y < last_y, scale * north, 0.0)
    coef_ref[x, 3] = scale * south
    coef_ref[x, 4] = jnp.where(in_z < last_z, scale * upper, 0.0)
    coef_ref[x, 5] = scale * lower
    coef_ref[x, 6] = right * share
    coef_ref[x, 7] = diag * (1.0 / OMEGA)


def all_coefficients(coef_ref, near_ref, far_ref, statics, tx_s, low, high):
    right_ref, wet_ref, tx_ref, ty_ref, tz_ref, st_ref = statics
    top = right_ref.shape[0] + HALO
    tx_s[pl.ds(HALO, top - HALO)] = tx_ref[...]
    if near_ref is not None:
        tx_s[pl.ds(top, HALO)] = near_ref[pl.ds(H_TX, HALO)]
    if far_ref is not None:
        tx_s[pl.ds(0, HALO)] = far_ref[pl.ds(H_TX, HALO)]
    turn = jnp.where(is_even(), 0, 1)

    def plane(u, quarters, right, north, upper, storage):
        coefficients(
            coef_ref, u, quarters.astype(F32), right, tx_s[u + turn], tx_s[u - 1 + turn], north, upper, storage
        )

    def own(u):
        x = u - HALO
        plane(u, wet_ref[x], right_ref[x], ty_ref[x], tz_ref[x], st_ref[x])

    def outside(u, halo, k):
        right = halo[H_WET + THIN + k].astype(F32) + halo[H_WET + 2 * THIN + k].astype(F32)
        plane(u, halo[H_WET + k], right, halo[H_REST + k], halo[H_REST + THIN + k], halo[H_REST + 2 * THIN + k])

    for u in range(low, HALO):
        outside(u, far_ref, u - 1)
    planes_in_groups(max(low, HALO), min(high, top), 8, own)
    for u in range(top, high):
        outside(u, near_ref, u - top)


def window_of(pieces, window_s, me):
    window_s[...] = jnp.zeros_like(window_s)
    for device, piece in pieces:
        window_s[pl.ds(pl.multiple_of((LEAD + device) * PER, PER), PER)] = piece
    return window_s[pl.ds(pl.multiple_of(me * PER, PER), WIN)].T[:NBF]


def blocks_in_order(rows_s, coupling_ref, me):
    lane = lax.broadcasted_iota(jnp.int32, (WIN, WIN), 1) + (me - LEAD) * PER
    for start in range(0, rows_s.shape[0], WIN):
        rows = rows_s[pl.ds(start, WIN)]
        block = rows[:, KROWS + NBF : KROWS + NBF + 1].astype(jnp.int32)
        chosen = (block == lane).astype(F32).astype(BF16)
        stacked = jnp.concatenate(three_parts(rows[:, :KROWS].T), axis=0)
        found = jnp.dot(stacked, chosen, preferred_element_type=F32)
        found = found[:KROWS] + found[KROWS : 2 * KROWS] + found[2 * KROWS :]
        coupling_ref[...] = found if start == 0 else coupling_ref[...] + found


def corrected_values(coupling_ref, inverse_ref, residual):
    values = coarse_solve(
        lambda k, i: coupling_ref[pl.ds((k * NBF + i) * NBF, NBF)],
        lambda i: inverse_ref[pl.ds(i * NBF, NBF)],
        residual,
    )
    return spread_blocks(values)


def prolong(state, places, gains, basis_at, base_at=None):
    wide = [
        [
            jnp.broadcast_to(gains[i : i + 1, yb * 128 : (yb + 1) * 128], (BLK, 128))
            for i in range(NBF)
        ]
        for yb in range(NYB)
    ]

    def step(u):
        for yb in range(NYB):
            rows = slice(yb * BLK, (yb + 1) * BLK)
            total = basis_at(0, u, rows).astype(F32) * wide[yb][0]
            for i in range(1, NBF):
                total = total + basis_at(i, u, rows).astype(F32) * wide[yb][i]
            state[u, rows] = total if base_at is None else base_at(u)[rows] + total

    planes_in_groups(places[0], places[1], 4, step)


def gains_of(spread, side):
    width = NYB * 128
    below, own, above = (spread[:, s * width : (s + 1) * width] for s in range(3))
    if side == 0:
        return own
    return jnp.where(is_even(), below if side < 0 else above, above if side < 0 else below)


def pulled(coef_ref, state, x):
    here = state[x]
    ny, nz = here.shape
    total = coef_ref[x, 6] + coef_ref[x, 0] * state[x + 1] + coef_ref[x, 1] * state[x - 1]
    total = total + coef_ref[x, 2] * pltpu.roll(here, ny - 1, 0) + coef_ref[x, 3] * pltpu.roll(here, 1, 0)
    total = total + coef_ref[x, 4] * pltpu.roll(here, nz - 1, 1) + coef_ref[x, 5] * pltpu.roll(here, 1, 1)
    return here, total


def sweep(coef_ref, source, target, low, high):
    def step(u):
        here, total = pulled(coef_ref, source, u)
        target[u] = (1.0 - OMEGA) * here + total

    planes_in_groups(low, high, high - low, step)


def misfit(coef_ref, source, x):
    here, total = pulled(coef_ref, source, x)
    return (total - OMEGA * here) * coef_ref[x, 7]


def body_kernel(
    basis_hbm, half_ref, other_ref, inverse_ref, near_ref, *refs
):
    statics, refs = refs[:6], refs[8:]
    pressure_ref, coupling_ref, spread_ref, one_out, two_out, totals_ref, edge_basis, send_near_hbm = refs[:8]
    rows_s, window_s, basis_ref, coef_ref, one_s, two_s, tx_s, sems = refs[8:]
    planes = pressure_ref.shape[0]
    top = planes + HALO
    me = lax.axis_index("gx")
    load = started(((basis_hbm, basis_ref),), sems)[0]
    core = lax.rem(me, 2)
    chips = half_ref.shape[0]

    def unpack(chip, carry):
        first = 2 * jnp.where(chip < 4, jnp.bitwise_xor(chip, 2), chip)
        for ref, device in ((half_ref, first + core), (other_ref, first + 1 - core)):
            at = device * PER
            for r in range(2):
                rows = pl.ds(pl.multiple_of(at + r * 8, 8), 8)
                for l in range(KROWS // 128):
                    piece = ref[chip, pl.ds((r * (KROWS // 128) + l) * 8, 8)]
                    rows_s[rows, pl.ds(l * 128, 128)] = piece
                piece = ref[chip, pl.ds(ROWS - 8, 8)]
                rows_s[rows, pl.ds(KROWS, 128)] = pltpu.roll(piece, 64, 1) if r else piece
        return carry

    lax.fori_loop(0, chips, unpack, 0)
    blocks_in_order(rows_s, coupling_ref, me)
    pieces = [(e, rows_s[pl.ds(e * PER, PER), pl.ds(KROWS, 128)]) for e in range(2 * chips)]
    spread = corrected_values(coupling_ref, inverse_ref, window_of(pieces, window_s, me))
    spread_ref[...] = spread
    near_thin = near_ref.at[pl.ds(0, H_ALL)]
    all_coefficients(coef_ref, near_thin, None, statics, tx_s, HALO + 1, top + THIN)
    load.wait()
    prolong(one_s, (HALO, top), gains_of(spread, 0), lambda i, u, rows: basis_ref[i, plane_at(u - HALO, planes), rows])
    prolong(
        one_s, (top, top + HALO), gains_of(spread, 1), lambda i, u, rows: near_ref[i * HALO + u - top, rows]
    )
    sweep(coef_ref, one_s, two_s, HALO + 1, top + HALO - 1)
    sweep(coef_ref, two_s, one_s, HALO + 2, top + HALO - 2)
    sweep(coef_ref, one_s, two_s, HALO + 3, top + HALO - 3)
    for k in range(HALO):
        for i in range(NBF):
            edge_basis[i, k] = basis_ref[i, plane_at(k, planes)]
    one_out[...] = one_s[pl.ds(HALO, HALO)]
    two_out[...] = two_s[pl.ds(HALO + 1, HALO)]
    stores = started(
        [(two_s.at[pl.ds(top - 1 - k, 1)], send_near_hbm.at[pl.ds(k, 1)]) for k in range(HALO)], sems, 1
    )
    done = planes - THIN
    pressure_ref[pl.ds(THIN, done)] = two_s[pl.ds(HALO + THIN, done)]

    def step(u):
        one_s[u] = misfit(coef_ref, two_s, u)

    planes_in_groups(HALO + THIN + 1, top, planes - THIN - 1, step)
    totals = restrict_totals(
        lambda i, u: basis_ref[i, plane_at(u - HALO, planes)], lambda u: one_s[u], HALO + THIN + 1, top
    )
    for k, total in enumerate(totals):
        totals_ref[k] = total
    for copy in stores:
        copy.wait()


def edge_kernel(
    count, spread_ref, one_in, two_in, totals_in, basis_ref, pressure_in, far_ref, *refs
):
    statics, refs = refs[:6], refs[6:]
    pressure_ref, send_far_hbm, packed_hbm = refs[:3]
    coef_ref, one_s, two_s, tx_s, tail_s, sems = refs[3:]
    me = lax.axis_index("gx")
    planes = pressure_ref.shape[0]
    pressure_ref[pl.ds(THIN, planes - THIN)] = pressure_in[pl.ds(THIN, planes - THIN)]
    one_s[pl.ds(HALO, HALO)] = one_in[...]
    two_s[pl.ds(HALO + 1, HALO)] = two_in[...]
    all_coefficients(coef_ref, None, far_ref, statics, tx_s, 1, 2 * HALO)
    prolong(
        one_s, (0, HALO), gains_of(spread_ref[...], -1), lambda i, u, rows: far_ref[i * HALO + u, rows]
    )
    sweep(coef_ref, one_s, two_s, 1, HALO + 1)
    sweep(coef_ref, two_s, one_s, 2, HALO + 2)
    sweep(coef_ref, one_s, two_s, 3, HALO + 3)
    stores = started(
        [(two_s.at[pl.ds(2 * HALO - 1 - k, 1)], send_far_hbm.at[pl.ds(k, 1)]) for k in range(HALO)], sems
    )
    pressure_ref[pl.ds(0, THIN)] = two_s[pl.ds(HALO, THIN)]
    for u in range(HALO, 2 * HALO):
        one_s[u] = misfit(coef_ref, two_s, u)
    totals = restrict_totals(
        lambda i, u: basis_ref[i, u - HALO],
        lambda u: one_s[u],
        HALO,
        2 * HALO,
        [totals_in[k] for k in range(NBF * NYB)],
    )
    tail_s[...] = restricted_tile(totals, lane_of(me))
    stores += started(
        [(tail_s, packed_hbm.at[e]) for e in range(count)], sems, HALO
    )
    for copy in stores:
        copy.wait()


def last_kernel(
    basis_hbm, gathered_ref, inverse_ref, near_ref, far_ref, coupling_ref, pressure_ref, near_p_ref, far_p_ref,
    *refs
):
    statics, refs = refs[:6], refs[6:]
    pressure_out, residual_out, basis_ref, coef_ref, one_s, two_s, tx_s, pressure_s, residual_s, sems = refs
    planes = pressure_ref.shape[0]
    top = planes + HALO
    me = lax.axis_index("gx")
    load = started(((basis_hbm, basis_ref),), sems)[0]
    spread = corrected_values(coupling_ref, inverse_ref, window_of_tiles(gathered_ref, me))
    all_coefficients(coef_ref, near_ref, far_ref, statics, tx_s, 1, top + THIN)
    prolong(
        one_s, (0, HALO), gains_of(spread, -1), lambda i, u, rows: far_ref[i * HALO + u, rows],
        lambda u: far_p_ref[u],
    )
    prolong(
        one_s, (top, top + HALO), gains_of(spread, 1), lambda i, u, rows: near_ref[i * HALO + u - top, rows],
        lambda u: near_p_ref[u - top],
    )
    load.wait()
    prolong(
        one_s, (HALO, top), gains_of(spread, 0), lambda i, u, rows: basis_ref[i, plane_at(u - HALO, planes), rows],
        lambda u: pressure_ref[u - HALO],
    )
    sweep(coef_ref, one_s, two_s, 1, top + HALO - 1)
    sweep(coef_ref, two_s, one_s, 2, top + HALO - 2)
    sweep(coef_ref, one_s, two_s, 3, top + HALO - 3)
    for place in range(planes):
        pressure_s[plane_at(place, planes)] = two_s[place + HALO]
    stores = started(((pressure_s, pressure_out),), sems, 1)

    def step(u):
        residual_s[plane_at(u - HALO, planes)] = misfit(coef_ref, two_s, u)

    half = planes // 2
    for part in range(2):
        planes_in_groups(HALO + part * half, HALO + (part + 1) * half, half, step)
        span = pl.ds(plane_at(part * half, planes) - jnp.where(is_even(), 0, half - 1), half)
        stores += started(((residual_s.at[span], residual_out.at[span]),), sems, 2 + part)
    for copy in stores:
        copy.wait()


VMEM = pl.BlockSpec(memory_space=pltpu.VMEM)
ANY = pl.BlockSpec(memory_space=pl.ANY)


def kernel_call(name, body, arguments, outputs, scratch, aliases=None):
    spec = {pltpu.HBM: ANY, pltpu.VMEM: VMEM}
    call = pl.pallas_call(
        body,
        out_shape=[space(shape, dtype) for space, shape, dtype in outputs],
        in_specs=[spec[space] for space, _ in arguments],
        out_specs=[spec[space] for space, _, _ in outputs],
        scratch_shapes=scratch,
        input_output_aliases=aliases or {},
        compiler_params=pltpu.CompilerParams(vmem_limit_bytes=16 * 1024 * 1024),
        name=name,
    )
    return call(*[pltpu.with_memory_space_constraint(value, space) for space, value in arguments])


def local(
    right_side, wet_quarters, trans_x, trans_y, trans_z, storage, basis, coupling, coarse_inverse,
    owned_block, block_slot, neighbours,
):
    count = lax.axis_size("gx")
    planes, ny, nz = right_side.shape
    field = (ny, nz)
    full = planes + 2 * HALO
    near_pairs = [(i, i ^ 1) for i in range(count)]
    far_pairs = [(i, i + 1) for i in range(1, count - 1, 2)]
    far_pairs = far_pairs + [(b, a) for a, b in far_pairs]
    H, V = pltpu.HBM, pltpu.VMEM
    statics = [(H, a) for a in (right_side, wet_quarters, trans_x, trans_y, trans_z, storage)]
    halo = (H_ALL,) + field
    factors = pltpu.VMEM((full, 8) + field, F32)
    state = pltpu.VMEM((full,) + field, F32)
    own = pltpu.VMEM((planes,) + field, F32)
    window = pltpu.VMEM((count * PER + WIN, 128), F32)
    around = pltpu.VMEM((full,) + field, BF16)
    whole_basis = pltpu.VMEM(basis.shape, BF16)

    blocks = coarse_inverse.shape[2]
    near, far, packed, *fields, inverse, room, more_room = kernel_call(
        "restrict_first",
        first_kernel,
        [
            (H, owned_block), (H, basis), *statics, (H, coupling.reshape(KROWS, PER)),
            (H, coarse_inverse.reshape(NBF * NBF, blocks)),
        ],
        [(H, halo, BF16), (H, halo, BF16), (H, (count // 2, ROWS, 128), F32), (V, right_side.shape, F32)]
        + [(V, right_side.shape, BF16)] * 5
        + [(V, (NBF * NBF, WIN), F32), (V, right_side.shape, F32), (V, (KROWS, WIN), F32)],
        [
            pltpu.SMEM(owned_block.shape, jnp.int32),
            whole_basis,
            *[pltpu.VMEM(a.shape, a.dtype) for _, a in statics],
            pltpu.VMEM((KROWS, PER), F32),
            pltpu.VMEM((NBF * NBF, blocks), F32),
            pltpu.VMEM((ROWS, 128), F32),
            pltpu.VMEM((2,) + halo, BF16),
            pltpu.SemaphoreType.DMA((16 + count // 2,)),
        ],
    )
    far = lax.ppermute(far, "gx", far_pairs)
    ranks = list(range(count // 2))
    ranks[:4] = ranks[2:4] + ranks[:2]
    chips = [[core + 2 * chip for chip in ranks] for core in range(2)]
    half = lax.all_to_all(packed, "gx", 0, 0, axis_index_groups=chips, tiled=True)
    near = lax.ppermute(near, "gx", near_pairs)
    other = lax.ppermute(half, "gx", near_pairs)

    pressure, coupled, spread, one, two, totals, edge_basis, send_near = kernel_call(
        "iteration_first",
        body_kernel,
        [(H, basis)] + [(V, a) for a in (half, other, inverse, near, *fields, room, more_room)],
        [
            (V, (planes,) + field, F32),
            (V, (KROWS, WIN), F32),
            (V, (NBF, 3 * NYB * nz), F32),
            (V, (HALO,) + field, F32),
            (V, (HALO,) + field, F32),
            (V, (NBF * NYB, 8, nz), F32),
            (V, (NBF, HALO) + field, BF16),
            (H, (HALO,) + field, F32),
        ],
        [
            pltpu.VMEM((count * PER, KROWS + 128), F32),
            window, whole_basis, factors, state, state, around, pltpu.SemaphoreType.DMA((1 + HALO,)),
        ],
        {11: 0, 12: 1},
    )
    near_p = lax.ppermute(send_near, "gx", near_pairs)
    far, near_p = lax.optimization_barrier((far, near_p))
    pressure, send_far, packed = kernel_call(
        "edge_first",
        functools.partial(edge_kernel, count),
        [(V, a) for a in (spread, one, two, totals, edge_basis, pressure, far, *fields)],
        [
            (V, (planes,) + field, F32),
            (H, (HALO,) + field, F32),
            (H, (count, NBF, 128), F32),
        ],
        [
            factors, state, state, around,
            pltpu.VMEM((NBF, 128), F32), pltpu.SemaphoreType.DMA((HALO + count,)),
        ],
        {5: 0},
    )

    far_p = lax.ppermute(send_far, "gx", far_pairs)
    gathered = lax.all_to_all(packed, "gx", 0, 0, axis_index_groups=[tile_order(count)], tiled=True)
    whole = (H, (planes,) + field, F32)
    return kernel_call(
        "iteration_last",
        last_kernel,
        [(H, basis)]
        + [(V, a) for a in (gathered, inverse, near, far, coupled, pressure, near_p, far_p, *fields)],
        [whole, whole],
        [
            whole_basis, factors, state, state, around, own, own,
            pltpu.SemaphoreType.DMA((4,)),
        ],
    )


def solution(mesh):
    slabs = P(("parts", "gx"), None, None)
    placed = (
        slabs, slabs, slabs, slabs, slabs, slabs,
        P(None, ("parts", "gx"), None, None),
        P(None, None, None, ("parts", "gx")),
        P(None, None, "parts"),
        P(),
        P("gx"),
        P(None, "gx"),
    )
    return jax.shard_map(local, mesh=mesh, in_specs=placed, out_specs=(slabs, slabs), check_vma=False)
```

```python
import functools

import jax
import jax.numpy as jnp
from jax import lax
from jax.experimental import pallas as pl
from jax.experimental.pallas import tpu as pltpu
from jax.sharding import PartitionSpec as P

BLK = 16
NBF = 8
NNB = 6
SWEEPS = 3
CSWEEPS = 4
NYB = 2
NZB = 8
PER = NYB * NZB
WIN = 16 * PER
LEAD = 4
HALO = 4
OMEGA = 2.0 / 3.0
KROWS = NNB * NBF * NBF
ROWS = (KROWS // 128 * 2 + 1) * 8
F32 = jnp.float32
BF16 = jnp.bfloat16


THIN = HALO - 1
H_TX = NBF * HALO
H_REST = H_TX + HALO
H_WET = H_REST + 3 * THIN
H_ALL = H_REST + 6 * THIN


def planes_in_groups(low, high, group, step):
    count = (high - low) // group

    def body(k, carry):
        for j in range(group):
            step(low + k * group + j)
        return carry

    if count > 1:
        lax.fori_loop(0, count, body, 0)
    elif count:
        body(0, 0)
    for x in range(low + count * group, high):
        step(x)


def three_parts(x):
    high = x.astype(BF16)
    rest = x - high.astype(F32)
    middle = rest.astype(BF16)
    low = (rest - middle.astype(F32)).astype(BF16)
    return high, middle, low


def restrict_totals(basis_at, field_at, low, high, totals=None):
    def step(x, totals):
        field = field_at(x)
        out = []
        for i in range(NBF):
            for yb in range(NYB):
                rows = slice(yb * BLK, (yb + 1) * BLK)
                product = basis_at(i, x)[rows].astype(F32) * field[rows]
                out.append(totals[i * NYB + yb] + product[:8] + product[8:])
        return tuple(out)

    if totals is None:
        totals = (jnp.zeros((8, 128), F32),) * (NBF * NYB)
    return lax.fori_loop(low, high, step, tuple(totals))


def restricted(totals):
    groups = lax.broadcasted_iota(jnp.int32, (NZB, 3 * 128), 1)
    owner = lax.broadcasted_iota(jnp.int32, (NZB, 3 * 128), 0)
    spread = ((groups % 128) // BLK == owner).astype(F32).astype(BF16)
    halves = []
    for yb in range(NYB):
        rows = [jnp.sum(totals[i * NYB + yb], axis=0, keepdims=True) for i in range(NBF)]
        stacked = jnp.concatenate(three_parts(jnp.concatenate(rows, 0)), axis=1)
        halves.append(
            lax.dot_general(
                spread, stacked, (((1,), (1,)), ((), ())), preferred_element_type=F32
            )
        )
    return halves


def restricted_tile(totals, first):
    block = lax.broadcasted_iota(jnp.int32, (128, 128), 0) // BLK + first
    lane = lax.broadcasted_iota(jnp.int32, (128, 128), 1)
    tile = 0.0
    for yb in range(NYB):
        rows = [jnp.sum(totals[i * NYB + yb], axis=0, keepdims=True) for i in range(NBF)]
        stacked = jnp.concatenate(three_parts(jnp.concatenate(rows, 0)), axis=0)
        chosen = (lane == block + yb * NZB).astype(F32).astype(BF16)
        tile = tile + jnp.dot(stacked, chosen, preferred_element_type=F32)
    return tile[:NBF] + tile[NBF : 2 * NBF] + tile[2 * NBF :]


def lane_of(device):
    return lax.rem(device, 128 // PER) * PER


def tile_order(count):
    order = list(range(count))
    order[:8] = order[4:8] + order[:4]
    return order


def window_of_tiles(gathered_ref, me):
    per = 128 // PER
    halves = [0.0] * (WIN // 128)
    for rank, device in enumerate(tile_order(gathered_ref.shape[0])):
        place = device - me + LEAD
        for half in range(WIN // 128):
            inside = (place >= half * per) & (place < (half + 1) * per)
            halves[half] = halves[half] + jnp.where(inside, gathered_ref[rank], 0.0)
    turn = lax.rem(128 - lane_of(me + per - LEAD), 128)
    return jnp.concatenate([pltpu.roll(half, turn, 1) for half in halves], axis=1)


def started(pairs, sems, first=0):
    copies = [pltpu.make_async_copy(a, b, sems.at[first + k]) for k, (a, b) in enumerate(pairs)]
    for copy in copies:
        copy.start()
    return copies


def is_even():
    return lax.rem(lax.axis_index("gx"), 2) == 0


def plane_at(place, planes):
    return jnp.where(is_even(), place, planes - 1 - place)


def first_kernel(
    owned_hbm, basis_hbm, right_hbm, wet_hbm, tx_hbm, ty_hbm, tz_hbm, st_hbm, coupling_hbm, all_inverse_hbm,
    near_hbm, far_hbm, packed_hbm, *rest
):
    field_refs, inverse_ref, rest = rest[:6], rest[6], rest[9:]
    (
        owned_s, basis_s, right_s, wet_s, tx_s, ty_s, tz_s, st_s, coupling_s, all_inverse, rows_s, halo_s, sems
    ) = rest
    me = lax.axis_index("gx")
    planes = right_s.shape[0]
    wides = [[plane_at(HALO - 1 - k, planes) for k in range(HALO)], [plane_at(planes - 1 - k, planes) for k in range(HALO)]]
    thins = [wides[0][1:], wides[1][:THIN]]
    quarter = planes // 4
    spans = [pl.ds(k * quarter, quarter) for k in (0, 3, 1, 2)]
    pairs = [(right_hbm, right_s)] + [(basis_hbm.at[:, span], basis_s.at[:, span]) for span in spans[:2]]
    pairs += list(zip((wet_hbm, tx_hbm, ty_hbm, tz_hbm, st_hbm), (wet_s, tx_s, ty_s, tz_s, st_s)))
    edge = len(pairs)
    pairs += [(basis_hbm.at[:, span], basis_s.at[:, span]) for span in spans[2:]]
    pairs += [(owned_hbm, owned_s), (coupling_hbm, coupling_s), (all_inverse_hbm, all_inverse)]
    loads = started(pairs, sems)

    def basis_at(i, x):
        return basis_s[i, x]

    def right_at(x):
        return right_s[x]

    loads[0].wait()
    totals = None
    for k in (0, 3):
        loads[1 + k // 3].wait()
        totals = restrict_totals(basis_at, right_at, k * quarter, (k + 1) * quarter, totals)
    for copy in loads[3:edge]:
        copy.wait()
    stores = []
    for side in range(2):
        for k in range(HALO):
            for i in range(NBF):
                halo_s[side, i * HALO + k] = basis_s[i, wides[side][k]]
            halo_s[side, H_TX + k] = tx_s[wides[side][k]]
        for k, x in enumerate(thins[side]):
            for j, field in enumerate((ty_s, tz_s, st_s)):
                halo_s[side, H_REST + j * THIN + k] = field[x]
            right = right_s[x]
            high = right.astype(BF16)
            halo_s[side, H_WET + k] = wet_s[x].astype(F32).astype(BF16)
            halo_s[side, H_WET + THIN + k] = high
            halo_s[side, H_WET + 2 * THIN + k] = (right - high.astype(F32)).astype(BF16)
        stores += started(
            ((halo_s.at[side], (far_hbm, near_hbm)[side]),), sems, len(loads) + side
        )
    for k in (1, 2):
        loads[edge + k - 1].wait()
        totals = restrict_totals(basis_at, right_at, k * quarter, (k + 1) * quarter, totals)
    for copy in loads[edge + 2 :]:
        copy.wait()
    slot = lax.broadcasted_iota(jnp.int32, (8, 1), 0)
    parts = []
    for half, coarse in enumerate(restricted(totals)):
        block = jnp.zeros((8, 1), jnp.int32)
        for s in range(8):
            block = jnp.where(slot == s, owned_s[me * PER + half * 8 + s], block)
        parts += [coarse, block.astype(F32), jnp.zeros((8, 64 - NBF - 1), F32)]
    wide = jnp.concatenate([coupling_s[...], jnp.zeros((KROWS, 128 - PER), F32)], axis=1).T
    for r in range(2):
        for l in range(KROWS // 128):
            rows_s[pl.ds((r * (KROWS // 128) + l) * 8, 8)] = wide[r * 8 : r * 8 + 8, l * 128 : l * 128 + 128]
    rows_s[pl.ds(ROWS - 8, 8)] = jnp.concatenate(parts, axis=1)
    stores += started(
        [(rows_s, packed_hbm.at[chip]) for chip in range(packed_hbm.shape[0])], sems, len(loads) + 2
    )

    def place_fields(place):
        x = plane_at(place, planes)
        for source, target in zip((right_s, wet_s, tx_s, ty_s, tz_s, st_s), field_refs):
            plane = source[x]
            target[place] = plane.astype(F32).astype(BF16) if source is wet_s else plane

    planes_in_groups(0, planes, 4, place_fields)
    blocks = all_inverse.shape[1]
    start = (me - LEAD) * PER
    turned = pltpu.roll(all_inverse[...], lax.rem(blocks - start, blocks), 1)[:, :WIN]
    block = lax.broadcasted_iota(jnp.int32, turned.shape, 1) + start
    inverse_ref[...] = jnp.where((block >= 0) & (block < blocks), turned, 0.0)
    for copy in stores:
        copy.wait()


def coarse_solve(coupling_at, inverse_at, residual):
    lane = lax.broadcasted_iota(jnp.int32, (NBF, WIN), 1)
    in_z, in_y = lane % NZB, (lane // NZB) % NYB

    def rows_of(parts):
        return jnp.concatenate([jnp.sum(p, axis=0, keepdims=True) for p in parts], 0)

    def inverted(v):
        return rows_of([inverse_at(i) * v for i in range(NBF)])

    values = inverted(residual)
    for _ in range(CSWEEPS - 1):
        near = (
            pltpu.roll(values, WIN - PER, 1),
            pltpu.roll(values, PER, 1),
            jnp.where(in_y < NYB - 1, pltpu.roll(values, WIN - NZB, 1), 0.0),
            jnp.where(in_y > 0, pltpu.roll(values, NZB, 1), 0.0),
            jnp.where(in_z < NZB - 1, pltpu.roll(values, WIN - 1, 1), 0.0),
            jnp.where(in_z > 0, pltpu.roll(values, 1, 1), 0.0),
        )
        parts = []
        for i in range(NBF):
            total = coupling_at(0, i) * near[0]
            for k in range(1, NNB):
                total = total + coupling_at(k, i) * near[k]
            parts.append(total)
        values = inverted(residual - rows_of(parts))
    return values


def spread_blocks(values):
    width = 3 * NYB * 128
    block = lax.broadcasted_iota(jnp.int32, (128, width), 0)
    column = lax.broadcasted_iota(jnp.int32, (128, width), 1)
    wanted = (LEAD - 1) * PER + column // BLK
    chosen = (block == wanted).astype(F32).astype(BF16)
    stacked = jnp.concatenate(three_parts(values[:, :128]), axis=0)
    spread = jnp.dot(stacked, chosen, preferred_element_type=F32)
    return spread[:NBF] + spread[NBF : 2 * NBF] + spread[2 * NBF :]


def coefficients(coef_ref, x, quarters, right, east, west, north, upper, storage):
    in_y = lax.broadcasted_iota(jnp.int32, north.shape, 0)
    in_z = lax.broadcasted_iota(jnp.int32, north.shape, 1)
    last_y, last_z = north.shape[0] - 1, north.shape[1] - 1
    east, west, north, upper = (a.astype(F32) for a in (east, west, north, upper))
    wet = quarters * 0.25
    dry = 1.0 - jnp.minimum(quarters, 1.0)
    south = jnp.where(in_y > 0, pltpu.roll(north, 1, 0), 0.0)
    lower = jnp.where(in_z > 0, pltpu.roll(upper, 1, 1), 0.0)
    diag = wet * (storage.astype(F32) + east + west + north + south + upper + lower) + dry
    share = OMEGA / diag
    scale = wet * share
    coef_ref[x, 0] = scale * east
    coef_ref[x, 1] = scale * west
    coef_ref[x, 2] = jnp.where(in_y < last_y, scale * north, 0.0)
    coef_ref[x, 3] = scale * south
    coef_ref[x, 4] = jnp.where(in_z < last_z, scale * upper, 0.0)
    coef_ref[x, 5] = scale * lower
    coef_ref[x, 6] = right * share
    coef_ref[x, 7] = diag * (1.0 / OMEGA)


def all_coefficients(coef_ref, near_ref, far_ref, statics, tx_s, low, high):
    right_ref, wet_ref, tx_ref, ty_ref, tz_ref, st_ref = statics
    top = right_ref.shape[0] + HALO
    tx_s[pl.ds(HALO, top - HALO)] = tx_ref[...]
    if near_ref is not None:
        tx_s[pl.ds(top, HALO)] = near_ref[pl.ds(H_TX, HALO)]
    if far_ref is not None:
        tx_s[pl.ds(0, HALO)] = far_ref[pl.ds(H_TX, HALO)]
    turn = jnp.where(is_even(), 0, 1)

    def plane(u, quarters, right, north, upper, storage):
        coefficients(
            coef_ref, u, quarters.astype(F32), right, tx_s[u + turn], tx_s[u - 1 + turn], north, upper, storage
        )

    def own(u):
        x = u - HALO
        plane(u, wet_ref[x], right_ref[x], ty_ref[x], tz_ref[x], st_ref[x])

    def outside(u, halo, k):
        right = halo[H_WET + THIN + k].astype(F32) + halo[H_WET + 2 * THIN + k].astype(F32)
        plane(u, halo[H_WET + k], right, halo[H_REST + k], halo[H_REST + THIN + k], halo[H_REST + 2 * THIN + k])

    for u in range(low, HALO):
        outside(u, far_ref, u - 1)
    planes_in_groups(max(low, HALO), min(high, top), 8, own)
    for u in range(top, high):
        outside(u, near_ref, u - top)


def window_of(pieces, window_s, me):
    window_s[...] = jnp.zeros_like(window_s)
    for device, piece in pieces:
        window_s[pl.ds(pl.multiple_of((LEAD + device) * PER, PER), PER)] = piece
    return window_s[pl.ds(pl.multiple_of(me * PER, PER), WIN)].T[:NBF]


def blocks_in_order(rows_s, coupling_ref, me):
    lane = lax.broadcasted_iota(jnp.int32, (WIN, WIN), 1) + (me - LEAD) * PER
    for start in range(0, rows_s.shape[0], WIN):
        rows = rows_s[pl.ds(start, WIN)]
        block = rows[:, KROWS + NBF : KROWS + NBF + 1].astype(jnp.int32)
        chosen = (block == lane).astype(F32).astype(BF16)
        stacked = jnp.concatenate(three_parts(rows[:, :KROWS].T), axis=0)
        found = jnp.dot(stacked, chosen, preferred_element_type=F32)
        found = found[:KROWS] + found[KROWS : 2 * KROWS] + found[2 * KROWS :]
        coupling_ref[...] = found if start == 0 else coupling_ref[...] + found


def corrected_values(coupling_ref, inverse_ref, residual):
    values = coarse_solve(
        lambda k, i: coupling_ref[pl.ds((k * NBF + i) * NBF, NBF)],
        lambda i: inverse_ref[pl.ds(i * NBF, NBF)],
        residual,
    )
    return spread_blocks(values)


def prolong(state, places, gains, basis_at, base_at=None):
    wide = [
        [
            jnp.broadcast_to(gains[i : i + 1, yb * 128 : (yb + 1) * 128], (BLK, 128))
            for i in range(NBF)
        ]
        for yb in range(NYB)
    ]

    def step(u):
        for yb in range(NYB):
            rows = slice(yb * BLK, (yb + 1) * BLK)
            total = basis_at(0, u, rows).astype(F32) * wide[yb][0]
            for i in range(1, NBF):
                total = total + basis_at(i, u, rows).astype(F32) * wide[yb][i]
            state[u, rows] = total if base_at is None else base_at(u)[rows] + total

    planes_in_groups(places[0], places[1], 4, step)


def gains_of(spread, side):
    width = NYB * 128
    below, own, above = (spread[:, s * width : (s + 1) * width] for s in range(3))
    if side == 0:
        return own
    return jnp.where(is_even(), below if side < 0 else above, above if side < 0 else below)


def pulled(coef_ref, state, x):
    here = state[x]
    ny, nz = here.shape
    total = coef_ref[x, 6] + coef_ref[x, 0] * state[x + 1] + coef_ref[x, 1] * state[x - 1]
    total = total + coef_ref[x, 2] * pltpu.roll(here, ny - 1, 0) + coef_ref[x, 3] * pltpu.roll(here, 1, 0)
    total = total + coef_ref[x, 4] * pltpu.roll(here, nz - 1, 1) + coef_ref[x, 5] * pltpu.roll(here, 1, 1)
    return here, total


def sweep(coef_ref, source, target, low, high):
    def step(u):
        here, total = pulled(coef_ref, source, u)
        target[u] = (1.0 - OMEGA) * here + total

    planes_in_groups(low, high, high - low, step)


def misfit(coef_ref, source, x):
    here, total = pulled(coef_ref, source, x)
    return (total - OMEGA * here) * coef_ref[x, 7]


def body_kernel(
    basis_hbm, half_ref, other_ref, inverse_ref, near_ref, *refs
):
    statics, refs = refs[:6], refs[8:]
    pressure_ref, coupling_ref, spread_ref, one_out, two_out, totals_ref, edge_basis, send_near_hbm = refs[:8]
    rows_s, window_s, basis_ref, coef_ref, one_s, two_s, tx_s, sems = refs[8:]
    planes = pressure_ref.shape[0]
    top = planes + HALO
    me = lax.axis_index("gx")
    load = started(((basis_hbm, basis_ref),), sems)[0]
    core = lax.rem(me, 2)
    chips = half_ref.shape[0]

    def unpack(chip, carry):
        first = 2 * jnp.bitwise_xor(chip, 4)
        for ref, device in ((half_ref, first + core), (other_ref, first + 1 - core)):
            at = device * PER
            for r in range(2):
                rows = pl.ds(pl.multiple_of(at + r * 8, 8), 8)
                for l in range(KROWS // 128):
                    piece = ref[chip, pl.ds((r * (KROWS // 128) + l) * 8, 8)]
                    rows_s[rows, pl.ds(l * 128, 128)] = piece
                piece = ref[chip, pl.ds(ROWS - 8, 8)]
                rows_s[rows, pl.ds(KROWS, 128)] = pltpu.roll(piece, 64, 1) if r else piece
        return carry

    lax.fori_loop(0, chips, unpack, 0)
    blocks_in_order(rows_s, coupling_ref, me)
    pieces = [(e, rows_s[pl.ds(e * PER, PER), pl.ds(KROWS, 128)]) for e in range(2 * chips)]
    spread = corrected_values(coupling_ref, inverse_ref, window_of(pieces, window_s, me))
    spread_ref[...] = spread
    near_thin = near_ref.at[pl.ds(0, H_ALL)]
    all_coefficients(coef_ref, near_thin, None, statics, tx_s, HALO + 1, top + THIN)
    load.wait()
    prolong(one_s, (HALO, top), gains_of(spread, 0), lambda i, u, rows: basis_ref[i, plane_at(u - HALO, planes), rows])
    prolong(
        one_s, (top, top + HALO), gains_of(spread, 1), lambda i, u, rows: near_ref[i * HALO + u - top, rows]
    )
    sweep(coef_ref, one_s, two_s, HALO + 1, top + HALO - 1)
    sweep(coef_ref, two_s, one_s, HALO + 2, top + HALO - 2)
    sweep(coef_ref, one_s, two_s, HALO + 3, top + HALO - 3)
    for k in range(HALO):
        for i in range(NBF):
            edge_basis[i, k] = basis_ref[i, plane_at(k, planes)]
    one_out[...] = one_s[pl.ds(HALO, HALO)]
    two_out[...] = two_s[pl.ds(HALO + 1, HALO)]
    stores = started(
        [(two_s.at[pl.ds(top - 1 - k, 1)], send_near_hbm.at[pl.ds(k, 1)]) for k in range(HALO)], sems, 1
    )
    done = planes - THIN
    pressure_ref[pl.ds(THIN, done)] = two_s[pl.ds(HALO + THIN, done)]

    def step(u):
        one_s[u] = misfit(coef_ref, two_s, u)

    planes_in_groups(HALO + THIN + 1, top, planes - THIN - 1, step)
    totals = restrict_totals(
        lambda i, u: basis_ref[i, plane_at(u - HALO, planes)], lambda u: one_s[u], HALO + THIN + 1, top
    )
    for k, total in enumerate(totals):
        totals_ref[k] = total
    for copy in stores:
        copy.wait()


def edge_kernel(
    count, spread_ref, one_in, two_in, totals_in, basis_ref, pressure_in, far_ref, *refs
):
    statics, refs = refs[:6], refs[6:]
    pressure_ref, send_far_hbm, packed_hbm = refs[:3]
    coef_ref, one_s, two_s, tx_s, tail_s, sems = refs[3:]
    me = lax.axis_index("gx")
    planes = pressure_ref.shape[0]
    pressure_ref[pl.ds(THIN, planes - THIN)] = pressure_in[pl.ds(THIN, planes - THIN)]
    one_s[pl.ds(HALO, HALO)] = one_in[...]
    two_s[pl.ds(HALO + 1, HALO)] = two_in[...]
    all_coefficients(coef_ref, None, far_ref, statics, tx_s, 1, 2 * HALO)
    prolong(
        one_s, (0, HALO), gains_of(spread_ref[...], -1), lambda i, u, rows: far_ref[i * HALO + u, rows]
    )
    sweep(coef_ref, one_s, two_s, 1, HALO + 1)
    sweep(coef_ref, two_s, one_s, 2, HALO + 2)
    sweep(coef_ref, one_s, two_s, 3, HALO + 3)
    stores = started(
        [(two_s.at[pl.ds(2 * HALO - 1 - k, 1)], send_far_hbm.at[pl.ds(k, 1)]) for k in range(HALO)], sems
    )
    pressure_ref[pl.ds(0, THIN)] = two_s[pl.ds(HALO, THIN)]
    for u in range(HALO, 2 * HALO):
        one_s[u] = misfit(coef_ref, two_s, u)
    totals = restrict_totals(
        lambda i, u: basis_ref[i, u - HALO],
        lambda u: one_s[u],
        HALO,
        2 * HALO,
        [totals_in[k] for k in range(NBF * NYB)],
    )
    tail_s[...] = restricted_tile(totals, lane_of(me))
    stores += started(
        [(tail_s, packed_hbm.at[e]) for e in range(count)], sems, HALO
    )
    for copy in stores:
        copy.wait()


def last_kernel(
    basis_hbm, gathered_ref, inverse_ref, near_ref, far_ref, coupling_ref, pressure_ref, near_p_ref, far_p_ref,
    *refs
):
    statics, refs = refs[:6], refs[6:]
    pressure_out, residual_out, basis_ref, coef_ref, one_s, two_s, tx_s, pressure_s, residual_s, sems = refs
    planes = pressure_ref.shape[0]
    top = planes + HALO
    me = lax.axis_index("gx")
    load = started(((basis_hbm, basis_ref),), sems)[0]
    spread = corrected_values(coupling_ref, inverse_ref, window_of_tiles(gathered_ref, me))
    all_coefficients(coef_ref, near_ref, far_ref, statics, tx_s, 1, top + THIN)
    prolong(
        one_s, (0, HALO), gains_of(spread, -1), lambda i, u, rows: far_ref[i * HALO + u, rows],
        lambda u: far_p_ref[u],
    )
    prolong(
        one_s, (top, top + HALO), gains_of(spread, 1), lambda i, u, rows: near_ref[i * HALO + u - top, rows],
        lambda u: near_p_ref[u - top],
    )
    load.wait()
    prolong(
        one_s, (HALO, top), gains_of(spread, 0), lambda i, u, rows: basis_ref[i, plane_at(u - HALO, planes), rows],
        lambda u: pressure_ref[u - HALO],
    )
    sweep(coef_ref, one_s, two_s, 1, top + HALO - 1)
    sweep(coef_ref, two_s, one_s, 2, top + HALO - 2)
    sweep(coef_ref, one_s, two_s, 3, top + HALO - 3)
    for place in range(planes):
        pressure_s[plane_at(place, planes)] = two_s[place + HALO]
    stores = started(((pressure_s, pressure_out),), sems, 1)

    def step(u):
        residual_s[plane_at(u - HALO, planes)] = misfit(coef_ref, two_s, u)

    half = planes // 2
    for part in range(2):
        planes_in_groups(HALO + part * half, HALO + (part + 1) * half, half, step)
        span = pl.ds(plane_at(part * half, planes) - jnp.where(is_even(), 0, half - 1), half)
        stores += started(((residual_s.at[span], residual_out.at[span]),), sems, 2 + part)
    for copy in stores:
        copy.wait()


VMEM = pl.BlockSpec(memory_space=pltpu.VMEM)
ANY = pl.BlockSpec(memory_space=pl.ANY)


def kernel_call(name, body, arguments, outputs, scratch, aliases=None):
    spec = {pltpu.HBM: ANY, pltpu.VMEM: VMEM}
    call = pl.pallas_call(
        body,
        out_shape=[space(shape, dtype) for space, shape, dtype in outputs],
        in_specs=[spec[space] for space, _ in arguments],
        out_specs=[spec[space] for space, _, _ in outputs],
        scratch_shapes=scratch,
        input_output_aliases=aliases or {},
        compiler_params=pltpu.CompilerParams(vmem_limit_bytes=16 * 1024 * 1024),
        name=name,
    )
    return call(*[pltpu.with_memory_space_constraint(value, space) for space, value in arguments])


def local(
    right_side, wet_quarters, trans_x, trans_y, trans_z, storage, basis, coupling, coarse_inverse,
    owned_block, block_slot, neighbours,
):
    count = lax.axis_size("gx")
    planes, ny, nz = right_side.shape
    field = (ny, nz)
    full = planes + 2 * HALO
    near_pairs = [(i, i ^ 1) for i in range(count)]
    far_pairs = [(i, i + 1) for i in range(1, count - 1, 2)]
    far_pairs = far_pairs + [(b, a) for a, b in far_pairs]
    H, V = pltpu.HBM, pltpu.VMEM
    statics = [(H, a) for a in (right_side, wet_quarters, trans_x, trans_y, trans_z, storage)]
    halo = (H_ALL,) + field
    factors = pltpu.VMEM((full, 8) + field, F32)
    state = pltpu.VMEM((full,) + field, F32)
    own = pltpu.VMEM((planes,) + field, F32)
    window = pltpu.VMEM((count * PER + WIN, 128), F32)
    around = pltpu.VMEM((full,) + field, BF16)
    whole_basis = pltpu.VMEM(basis.shape, BF16)

    blocks = coarse_inverse.shape[2]
    near, far, packed, *fields, inverse, room, more_room = kernel_call(
        "restrict_first",
        first_kernel,
        [
            (H, owned_block), (H, basis), *statics, (H, coupling.reshape(KROWS, PER)),
            (H, coarse_inverse.reshape(NBF * NBF, blocks)),
        ],
        [(H, halo, BF16), (H, halo, BF16), (H, (count // 2, ROWS, 128), F32), (V, right_side.shape, F32)]
        + [(V, right_side.shape, BF16)] * 5
        + [(V, (NBF * NBF, WIN), F32), (V, right_side.shape, F32), (V, (KROWS, WIN), F32)],
        [
            pltpu.SMEM(owned_block.shape, jnp.int32),
            whole_basis,
            *[pltpu.VMEM(a.shape, a.dtype) for _, a in statics],
            pltpu.VMEM((KROWS, PER), F32),
            pltpu.VMEM((NBF * NBF, blocks), F32),
            pltpu.VMEM((ROWS, 128), F32),
            pltpu.VMEM((2,) + halo, BF16),
            pltpu.SemaphoreType.DMA((16 + count // 2,)),
        ],
    )
    far = lax.ppermute(far, "gx", far_pairs)
    ranks = list(range(count // 2))
    ranks = [rank ^ 4 for rank in ranks]
    chips = [[core + 2 * chip for chip in ranks] for core in range(2)]
    half = lax.all_to_all(packed, "gx", 0, 0, axis_index_groups=chips, tiled=True)
    near = lax.ppermute(near, "gx", near_pairs)
    other = lax.ppermute(half, "gx", near_pairs)

    pressure, coupled, spread, one, two, totals, edge_basis, send_near = kernel_call(
        "iteration_first",
        body_kernel,
        [(H, basis)] + [(V, a) for a in (half, other, inverse, near, *fields, room, more_room)],
        [
            (V, (planes,) + field, F32),
            (V, (KROWS, WIN), F32),
            (V, (NBF, 3 * NYB * nz), F32),
            (V, (HALO,) + field, F32),
            (V, (HALO,) + field, F32),
            (V, (NBF * NYB, 8, nz), F32),
            (V, (NBF, HALO) + field, BF16),
            (H, (HALO,) + field, F32),
        ],
        [
            pltpu.VMEM((count * PER, KROWS + 128), F32),
            window, whole_basis, factors, state, state, around, pltpu.SemaphoreType.DMA((1 + HALO,)),
        ],
        {11: 0, 12: 1},
    )
    near_p = lax.ppermute(send_near, "gx", near_pairs)
    far, near_p = lax.optimization_barrier((far, near_p))
    pressure, send_far, packed = kernel_call(
        "edge_first",
        functools.partial(edge_kernel, count),
        [(V, a) for a in (spread, one, two, totals, edge_basis, pressure, far, *fields)],
        [
            (V, (planes,) + field, F32),
            (H, (HALO,) + field, F32),
            (H, (count, NBF, 128), F32),
        ],
        [
            factors, state, state, around,
            pltpu.VMEM((NBF, 128), F32), pltpu.SemaphoreType.DMA((HALO + count,)),
        ],
        {5: 0},
    )

    far_p = lax.ppermute(send_far, "gx", far_pairs)
    gathered = lax.all_to_all(packed, "gx", 0, 0, axis_index_groups=[tile_order(count)], tiled=True)
    whole = (H, (planes,) + field, F32)
    return kernel_call(
        "iteration_last",
        last_kernel,
        [(H, basis)]
        + [(V, a) for a in (gathered, inverse, near, far, coupled, pressure, near_p, far_p, *fields)],
        [whole, whole],
        [
            whole_basis, factors, state, state, around, own, own,
            pltpu.SemaphoreType.DMA((4,)),
        ],
    )


def solution(mesh):
    slabs = P(("parts", "gx"), None, None)
    placed = (
        slabs, slabs, slabs, slabs, slabs, slabs,
        P(None, ("parts", "gx"), None, None),
        P(None, None, None, ("parts", "gx")),
        P(None, None, "parts"),
        P(),
        P("gx"),
        P(None, "gx"),
    )
    return jax.shard_map(local, mesh=mesh, in_specs=placed, out_specs=(slabs, slabs), check_vma=False)
```

```python
import functools

import jax
import jax.numpy as jnp
from jax import lax
from jax.experimental import pallas as pl
from jax.experimental.pallas import tpu as pltpu
from jax.sharding import PartitionSpec as P

BLK = 16
NBF = 8
NNB = 6
SWEEPS = 3
CSWEEPS = 4
NYB = 2
NZB = 8
PER = NYB * NZB
WIN = 16 * PER
LEAD = 4
HALO = 4
OMEGA = 2.0 / 3.0
KROWS = NNB * NBF * NBF
ROWS = (KROWS // 128 * 2 + 1) * 8
F32 = jnp.float32
BF16 = jnp.bfloat16


THIN = HALO - 1
H_TX = NBF * HALO
H_REST = H_TX + HALO
H_WET = H_REST + 3 * THIN
H_ALL = H_REST + 6 * THIN


def planes_in_groups(low, high, group, step):
    count = (high - low) // group

    def body(k, carry):
        for j in range(group):
            step(low + k * group + j)
        return carry

    if count > 1:
        lax.fori_loop(0, count, body, 0)
    elif count:
        body(0, 0)
    for x in range(low + count * group, high):
        step(x)


def three_parts(x):
    high = x.astype(BF16)
    rest = x - high.astype(F32)
    middle = rest.astype(BF16)
    low = (rest - middle.astype(F32)).astype(BF16)
    return high, middle, low


def restrict_totals(basis_at, field_at, low, high, totals=None):
    def step(x, totals):
        field = field_at(x)
        out = []
        for i in range(NBF):
            for yb in range(NYB):
                rows = slice(yb * BLK, (yb + 1) * BLK)
                product = basis_at(i, x)[rows].astype(F32) * field[rows]
                out.append(totals[i * NYB + yb] + product[:8] + product[8:])
        return tuple(out)

    if totals is None:
        totals = (jnp.zeros((8, 128), F32),) * (NBF * NYB)
    return lax.fori_loop(low, high, step, tuple(totals), unroll=high - low <= 4)


def restricted(totals):
    groups = lax.broadcasted_iota(jnp.int32, (NZB, 3 * 128), 1)
    owner = lax.broadcasted_iota(jnp.int32, (NZB, 3 * 128), 0)
    spread = ((groups % 128) // BLK == owner).astype(F32).astype(BF16)
    halves = []
    for yb in range(NYB):
        rows = [jnp.sum(totals[i * NYB + yb], axis=0, keepdims=True) for i in range(NBF)]
        stacked = jnp.concatenate(three_parts(jnp.concatenate(rows, 0)), axis=1)
        halves.append(
            lax.dot_general(
                spread, stacked, (((1,), (1,)), ((), ())), preferred_element_type=F32
            )
        )
    return halves


def restricted_tile(totals, first):
    block = lax.broadcasted_iota(jnp.int32, (128, 128), 0) // BLK + first
    lane = lax.broadcasted_iota(jnp.int32, (128, 128), 1)
    tile = 0.0
    for yb in range(NYB):
        rows = [jnp.sum(totals[i * NYB + yb], axis=0, keepdims=True) for i in range(NBF)]
        stacked = jnp.concatenate(three_parts(jnp.concatenate(rows, 0)), axis=0)
        chosen = (lane == block + yb * NZB).astype(F32).astype(BF16)
        tile = tile + jnp.dot(stacked, chosen, preferred_element_type=F32)
    return tile[:NBF] + tile[NBF : 2 * NBF] + tile[2 * NBF :]


def lane_of(device):
    return lax.rem(device, 128 // PER) * PER


def tile_order(count):
    order = list(range(count))
    order[:8] = order[4:8] + order[:4]
    return order


def window_of_tiles(gathered_ref, me):
    per = 128 // PER
    halves = [0.0] * (WIN // 128)
    for rank, device in enumerate(tile_order(gathered_ref.shape[0])):
        place = device - me + LEAD
        for half in range(WIN // 128):
            inside = (place >= half * per) & (place < (half + 1) * per)
            halves[half] = halves[half] + jnp.where(inside, gathered_ref[rank], 0.0)
    turn = lax.rem(128 - lane_of(me + per - LEAD), 128)
    return jnp.concatenate([pltpu.roll(half, turn, 1) for half in halves], axis=1)


def started(pairs, sems, first=0):
    copies = [pltpu.make_async_copy(a, b, sems.at[first + k]) for k, (a, b) in enumerate(pairs)]
    for copy in copies:
        copy.start()
    return copies


def is_even():
    return lax.rem(lax.axis_index("gx"), 2) == 0


def plane_at(place, planes):
    return jnp.where(is_even(), place, planes - 1 - place)


def first_kernel(
    owned_hbm, basis_hbm, right_hbm, wet_hbm, tx_hbm, ty_hbm, tz_hbm, st_hbm, coupling_hbm, all_inverse_hbm,
    near_hbm, far_hbm, packed_hbm, *rest
):
    field_refs, inverse_ref, rest = rest[:6], rest[6], rest[9:]
    (
        owned_s, basis_s, right_s, wet_s, tx_s, ty_s, tz_s, st_s, coupling_s, all_inverse, rows_s, halo_s, sems
    ) = rest
    me = lax.axis_index("gx")
    planes = right_s.shape[0]
    wides = [[plane_at(HALO - 1 - k, planes) for k in range(HALO)], [plane_at(planes - 1 - k, planes) for k in range(HALO)]]
    thins = [wides[0][1:], wides[1][:THIN]]
    quarter = planes // 4
    spans = [pl.ds(k * quarter, quarter) for k in (0, 3, 1, 2)]
    pairs = [(right_hbm, right_s)] + [(basis_hbm.at[:, span], basis_s.at[:, span]) for span in spans[:2]]
    pairs += list(zip((wet_hbm, tx_hbm, ty_hbm, tz_hbm, st_hbm), (wet_s, tx_s, ty_s, tz_s, st_s)))
    edge = len(pairs)
    pairs += [(basis_hbm.at[:, span], basis_s.at[:, span]) for span in spans[2:]]
    pairs += [(owned_hbm, owned_s), (coupling_hbm, coupling_s), (all_inverse_hbm, all_inverse)]
    loads = started(pairs, sems)

    def basis_at(i, x):
        return basis_s[i, x]

    def right_at(x):
        return right_s[x]

    loads[0].wait()
    totals = None
    for k in (0, 3):
        loads[1 + k // 3].wait()
        totals = restrict_totals(basis_at, right_at, k * quarter, (k + 1) * quarter, totals)
    for copy in loads[3:edge]:
        copy.wait()
    stores = []
    for side in range(2):
        for k in range(HALO):
            for i in range(NBF):
                halo_s[side, i * HALO + k] = basis_s[i, wides[side][k]]
            halo_s[side, H_TX + k] = tx_s[wides[side][k]]
        for k, x in enumerate(thins[side]):
            for j, field in enumerate((ty_s, tz_s, st_s)):
                halo_s[side, H_REST + j * THIN + k] = field[x]
            right = right_s[x]
            high = right.astype(BF16)
            halo_s[side, H_WET + k] = wet_s[x].astype(F32).astype(BF16)
            halo_s[side, H_WET + THIN + k] = high
            halo_s[side, H_WET + 2 * THIN + k] = (right - high.astype(F32)).astype(BF16)
        stores += started(
            ((halo_s.at[side], (far_hbm, near_hbm)[side]),), sems, len(loads) + side
        )
    for k in (1, 2):
        loads[edge + k - 1].wait()
        totals = restrict_totals(basis_at, right_at, k * quarter, (k + 1) * quarter, totals)
    for copy in loads[edge + 2 :]:
        copy.wait()
    slot = lax.broadcasted_iota(jnp.int32, (8, 1), 0)
    parts = []
    for half, coarse in enumerate(restricted(totals)):
        block = jnp.zeros((8, 1), jnp.int32)
        for s in range(8):
            block = jnp.where(slot == s, owned_s[me * PER + half * 8 + s], block)
        parts += [coarse, block.astype(F32), jnp.zeros((8, 64 - NBF - 1), F32)]
    wide = jnp.concatenate([coupling_s[...], jnp.zeros((KROWS, 128 - PER), F32)], axis=1).T
    for r in range(2):
        for l in range(KROWS // 128):
            rows_s[pl.ds((r * (KROWS // 128) + l) * 8, 8)] = wide[r * 8 : r * 8 + 8, l * 128 : l * 128 + 128]
    rows_s[pl.ds(ROWS - 8, 8)] = jnp.concatenate(parts, axis=1)
    stores += started(
        [(rows_s, packed_hbm.at[chip]) for chip in range(packed_hbm.shape[0])], sems, len(loads) + 2
    )

    def place_fields(place):
        x = plane_at(place, planes)
        for source, target in zip((right_s, wet_s, tx_s, ty_s, tz_s, st_s), field_refs):
            plane = source[x]
            target[place] = plane.astype(F32).astype(BF16) if source is wet_s else plane

    planes_in_groups(0, planes, 4, place_fields)
    blocks = all_inverse.shape[1]
    start = (me - LEAD) * PER
    turned = pltpu.roll(all_inverse[...], lax.rem(blocks - start, blocks), 1)[:, :WIN]
    block = lax.broadcasted_iota(jnp.int32, turned.shape, 1) + start
    inverse_ref[...] = jnp.where((block >= 0) & (block < blocks), turned, 0.0)
    for copy in stores:
        copy.wait()


def coarse_solve(coupling_at, inverse_at, residual):
    lane = lax.broadcasted_iota(jnp.int32, (NBF, WIN), 1)
    in_z, in_y = lane % NZB, (lane // NZB) % NYB

    def rows_of(parts):
        return jnp.concatenate([jnp.sum(p, axis=0, keepdims=True) for p in parts], 0)

    def inverted(v):
        return rows_of([inverse_at(i) * v for i in range(NBF)])

    values = inverted(residual)
    for _ in range(CSWEEPS - 1):
        near = (
            pltpu.roll(values, WIN - PER, 1),
            pltpu.roll(values, PER, 1),
            jnp.where(in_y < NYB - 1, pltpu.roll(values, WIN - NZB, 1), 0.0),
            jnp.where(in_y > 0, pltpu.roll(values, NZB, 1), 0.0),
            jnp.where(in_z < NZB - 1, pltpu.roll(values, WIN - 1, 1), 0.0),
            jnp.where(in_z > 0, pltpu.roll(values, 1, 1), 0.0),
        )
        parts = []
        for i in range(NBF):
            total = coupling_at(0, i) * near[0]
            for k in range(1, NNB):
                total = total + coupling_at(k, i) * near[k]
            parts.append(total)
        values = inverted(residual - rows_of(parts))
    return values


def spread_blocks(values):
    width = 3 * NYB * 128
    block = lax.broadcasted_iota(jnp.int32, (128, width), 0)
    column = lax.broadcasted_iota(jnp.int32, (128, width), 1)
    wanted = (LEAD - 1) * PER + column // BLK
    chosen = (block == wanted).astype(F32).astype(BF16)
    stacked = jnp.concatenate(three_parts(values[:, :128]), axis=0)
    spread = jnp.dot(stacked, chosen, preferred_element_type=F32)
    return spread[:NBF] + spread[NBF : 2 * NBF] + spread[2 * NBF :]


def coefficients(coef_ref, x, quarters, right, east, west, north, upper, storage):
    in_y = lax.broadcasted_iota(jnp.int32, north.shape, 0)
    in_z = lax.broadcasted_iota(jnp.int32, north.shape, 1)
    last_y, last_z = north.shape[0] - 1, north.shape[1] - 1
    east, west, north, upper = (a.astype(F32) for a in (east, west, north, upper))
    wet = quarters * 0.25
    dry = 1.0 - jnp.minimum(quarters, 1.0)
    south = jnp.where(in_y > 0, pltpu.roll(north, 1, 0), 0.0)
    lower = jnp.where(in_z > 0, pltpu.roll(upper, 1, 1), 0.0)
    diag = wet * (storage.astype(F32) + east + west + north + south + upper + lower) + dry
    share = OMEGA / diag
    scale = wet * share
    coef_ref[x, 0] = scale * east
    coef_ref[x, 1] = scale * west
    coef_ref[x, 2] = jnp.where(in_y < last_y, scale * north, 0.0)
    coef_ref[x, 3] = scale * south
    coef_ref[x, 4] = jnp.where(in_z < last_z, scale * upper, 0.0)
    coef_ref[x, 5] = scale * lower
    coef_ref[x, 6] = right * share
    coef_ref[x, 7] = diag * (1.0 / OMEGA)


def all_coefficients(coef_ref, near_ref, far_ref, statics, tx_s, low, high):
    right_ref, wet_ref, tx_ref, ty_ref, tz_ref, st_ref = statics
    top = right_ref.shape[0] + HALO
    tx_s[pl.ds(HALO, top - HALO)] = tx_ref[...]
    if near_ref is not None:
        tx_s[pl.ds(top, HALO)] = near_ref[pl.ds(H_TX, HALO)]
    if far_ref is not None:
        tx_s[pl.ds(0, HALO)] = far_ref[pl.ds(H_TX, HALO)]
    turn = jnp.where(is_even(), 0, 1)

    def plane(u, quarters, right, north, upper, storage):
        coefficients(
            coef_ref, u, quarters.astype(F32), right, tx_s[u + turn], tx_s[u - 1 + turn], north, upper, storage
        )

    def own(u):
        x = u - HALO
        plane(u, wet_ref[x], right_ref[x], ty_ref[x], tz_ref[x], st_ref[x])

    def outside(u, halo, k):
        right = halo[H_WET + THIN + k].astype(F32) + halo[H_WET + 2 * THIN + k].astype(F32)
        plane(u, halo[H_WET + k], right, halo[H_REST + k], halo[H_REST + THIN + k], halo[H_REST + 2 * THIN + k])

    for u in range(low, HALO):
        outside(u, far_ref, u - 1)
    planes_in_groups(max(low, HALO), min(high, top), 8, own)
    for u in range(top, high):
        outside(u, near_ref, u - top)


def window_of(pieces, window_s, me):
    window_s[...] = jnp.zeros_like(window_s)
    for device, piece in pieces:
        window_s[pl.ds(pl.multiple_of((LEAD + device) * PER, PER), PER)] = piece
    return window_s[pl.ds(pl.multiple_of(me * PER, PER), WIN)].T[:NBF]


def blocks_in_order(rows_s, coupling_ref, me):
    lane = lax.broadcasted_iota(jnp.int32, (WIN, WIN), 1) + (me - LEAD) * PER
    for start in range(0, rows_s.shape[0], WIN):
        rows = rows_s[pl.ds(start, WIN)]
        block = rows[:, KROWS + NBF : KROWS + NBF + 1].astype(jnp.int32)
        chosen = (block == lane).astype(F32).astype(BF16)
        stacked = jnp.concatenate(three_parts(rows[:, :KROWS].T), axis=0)
        found = jnp.dot(stacked, chosen, preferred_element_type=F32)
        found = found[:KROWS] + found[KROWS : 2 * KROWS] + found[2 * KROWS :]
        coupling_ref[...] = found if start == 0 else coupling_ref[...] + found


def corrected_values(coupling_ref, inverse_ref, residual):
    values = coarse_solve(
        lambda k, i: coupling_ref[pl.ds((k * NBF + i) * NBF, NBF)],
        lambda i: inverse_ref[pl.ds(i * NBF, NBF)],
        residual,
    )
    return spread_blocks(values)


def prolong(state, places, gains, basis_at, base_at=None):
    wide = [
        [
            jnp.broadcast_to(gains[i : i + 1, yb * 128 : (yb + 1) * 128], (BLK, 128))
            for i in range(NBF)
        ]
        for yb in range(NYB)
    ]

    def step(u):
        for yb in range(NYB):
            rows = slice(yb * BLK, (yb + 1) * BLK)
            total = basis_at(0, u, rows).astype(F32) * wide[yb][0]
            for i in range(1, NBF):
                total = total + basis_at(i, u, rows).astype(F32) * wide[yb][i]
            state[u, rows] = total if base_at is None else base_at(u)[rows] + total

    planes_in_groups(places[0], places[1], 4, step)


def gains_of(spread, side):
    width = NYB * 128
    below, own, above = (spread[:, s * width : (s + 1) * width] for s in range(3))
    if side == 0:
        return own
    return jnp.where(is_even(), below if side < 0 else above, above if side < 0 else below)


def pulled(coef_ref, state, x):
    here = state[x]
    ny, nz = here.shape
    total = coef_ref[x, 6] + coef_ref[x, 0] * state[x + 1] + coef_ref[x, 1] * state[x - 1]
    total = total + coef_ref[x, 2] * pltpu.roll(here, ny - 1, 0) + coef_ref[x, 3] * pltpu.roll(here, 1, 0)
    total = total + coef_ref[x, 4] * pltpu.roll(here, nz - 1, 1) + coef_ref[x, 5] * pltpu.roll(here, 1, 1)
    return here, total


def sweep(coef_ref, source, target, low, high):
    def step(u):
        here, total = pulled(coef_ref, source, u)
        target[u] = (1.0 - OMEGA) * here + total

    planes_in_groups(low, high, high - low, step)


def misfit(coef_ref, source, x):
    here, total = pulled(coef_ref, source, x)
    return (total - OMEGA * here) * coef_ref[x, 7]


def body_kernel(
    basis_hbm, half_ref, other_ref, inverse_ref, near_ref, *refs
):
    statics, refs = refs[:6], refs[8:]
    pressure_ref, coupling_ref, spread_ref, one_out, two_out, totals_ref, edge_basis, send_near_hbm = refs[:8]
    rows_s, window_s, basis_ref, coef_ref, one_s, two_s, tx_s, sems = refs[8:]
    planes = pressure_ref.shape[0]
    top = planes + HALO
    me = lax.axis_index("gx")
    load = started(((basis_hbm, basis_ref),), sems)[0]
    core = lax.rem(me, 2)
    chips = half_ref.shape[0]

    def unpack(chip, carry):
        first = 2 * jnp.bitwise_xor(chip, 4)
        for ref, device in ((half_ref, first + core), (other_ref, first + 1 - core)):
            at = device * PER
            for r in range(2):
                rows = pl.ds(pl.multiple_of(at + r * 8, 8), 8)
                for l in range(KROWS // 128):
                    piece = ref[chip, pl.ds((r * (KROWS // 128) + l) * 8, 8)]
                    rows_s[rows, pl.ds(l * 128, 128)] = piece
                piece = ref[chip, pl.ds(ROWS - 8, 8)]
                rows_s[rows, pl.ds(KROWS, 128)] = pltpu.roll(piece, 64, 1) if r else piece
        return carry

    lax.fori_loop(0, chips, unpack, 0)
    blocks_in_order(rows_s, coupling_ref, me)
    pieces = [(e, rows_s[pl.ds(e * PER, PER), pl.ds(KROWS, 128)]) for e in range(2 * chips)]
    spread = corrected_values(coupling_ref, inverse_ref, window_of(pieces, window_s, me))
    spread_ref[...] = spread
    near_thin = near_ref.at[pl.ds(0, H_ALL)]
    all_coefficients(coef_ref, near_thin, None, statics, tx_s, HALO + 1, top + THIN)
    load.wait()
    prolong(one_s, (HALO, top), gains_of(spread, 0), lambda i, u, rows: basis_ref[i, plane_at(u - HALO, planes), rows])
    prolong(
        one_s, (top, top + HALO), gains_of(spread, 1), lambda i, u, rows: near_ref[i * HALO + u - top, rows]
    )
    sweep(coef_ref, one_s, two_s, HALO + 1, top + HALO - 1)
    sweep(coef_ref, two_s, one_s, HALO + 2, top + HALO - 2)
    sweep(coef_ref, one_s, two_s, HALO + 3, top + HALO - 3)
    for k in range(HALO):
        for i in range(NBF):
            edge_basis[i, k] = basis_ref[i, plane_at(k, planes)]
    one_out[...] = one_s[pl.ds(HALO, HALO)]
    two_out[...] = two_s[pl.ds(HALO + 1, HALO)]
    stores = started(
        [(two_s.at[pl.ds(top - 1 - k, 1)], send_near_hbm.at[pl.ds(k, 1)]) for k in range(HALO)], sems, 1
    )
    done = planes - THIN
    pressure_ref[pl.ds(THIN, done)] = two_s[pl.ds(HALO + THIN, done)]

    def step(u):
        one_s[u] = misfit(coef_ref, two_s, u)

    planes_in_groups(HALO + THIN + 1, top, planes - THIN - 1, step)
    totals = restrict_totals(
        lambda i, u: basis_ref[i, plane_at(u - HALO, planes)], lambda u: one_s[u], HALO + THIN + 1, top
    )
    for k, total in enumerate(totals):
        totals_ref[k] = total
    for copy in stores:
        copy.wait()


def edge_kernel(
    count, spread_ref, one_in, two_in, totals_in, basis_ref, pressure_in, far_ref, *refs
):
    statics, refs = refs[:6], refs[6:]
    pressure_ref, send_far_hbm, packed_hbm = refs[:3]
    coef_ref, one_s, two_s, tx_s, tail_s, sems = refs[3:]
    me = lax.axis_index("gx")
    planes = pressure_ref.shape[0]
    pressure_ref[pl.ds(THIN, planes - THIN)] = pressure_in[pl.ds(THIN, planes - THIN)]
    one_s[pl.ds(HALO, HALO)] = one_in[...]
    two_s[pl.ds(HALO + 1, HALO)] = two_in[...]
    all_coefficients(coef_ref, None, far_ref, statics, tx_s, 1, 2 * HALO)
    prolong(
        one_s, (0, HALO), gains_of(spread_ref[...], -1), lambda i, u, rows: far_ref[i * HALO + u, rows]
    )
    sweep(coef_ref, one_s, two_s, 1, HALO + 1)
    sweep(coef_ref, two_s, one_s, 2, HALO + 2)
    sweep(coef_ref, one_s, two_s, 3, HALO + 3)
    stores = started(
        [(two_s.at[pl.ds(2 * HALO - 1 - k, 1)], send_far_hbm.at[pl.ds(k, 1)]) for k in range(HALO)], sems
    )
    pressure_ref[pl.ds(0, THIN)] = two_s[pl.ds(HALO, THIN)]
    for u in range(HALO, 2 * HALO):
        one_s[u] = misfit(coef_ref, two_s, u)
    totals = restrict_totals(
        lambda i, u: basis_ref[i, u - HALO],
        lambda u: one_s[u],
        HALO,
        2 * HALO,
        [totals_in[k] for k in range(NBF * NYB)],
    )
    tail_s[...] = restricted_tile(totals, lane_of(me))
    stores += started(
        [(tail_s, packed_hbm.at[e]) for e in range(count)], sems, HALO
    )
    for copy in stores:
        copy.wait()


def last_kernel(
    basis_hbm, gathered_ref, inverse_ref, near_ref, far_ref, coupling_ref, pressure_ref, near_p_ref, far_p_ref,
    *refs
):
    statics, refs = refs[:6], refs[6:]
    pressure_out, residual_out, basis_ref, coef_ref, one_s, two_s, tx_s, pressure_s, residual_s, sems = refs
    planes = pressure_ref.shape[0]
    top = planes + HALO
    me = lax.axis_index("gx")
    load = started(((basis_hbm, basis_ref),), sems)[0]
    spread = corrected_values(coupling_ref, inverse_ref, window_of_tiles(gathered_ref, me))
    all_coefficients(coef_ref, near_ref, far_ref, statics, tx_s, 1, top + THIN)
    prolong(
        one_s, (0, HALO), gains_of(spread, -1), lambda i, u, rows: far_ref[i * HALO + u, rows],
        lambda u: far_p_ref[u],
    )
    prolong(
        one_s, (top, top + HALO), gains_of(spread, 1), lambda i, u, rows: near_ref[i * HALO + u - top, rows],
        lambda u: near_p_ref[u - top],
    )
    load.wait()
    prolong(
        one_s, (HALO, top), gains_of(spread, 0), lambda i, u, rows: basis_ref[i, plane_at(u - HALO, planes), rows],
        lambda u: pressure_ref[u - HALO],
    )
    sweep(coef_ref, one_s, two_s, 1, top + HALO - 1)
    sweep(coef_ref, two_s, one_s, 2, top + HALO - 2)
    sweep(coef_ref, one_s, two_s, 3, top + HALO - 3)
    for place in range(planes):
        pressure_s[plane_at(place, planes)] = two_s[place + HALO]
    stores = started(((pressure_s, pressure_out),), sems, 1)

    def step(u):
        residual_s[plane_at(u - HALO, planes)] = misfit(coef_ref, two_s, u)

    half = planes // 2
    for part in range(2):
        planes_in_groups(HALO + part * half, HALO + (part + 1) * half, half, step)
        span = pl.ds(plane_at(part * half, planes) - jnp.where(is_even(), 0, half - 1), half)
        stores += started(((residual_s.at[span], residual_out.at[span]),), sems, 2 + part)
    for copy in stores:
        copy.wait()


VMEM = pl.BlockSpec(memory_space=pltpu.VMEM)
ANY = pl.BlockSpec(memory_space=pl.ANY)


def kernel_call(name, body, arguments, outputs, scratch, aliases=None):
    spec = {pltpu.HBM: ANY, pltpu.VMEM: VMEM}
    call = pl.pallas_call(
        body,
        out_shape=[space(shape, dtype) for space, shape, dtype in outputs],
        in_specs=[spec[space] for space, _ in arguments],
        out_specs=[spec[space] for space, _, _ in outputs],
        scratch_shapes=scratch,
        input_output_aliases=aliases or {},
        compiler_params=pltpu.CompilerParams(vmem_limit_bytes=16 * 1024 * 1024),
        name=name,
    )
    return call(*[pltpu.with_memory_space_constraint(value, space) for space, value in arguments])


def local(
    right_side, wet_quarters, trans_x, trans_y, trans_z, storage, basis, coupling, coarse_inverse,
    owned_block, block_slot, neighbours,
):
    count = lax.axis_size("gx")
    planes, ny, nz = right_side.shape
    field = (ny, nz)
    full = planes + 2 * HALO
    near_pairs = [(i, i ^ 1) for i in range(count)]
    far_pairs = [(i, i + 1) for i in range(1, count - 1, 2)]
    far_pairs = far_pairs + [(b, a) for a, b in far_pairs]
    H, V = pltpu.HBM, pltpu.VMEM
    statics = [(H, a) for a in (right_side, wet_quarters, trans_x, trans_y, trans_z, storage)]
    halo = (H_ALL,) + field
    factors = pltpu.VMEM((full, 8) + field, F32)
    state = pltpu.VMEM((full,) + field, F32)
    own = pltpu.VMEM((planes,) + field, F32)
    window = pltpu.VMEM((count * PER + WIN, 128), F32)
    around = pltpu.VMEM((full,) + field, BF16)
    whole_basis = pltpu.VMEM(basis.shape, BF16)

    blocks = coarse_inverse.shape[2]
    near, far, packed, *fields, inverse, room, more_room = kernel_call(
        "restrict_first",
        first_kernel,
        [
            (H, owned_block), (H, basis), *statics, (H, coupling.reshape(KROWS, PER)),
            (H, coarse_inverse.reshape(NBF * NBF, blocks)),
        ],
        [(H, halo, BF16), (H, halo, BF16), (H, (count // 2, ROWS, 128), F32), (V, right_side.shape, F32)]
        + [(V, right_side.shape, BF16)] * 5
        + [(V, (NBF * NBF, WIN), F32), (V, right_side.shape, F32), (V, (KROWS, WIN), F32)],
        [
            pltpu.SMEM(owned_block.shape, jnp.int32),
            whole_basis,
            *[pltpu.VMEM(a.shape, a.dtype) for _, a in statics],
            pltpu.VMEM((KROWS, PER), F32),
            pltpu.VMEM((NBF * NBF, blocks), F32),
            pltpu.VMEM((ROWS, 128), F32),
            pltpu.VMEM((2,) + halo, BF16),
            pltpu.SemaphoreType.DMA((16 + count // 2,)),
        ],
    )
    far = lax.ppermute(far, "gx", far_pairs)
    ranks = list(range(count // 2))
    ranks = [rank ^ 4 for rank in ranks]
    chips = [[core + 2 * chip for chip in ranks] for core in range(2)]
    half = lax.all_to_all(packed, "gx", 0, 0, axis_index_groups=chips, tiled=True)
    near = lax.ppermute(near, "gx", near_pairs)
    other = lax.ppermute(half, "gx", near_pairs)

    pressure, coupled, spread, one, two, totals, edge_basis, send_near = kernel_call(
        "iteration_first",
        body_kernel,
        [(H, basis)] + [(V, a) for a in (half, other, inverse, near, *fields, room, more_room)],
        [
            (V, (planes,) + field, F32),
            (V, (KROWS, WIN), F32),
            (V, (NBF, 3 * NYB * nz), F32),
            (V, (HALO,) + field, F32),
            (V, (HALO,) + field, F32),
            (V, (NBF * NYB, 8, nz), F32),
            (V, (NBF, HALO) + field, BF16),
            (H, (HALO,) + field, F32),
        ],
        [
            pltpu.VMEM((count * PER, KROWS + 128), F32),
            window, whole_basis, factors, state, state, around, pltpu.SemaphoreType.DMA((1 + HALO,)),
        ],
        {11: 0, 12: 1},
    )
    near_p = lax.ppermute(send_near, "gx", near_pairs)
    far, near_p = lax.optimization_barrier((far, near_p))
    pressure, send_far, packed = kernel_call(
        "edge_first",
        functools.partial(edge_kernel, count),
        [(V, a) for a in (spread, one, two, totals, edge_basis, pressure, far, *fields)],
        [
            (V, (planes,) + field, F32),
            (H, (HALO,) + field, F32),
            (H, (count, NBF, 128), F32),
        ],
        [
            factors, state, state, around,
            pltpu.VMEM((NBF, 128), F32), pltpu.SemaphoreType.DMA((HALO + count,)),
        ],
        {5: 0},
    )

    far_p = lax.ppermute(send_far, "gx", far_pairs)
    gathered = lax.all_to_all(packed, "gx", 0, 0, axis_index_groups=[tile_order(count)], tiled=True)
    whole = (H, (planes,) + field, F32)
    return kernel_call(
        "iteration_last",
        last_kernel,
        [(H, basis)]
        + [(V, a) for a in (gathered, inverse, near, far, coupled, pressure, near_p, far_p, *fields)],
        [whole, whole],
        [
            whole_basis, factors, state, state, around, own, own,
            pltpu.SemaphoreType.DMA((4,)),
        ],
    )


def solution(mesh):
    slabs = P(("parts", "gx"), None, None)
    placed = (
        slabs, slabs, slabs, slabs, slabs, slabs,
        P(None, ("parts", "gx"), None, None),
        P(None, None, None, ("parts", "gx")),
        P(None, None, "parts"),
        P(),
        P("gx"),
        P(None, "gx"),
    )
    return jax.shard_map(local, mesh=mesh, in_specs=placed, out_specs=(slabs, slabs), check_vma=False)
```
